32 devices in a mesh: seq: 8 (over y, x, core), head: 4 (over z).
Axes of the slice: x: 2, y: 2, z: 4, core: 2. Of those that a mesh axis runs over, the one named last changes fastest.
Arguments:
- queries: bfloat16 [9216, 5120], P(('seq', 'head')), may hold values from -120 to 120
- key_vectors: bfloat16 [9216, 5120], P(('seq', 'head')), may hold values from -20 to 20
- value_vectors: bfloat16 [9216, 5120], P(('seq', 'head')), may hold values from -6 to 6
- reach_time: int32 [24], P('seq'), may hold values from 0 to 1
- reach_width: int32 [24], P('seq'), may hold values from 0 to 2
- keep_mask: int32 [9216, 40], P('seq', 'head'), may hold values 0 or 1
Outputs:
- attended: bfloat16 [9216, 5120], P(('seq', 'head'))
The draws below stay inside these ranges and needn't reach their ends.
All inputs are finite; a program needn't handle non-finite values. No bound on the sum of `keep_mask` on one device may be relied on, other than what follows from the above.
Results may differ from the reference program's by a relative error of at most 0.0046.
Values may be sent and summed in bfloat16 or wider, within the bound.
No kernel may reach another device: no remote copies, remote signals or barrier semaphores. Data moves between devices by JAX's collectives and lax.ppermute only.
A program may use at most 128 MiB of HBM per device.

```python
import math
import jax
import jax.numpy as jnp
from jax import lax

H = 40
HD = 128
TILE = 384
TILES_W = 3
TOKENS = 9216
NTILES = 24
N_SEQ = 8


def paired_draw(key):
    base_key = jax.random.fold_in(key, 11)
    first, second = jax.random.split(base_key, 2)
    width = H * HD
    query_draw = jnp.clip(jax.random.normal(first, (TOKENS, width), jnp.float32), -4.0, 4.0)
    key_draw = jnp.clip(jax.random.normal(second, (TOKENS, width), jnp.float32), -4.0, 4.0)
    return (query_draw, key_draw)


def draw_queries(key, part):
    return paired_draw(key)[0].astype(jnp.bfloat16)


def draw_key_vectors(key, part):
    return paired_draw(key)[1].astype(jnp.bfloat16)


def with_ends(drawn, own_key, least, top_value):
    longest = drawn.shape.index(max(drawn.shape))
    spots = []
    for shift in (0, 1):
        where = [jax.random.randint(jax.random.fold_in(own_key, axis), (), 0, length) for axis, length in enumerate(drawn.shape)]
        where[longest] = (where[longest] + shift) % drawn.shape[longest]
        spots.append(tuple(where))
    return drawn.at[spots[0]].set(least).at[spots[1]].set(top_value)


def level_of(stream_key, extent, cuts, least, largest):
    factor_of = 1.0
    for dim, parts in cuts:
        draws = jax.random.uniform(jax.random.fold_in(jax.random.fold_in(stream_key, 6), dim), (parts,), jnp.float32, least / len(cuts), largest / len(cuts))
        factor_of = factor_of * jnp.repeat(jnp.exp(draws), extent[dim] // parts).reshape((-1,) + (1,) * (len(extent) - 1 - dim))
    return factor_of


def scatter_about(stream_key, extent, spread, bound, shards=(), held_as=jnp.bfloat16):
    array = spread * jax.random.normal(stream_key, extent, jnp.float32)
    if shards:
        array = array * level_of(stream_key, extent, shards, -0.22, 0.18)
    return jnp.clip(array, -bound, bound).astype(held_as)


def setup_inputs(seed: int = 0) -> dict:
    splits = jax.random.split(jax.random.key(seed), 7)
    queries = draw_queries(jax.random.fold_in(splits[6], 71), 0)
    key_vectors = draw_key_vectors(jax.random.fold_in(splits[6], 71), 0)
    value_vectors = scatter_about(splits[2], (TOKENS, H * HD), 1.0, 6.0, ((0, 32),))
    reach_time = with_ends(jax.random.randint(splits[3], (NTILES,), 0, 2), jax.random.fold_in(splits[3], 1), 0, 1).astype(jnp.int32)
    reach_width = with_ends(jax.random.randint(splits[4], (NTILES,), 0, 3), jax.random.fold_in(splits[4], 1), 0, 2).astype(jnp.int32)
    keep_mask = with_ends((jax.random.randint(splits[5], (TOKENS, H), 0, 10) < 9).astype(jnp.int32), jax.random.fold_in(splits[5], 1), 0, 1)
    return dict(queries=queries, key_vectors=key_vectors, value_vectors=value_vectors, reach_time=reach_time, reach_width=reach_width, keep_mask=keep_mask)


def tile_mask(reach_t, reach_w, slab_index, slab_count):
    tile_count = reach_t.shape[0]
    places = jnp.arange(tile_count, dtype=jnp.int32)
    columns = jnp.arange(3 * tile_count, dtype=jnp.int32)
    offsets = columns // tile_count - 1
    key_place = columns % tile_count
    inside = (slab_index + offsets >= 0) & (slab_index + offsets < slab_count)
    near_time = jnp.abs(offsets)[None, :] <= reach_t[:, None]
    near_width = jnp.abs(key_place[None, :] - places[:, None]) <= reach_w[:, None]
    return near_time & near_width & inside[None, :]

def head_terms(query_head, key_head, value_head, allowed):
    tile_count = allowed.shape[0]
    slab_rows = query_head.shape[0]
    tile_rows = slab_rows // tile_count
    scores = jnp.dot(query_head.astype(jnp.float32), key_head.astype(jnp.float32).T, preferred_element_type=jnp.float32) * (1.0 / math.sqrt(query_head.shape[1]))
    scores = scores.reshape(tile_count, tile_rows, 3 * tile_count, tile_rows)
    mask_full = allowed[:, None, :, None]
    scores = jnp.where(mask_full, scores, -1e+30)
    highest = lax.optimization_barrier(jnp.max(scores, axis=(2, 3), keepdims=True))
    weights = jnp.where(mask_full, jnp.exp(scores - highest), 0.0)
    totals = lax.optimization_barrier(jnp.sum(weights, axis=(2, 3))).reshape(slab_rows)
    rounded = lax.optimization_barrier(weights.reshape(slab_rows, 3 * slab_rows).astype(jnp.bfloat16))
    summed = jnp.dot(rounded.astype(jnp.float32), value_head.astype(jnp.float32), preferred_element_type=jnp.float32)
    return (summed, totals)

def reference(queries, key_vectors, value_vectors, reach_time, reach_width, keep_mask):
    slab_rows = TILE * TILES_W
    query_slabs = queries.reshape(N_SEQ, slab_rows, H, HD)
    key_padded = jnp.pad(key_vectors.reshape(TOKENS, H, HD), ((slab_rows, slab_rows), (0, 0), (0, 0)))
    value_padded = jnp.pad(value_vectors.reshape(TOKENS, H, HD), ((slab_rows, slab_rows), (0, 0), (0, 0)))
    keep_slabs = keep_mask.reshape(N_SEQ, slab_rows, H)
    reach_t = reach_time.reshape(N_SEQ, TILES_W)
    reach_w = reach_width.reshape(N_SEQ, TILES_W)

    def one_slab(slab_index):
        allowed = tile_mask(reach_t[slab_index], reach_w[slab_index], slab_index, N_SEQ)
        key_rows = lax.dynamic_slice_in_dim(key_padded, slab_index * slab_rows, 3 * slab_rows, 0)
        value_rows = lax.dynamic_slice_in_dim(value_padded, slab_index * slab_rows, 3 * slab_rows, 0)
        query_heads = jnp.moveaxis(query_slabs[slab_index], 1, 0)
        key_heads = jnp.moveaxis(key_rows, 1, 0)
        value_heads = jnp.moveaxis(value_rows, 1, 0)

        def per_head(triple):
            return head_terms(triple[0], triple[1], triple[2], allowed)
        summed, totals = lax.map(per_head, (query_heads, key_heads, value_heads))
        factor = jnp.moveaxis(keep_slabs[slab_index], 1, 0).astype(jnp.float32) * (10.0 / 9.0)
        output = (summed * factor[:, :, None] / totals[:, :, None]).astype(jnp.bfloat16)
        return jnp.moveaxis(output, 0, 1)
    outputs = lax.map(one_slab, jnp.arange(N_SEQ, dtype=jnp.int32))
    return outputs.reshape(TOKENS, H * HD)
```

```python
import functools
import math

import jax
import jax.numpy as jnp
from jax import lax
from jax.experimental import pallas as pl
from jax.experimental.pallas import tpu as pltpu
from jax.sharding import PartitionSpec as P

LANES = 128
HEADS_PER_CHUNK = 2


def tile_mask(reach_t, reach_w, slab_index, slab_count):
    tile_count = reach_t.shape[0]
    places = jnp.arange(tile_count, dtype=jnp.int32)
    columns = jnp.arange(3 * tile_count, dtype=jnp.int32)
    offsets = columns // tile_count - 1
    key_place = columns % tile_count
    inside = (slab_index + offsets >= 0) & (slab_index + offsets < slab_count)
    near_time = jnp.abs(offsets)[None, :] <= reach_t[:, None]
    near_width = jnp.abs(key_place[None, :] - places[:, None]) <= reach_w[:, None]
    return near_time & near_width & inside[None, :]


def lane_fold(op, wide):
    folded = wide[:, :LANES]
    for start in range(LANES, wide.shape[1], LANES):
        folded = op(folded, wide[:, start : start + LANES])
    return folded


def attend_kernel(
    tile_count,
    first_head,
    plan_ref,
    q_ref,
    k_own,
    v_own,
    k_prev,
    v_prev,
    k_next,
    v_next,
    keep_ref,
    out_ref,
    scores_ref,
    top_ref,
    total_ref,
    sum_ref,
):
    slab_rows, head_size = q_ref.shape
    tile_rows = slab_rows // tile_count
    scale = math.log2(math.e) / math.sqrt(head_size)
    slabs = ((0, k_prev, v_prev), (1, k_own, v_own), (2, k_next, v_next))
    head = first_head + pl.program_id(0)

    def tile(index):
        return pl.ds(pl.multiple_of(index * tile_rows, tile_rows), tile_rows)

    def one_tile(i, carry):
        top_ref[...] = jnp.full_like(top_ref, -jnp.inf)
        total_ref[...] = jnp.zeros_like(total_ref)
        sum_ref[...] = jnp.zeros_like(sum_ref)

        for slab, k_ref, _ in slabs:

            def score(place, carry, slab=slab, k_ref=k_ref):
                column = slab * tile_count + place

                @pl.when(plan_ref[i * 3 * tile_count + column] > 0)
                def _():
                    found = lax.dot_general(
                        q_ref[tile(i), :],
                        k_ref[tile(place), :],
                        (((1,), (1,)), ((), ())),
                        preferred_element_type=jnp.float32,
                    )
                    scores_ref[column] = found
                    top_ref[...] = jnp.maximum(top_ref[...], lane_fold(jnp.maximum, found))

                return carry

            lax.fori_loop(0, tile_count, score, 0)

        highest = jnp.max(top_ref[...], axis=1, keepdims=True) * scale

        for slab, _, v_ref in slabs:

            def weigh(place, carry, slab=slab, v_ref=v_ref):
                column = slab * tile_count + place

                @pl.when(plan_ref[i * 3 * tile_count + column] > 0)
                def _():
                    weights = jnp.exp2(scores_ref[column] * scale - highest)
                    total_ref[...] += lane_fold(jnp.add, weights)
                    sum_ref[...] += jnp.dot(
                        weights.astype(jnp.bfloat16),
                        v_ref[tile(place), :],
                        preferred_element_type=jnp.float32,
                    )

                return carry

            lax.fori_loop(0, tile_count, weigh, 0)

        totals = jnp.sum(total_ref[...], axis=1, keepdims=True)
        keep = keep_ref[tile(i), :].astype(jnp.float32)
        mine = lax.broadcasted_iota(jnp.int32, keep.shape, 1) == head
        factor = jnp.sum(jnp.where(mine, keep, 0.0), axis=1, keepdims=True) * (10.0 / 9.0)
        out_ref[tile(i), :] = (sum_ref[...] * (factor / totals)).astype(out_ref.dtype)
        return carry

    lax.fori_loop(0, tile_count, one_tile, 0)


def attend(plan, queries, pairs_own, pairs_prev, pairs_next, keep_mask, first_head, head_size):
    slab_rows, width = queries.shape
    heads = width // head_size
    tile_count = math.isqrt(plan.shape[0] // 3)
    tile_rows = slab_rows // tile_count
    block = (slab_rows, head_size)
    key_spec = pl.BlockSpec(block, lambda h, plan: (0, h))
    value_spec = pl.BlockSpec(block, lambda h, plan: (0, heads + h))
    pairs = heads * slab_rows * 3 * slab_rows
    return pl.pallas_call(
        functools.partial(attend_kernel, tile_count, first_head),
        grid_spec=pltpu.PrefetchScalarGridSpec(
            num_scalar_prefetch=1,
            grid=(heads,),
            in_specs=[
                key_spec,
                key_spec,
                value_spec,
                key_spec,
                value_spec,
                key_spec,
                value_spec,
                pl.BlockSpec(keep_mask.shape, lambda h, plan: (0, 0)),
            ],
            out_specs=key_spec,
            scratch_shapes=[
                pltpu.VMEM((3 * tile_count, tile_rows, tile_rows), jnp.float32),
                pltpu.VMEM((tile_rows, LANES), jnp.float32),
                pltpu.VMEM((tile_rows, LANES), jnp.float32),
                pltpu.VMEM((tile_rows, head_size), jnp.float32),
            ],
        ),
        out_shape=jax.ShapeDtypeStruct((slab_rows, width), jnp.bfloat16),
        compiler_params=pltpu.CompilerParams(vmem_limit_bytes=40 * 2**20),
        cost_estimate=pl.CostEstimate(
            flops=8 * pairs * head_size,
            bytes_accessed=16 * slab_rows * width,
            transcendentals=pairs,
        ),
    )(plan, queries, pairs_own, pairs_own, pairs_prev, pairs_prev, pairs_next, pairs_next, keep_mask)


def regroup(parts):
    return lax.all_to_all(parts, "head", split_axis=0, concat_axis=0, tiled=True)


def on_device(queries, key_vectors, value_vectors, reach_time, reach_width, keep_mask):
    groups = lax.axis_size("head")
    slab_count = lax.axis_size("seq")
    local_rows, width = queries.shape
    group_heads = keep_mask.shape[1]
    head_size = width // (group_heads * groups)
    slab_rows = local_rows * groups
    allowed = tile_mask(reach_time, reach_width, lax.axis_index("seq"), slab_count)
    plan = allowed.astype(jnp.int32).reshape(-1)
    onward = [(i, i + 1) for i in range(slab_count - 1)]
    backward = [(i + 1, i) for i in range(slab_count - 1)]

    def columns(array, group, first, last):
        start = group * group_heads * head_size
        return array[:, start + first * head_size : start + last * head_size]

    returned = []
    for first in range(0, group_heads, HEADS_PER_CHUNK):
        last = min(first + HEADS_PER_CHUNK, group_heads)
        pair_parts = jnp.stack(
            [
                jnp.concatenate(
                    [columns(key_vectors, g, first, last), columns(value_vectors, g, first, last)],
                    axis=1,
                )
                for g in range(groups)
            ]
        )
        query_parts = jnp.stack([columns(queries, g, first, last) for g in range(groups)])
        own = regroup(pair_parts).reshape(slab_rows, -1)
        chunk_queries = regroup(query_parts).reshape(slab_rows, -1)
        before = lax.ppermute(own, "seq", onward)
        after = lax.ppermute(own, "seq", backward)
        output = attend(plan, chunk_queries, own, before, after, keep_mask, first, head_size)
        returned.append(regroup(output.reshape(groups, local_rows, -1)))
    return jnp.concatenate([part[g] for g in range(groups) for part in returned], axis=1)


def solution(mesh):
    return jax.shard_map(
        on_device,
        mesh=mesh,
        in_specs=(
            P(("seq", "head"), None),
            P(("seq", "head"), None),
            P(("seq", "head"), None),
            P("seq"),
            P("seq"),
            P("seq", "head"),
        ),
        out_specs=P(("seq", "head"), None),
        check_vma=False,
    )
```

```python
import functools
import math

import jax
import jax.numpy as jnp
from jax import lax
from jax.experimental import pallas as pl
from jax.experimental.pallas import tpu as pltpu
from jax.sharding import PartitionSpec as P

LANES = 128
CHUNKS = 4
ANY = pl.BlockSpec(memory_space=pl.ANY)
VMEM_LIMIT = 56 * 2**20


def tile_mask(reach_t, reach_w, slab_index, slab_count):
    tile_count = reach_t.shape[0]
    places = jnp.arange(tile_count, dtype=jnp.int32)
    columns = jnp.arange(3 * tile_count, dtype=jnp.int32)
    offsets = columns // tile_count - 1
    key_place = columns % tile_count
    inside = (slab_index + offsets >= 0) & (slab_index + offsets < slab_count)
    near_time = jnp.abs(offsets)[None, :] <= reach_t[:, None]
    near_width = jnp.abs(key_place[None, :] - places[:, None]) <= reach_w[:, None]
    return near_time & near_width & inside[None, :]


def run_copies(sems, pairs):
    copies = [
        pltpu.make_async_copy(source, target, sems.at[i]) for i, (source, target) in enumerate(pairs)
    ]
    for copy in copies:
        copy.start()
    for copy in copies:
        copy.wait()


def pack(arrays, after, groups, group_width, start, width):
    rows = arrays[0].shape[0]

    def kernel(*refs):
        sources, outs, sems = refs[:3], refs[3 + len(after) : -1], refs[-1]
        me = lax.axis_index("head")
        pairs = []
        for shift in range(groups):
            group = lax.rem(me + shift, groups)
            column = pl.multiple_of(group * group_width + start, LANES)
            for i, source in enumerate(sources):
                pairs.append(
                    (source.at[:, pl.ds(column, width)], outs[shift].at[:, pl.ds(i * width, width)])
                )
        run_copies(sems, pairs)

    return pl.pallas_call(
        kernel,
        in_specs=[ANY] * (3 + len(after)),
        out_specs=[ANY] * groups,
        out_shape=[jax.ShapeDtypeStruct((rows, 3 * width), jnp.bfloat16)] * groups,
        scratch_shapes=[pltpu.SemaphoreType.DMA((3 * groups,))],
        cost_estimate=pl.CostEstimate(
            flops=0, bytes_accessed=12 * groups * rows * width, transcendentals=0
        ),
        compiler_params=pltpu.CompilerParams(vmem_limit_bytes=VMEM_LIMIT),
        name="pack",
    )(*arrays, *after)


def assemble(pieces, after, width):
    groups = len(pieces)
    rows = pieces[0].shape[0]

    def kernel(*refs):
        parts, out, sems = refs[:groups], refs[-2], refs[-1]
        me = lax.axis_index("head")
        pairs = []
        for shift in range(groups):
            owner = lax.rem(me + groups - shift, groups)
            row = pl.multiple_of(owner * rows, 16)
            pairs.append((parts[shift].at[:, pl.ds(0, 2 * width)], out.at[pl.ds(row, rows), :]))
        run_copies(sems, pairs)

    return pl.pallas_call(
        kernel,
        in_specs=[ANY] * (groups + len(after)),
        out_specs=ANY,
        out_shape=jax.ShapeDtypeStruct((groups * rows, 2 * width), jnp.bfloat16),
        scratch_shapes=[pltpu.SemaphoreType.DMA((groups,))],
        cost_estimate=pl.CostEstimate(
            flops=0, bytes_accessed=8 * groups * rows * width, transcendentals=0
        ),
        compiler_params=pltpu.CompilerParams(vmem_limit_bytes=VMEM_LIMIT),
        name="assemble",
    )(*pieces, *after)


def place(chunks, group_width, total_width, target=None):
    groups = len(chunks[0][1])
    rows = chunks[0][1][0].shape[0]
    blocks = [block for _, parts in chunks for block in parts]
    extra = [] if target is None else [target]

    def kernel(*refs):
        out, sems = refs[-2], refs[-1]
        me = lax.axis_index("head")
        pairs = []
        for i, (start, parts) in enumerate(chunks):
            for shift, part in enumerate(parts):
                group = lax.rem(me + shift, groups)
                column = pl.multiple_of(group * group_width + start, LANES)
                pairs.append((refs[i * groups + shift], out.at[:, pl.ds(column, part.shape[1])]))
        run_copies(sems, pairs)

    return pl.pallas_call(
        kernel,
        in_specs=[ANY] * (len(blocks) + len(extra)),
        out_specs=ANY,
        out_shape=jax.ShapeDtypeStruct((rows, total_width), jnp.bfloat16),
        scratch_shapes=[pltpu.SemaphoreType.DMA((len(blocks),))],
        input_output_aliases={len(blocks): 0} if extra else {},
        cost_estimate=pl.CostEstimate(
            flops=0,
            bytes_accessed=4 * rows * sum(block.shape[1] for block in blocks),
            transcendentals=0,
        ),
        compiler_params=pltpu.CompilerParams(vmem_limit_bytes=VMEM_LIMIT),
        name="place",
    )(*blocks, *extra)


def lane_fold(op, wide):
    folded = wide[:, :LANES]
    for start in range(LANES, wide.shape[1], LANES):
        folded = op(folded, wide[:, start : start + LANES])
    return folded


def attend_kernel(groups, heads, first_head, tile_count, *refs):
    plan_ref, pieces = refs[0], refs[1 : 1 + groups]
    prev_ref, own_ref, next_ref, keep_ref = refs[1 + groups : 5 + groups]
    outs = refs[-6 - groups : -6]
    q_ref, out_ref, scores_ref, top_ref, total_ref, sum_ref = refs[-6:]
    slab_rows, width = q_ref.shape
    local_rows = slab_rows // groups
    head_size = width // heads
    tile_rows = slab_rows // tile_count
    scale = math.log2(math.e) / math.sqrt(head_size)
    slabs = ((0, prev_ref), (1, own_ref), (2, next_ref))
    me = lax.axis_index("head")

    def owner_rows(shift):
        owner = lax.rem(me + groups - shift, groups)
        return pl.ds(pl.multiple_of(owner * local_rows, 16), local_rows)

    def tile(index):
        return pl.ds(pl.multiple_of(index * tile_rows, tile_rows), tile_rows)

    def lanes(index):
        return pl.ds(index * head_size, head_size)

    for shift in range(groups):
        q_ref[owner_rows(shift), :] = pieces[shift][...]

    def one_tile(i, carry):
        top_ref[...] = jnp.full_like(top_ref, -jnp.inf)
        total_ref[...] = jnp.zeros_like(total_ref)
        sum_ref[...] = jnp.zeros_like(sum_ref)

        for slab, pair_ref in slabs:

            def score(place, carry, slab=slab, pair_ref=pair_ref):
                column = slab * tile_count + place

                @pl.when(plan_ref[i * 3 * tile_count + column] > 0)
                def _():
                    for h in range(heads):
                        found = lax.dot_general(
                            q_ref[tile(i), lanes(h)],
                            pair_ref[tile(place), lanes(h)],
                            (((1,), (1,)), ((), ())),
                            preferred_element_type=jnp.float32,
                        )
                        scores_ref[h, column] = found
                        top_ref[h] = jnp.maximum(top_ref[h], lane_fold(jnp.maximum, found))

                return carry

            lax.fori_loop(0, tile_count, score, 0)

        for h in range(heads):
            highest = jnp.max(top_ref[h], axis=1, keepdims=True) * scale
            top_ref[h] = jnp.broadcast_to(highest, top_ref.shape[1:])

        for slab, pair_ref in slabs:

            def weigh(place, carry, slab=slab, pair_ref=pair_ref):
                column = slab * tile_count + place

                @pl.when(plan_ref[i * 3 * tile_count + column] > 0)
                def _():
                    for h in range(heads):
                        highest = jnp.concatenate([top_ref[h]] * (tile_rows // LANES), axis=1)
                        weights = jnp.exp2(scores_ref[h, column] * scale - highest)
                        total_ref[h] += lane_fold(jnp.add, weights)
                        sum_ref[h] += jnp.dot(
                            weights.astype(jnp.bfloat16),
                            pair_ref[tile(place), lanes(heads + h)],
                            preferred_element_type=jnp.float32,
                        )

                return carry

            lax.fori_loop(0, tile_count, weigh, 0)

        keep = keep_ref[tile(i), :].astype(jnp.float32)
        numbers = lax.broadcasted_iota(jnp.int32, keep.shape, 1)
        for h in range(heads):
            totals = jnp.sum(total_ref[h], axis=1, keepdims=True)
            mine = jnp.where(numbers == first_head + h, keep, 0.0)
            factor = jnp.sum(mine, axis=1, keepdims=True) * (10.0 / 9.0)
            out_ref[tile(i), lanes(h)] = (sum_ref[h] * (factor / totals)).astype(out_ref.dtype)
        return carry

    lax.fori_loop(0, tile_count, one_tile, 0)

    for shift in range(groups):
        outs[shift][...] = out_ref[owner_rows(shift), :]


def attend(plan, pieces, prev, own, behind, keep_mask, after, first_head, heads, tile_count):
    groups = len(pieces)
    slab_rows = own.shape[0]
    local_rows = slab_rows // groups
    width = own.shape[1] // 2
    tile_rows = slab_rows // tile_count
    head_size = width // heads
    pairs = heads * slab_rows * 3 * slab_rows
    whole = pl.BlockSpec(own.shape, lambda s, plan: (0, 0))
    accumulator = pltpu.VMEM((heads, tile_rows, LANES), jnp.float32)
    return pl.pallas_call(
        functools.partial(attend_kernel, groups, heads, first_head, tile_count),
        grid_spec=pltpu.PrefetchScalarGridSpec(
            num_scalar_prefetch=1,
            grid=(1,),
            in_specs=[pl.BlockSpec((local_rows, width), lambda s, plan: (0, 2))] * groups
            + [whole] * 3
            + [pl.BlockSpec(keep_mask.shape, lambda s, plan: (0, 0))]
            + [ANY] * len(after),
            out_specs=[pl.BlockSpec((local_rows, width), lambda s, plan: (0, 0))] * groups,
            scratch_shapes=[
                pltpu.VMEM((slab_rows, width), jnp.bfloat16),
                pltpu.VMEM((slab_rows, width), jnp.bfloat16),
                pltpu.VMEM((heads, 3 * tile_count, tile_rows, tile_rows), jnp.float32),
                accumulator,
                accumulator,
                pltpu.VMEM((heads, tile_rows, head_size), jnp.float32),
            ],
        ),
        out_shape=[jax.ShapeDtypeStruct((local_rows, width), jnp.bfloat16)] * groups,
        compiler_params=pltpu.CompilerParams(vmem_limit_bytes=VMEM_LIMIT),
        cost_estimate=pl.CostEstimate(
            flops=16 * pairs * head_size,
            bytes_accessed=16 * slab_rows * width,
            transcendentals=pairs,
        ),
        name="attend",
    )(plan, *pieces, prev, own, behind, keep_mask, *after)


def on_device(queries, key_vectors, value_vectors, reach_time, reach_width, keep_mask):
    groups = lax.axis_size("head")
    slab_count = lax.axis_size("seq")
    total_width = queries.shape[1]
    group_heads = keep_mask.shape[1]
    group_width = total_width // groups
    head_size = group_width // group_heads
    tile_count = reach_time.shape[0]
    allowed = tile_mask(reach_time, reach_width, lax.axis_index("seq"), slab_count)
    plan = allowed.astype(jnp.int32).reshape(-1)
    onward = [(i, i + 1) for i in range(slab_count - 1)]
    backward = [(i + 1, i) for i in range(slab_count - 1)]

    def turn(array, shift):
        return lax.ppermute(array, "head", [(i, (i + shift) % groups) for i in range(groups)])

    count = min(CHUNKS, group_heads)
    sizes = [group_heads // count + (i < group_heads % count) for i in range(count)]
    firsts = [sum(sizes[:i]) for i in range(count)]
    sources = (key_vectors, value_vectors, queries)

    def send(i, after):
        width = sizes[i] * head_size
        blocks = pack(sources, after, groups, group_width, firsts[i] * head_size, width)
        return [blocks[0]] + [turn(blocks[shift], shift) for shift in range(1, groups)]

    pieces = [send(i, []) for i in range(min(2, count))]
    done = []
    for i, heads in enumerate(sizes):
        own = assemble(
            pieces[i],
            [part[0] for part in pieces[i + 1 :]] + [part[1][0] for part in done[-1:]],
            heads * head_size,
        )
        before = lax.ppermute(own, "seq", onward)
        behind = lax.ppermute(own, "seq", backward)
        if i + 2 < count:
            pieces.append(send(i + 2, [own]))
        hold = [part[0] for part in pieces[i + 2 :]]
        outs = attend(
            plan, pieces[i], before, own, behind, keep_mask, hold, firsts[i], heads, tile_count
        )
        back = [outs[0]] + [turn(outs[shift], groups - shift) for shift in range(1, groups)]
        done.append((firsts[i] * head_size, back))
    early = place(done[:-1], group_width, total_width) if count > 1 else None
    return place(done[-1:], group_width, total_width, early)


def solution(mesh):
    return jax.shard_map(
        on_device,
        mesh=mesh,
        in_specs=(
            P(("seq", "head"), None),
            P(("seq", "head"), None),
            P(("seq", "head"), None),
            P("seq"),
            P("seq"),
            P("seq", "head"),
        ),
        out_specs=P(("seq", "head"), None),
        check_vma=False,
    )
```

```python
import functools
import math

import jax
import jax.numpy as jnp
from jax import lax
from jax.experimental import pallas as pl
from jax.experimental.pallas import tpu as pltpu
from jax.sharding import PartitionSpec as P

LANES = 128
CHUNKS = 4
ANY = pl.BlockSpec(memory_space=pl.ANY)
VMEM_LIMIT = 56 * 2**20


def tile_mask(reach_t, reach_w, slab_index, slab_count):
    tile_count = reach_t.shape[0]
    places = jnp.arange(tile_count, dtype=jnp.int32)
    columns = jnp.arange(3 * tile_count, dtype=jnp.int32)
    offsets = columns // tile_count - 1
    key_place = columns % tile_count
    inside = (slab_index + offsets >= 0) & (slab_index + offsets < slab_count)
    near_time = jnp.abs(offsets)[None, :] <= reach_t[:, None]
    near_width = jnp.abs(key_place[None, :] - places[:, None]) <= reach_w[:, None]
    return near_time & near_width & inside[None, :]


def staged(pairs, stages, sems):
    arriving, leaving = [], []
    for i, (source, target) in enumerate(pairs):
        arriving.append(pltpu.make_async_copy(source, stages[i], sems.at[0, i]))
        leaving.append(pltpu.make_async_copy(stages[i], target, sems.at[1, i]))
    for copy in arriving:
        copy.start()
    for first, second in zip(arriving, leaving):
        first.wait()
        second.start()
    for copy in leaving:
        copy.wait()


def stage_shapes(shapes):
    return [pltpu.VMEM(shape, jnp.bfloat16) for shape in shapes] + [
        pltpu.SemaphoreType.DMA((2, len(shapes)))
    ]


def pack(arrays, after, groups, group_width, start, width):
    rows = arrays[0].shape[0]

    def kernel(*refs):
        sources, outs = refs[:3], refs[3 + len(after) : 3 + len(after) + groups]
        stages, sems = refs[3 + len(after) + groups : -1], refs[-1]
        me = lax.axis_index("head")
        pairs = []
        for shift in range(groups):
            group = lax.rem(me + shift, groups)
            column = pl.multiple_of(group * group_width + start, LANES)
            for i, source in enumerate(sources):
                pairs.append(
                    (source.at[:, pl.ds(column, width)], outs[shift].at[:, pl.ds(i * width, width)])
                )
        staged(pairs, stages, sems)

    return pl.pallas_call(
        kernel,
        in_specs=[ANY] * (3 + len(after)),
        out_specs=[ANY] * groups,
        out_shape=[jax.ShapeDtypeStruct((rows, 3 * width), jnp.bfloat16)] * groups,
        scratch_shapes=stage_shapes([(rows, width)] * (3 * groups)),
        cost_estimate=pl.CostEstimate(
            flops=0, bytes_accessed=12 * groups * rows * width, transcendentals=0
        ),
        compiler_params=pltpu.CompilerParams(vmem_limit_bytes=VMEM_LIMIT),
        name="pack",
    )(*arrays, *after)


def assemble(pieces, after, width):
    groups = len(pieces)
    rows = pieces[0].shape[0]

    def kernel(*refs):
        parts, out = refs[:groups], refs[groups + len(after)]
        stages, sems = refs[groups + len(after) + 1 : -1], refs[-1]
        me = lax.axis_index("head")
        pairs = []
        for shift in range(groups):
            owner = lax.rem(me + groups - shift, groups)
            row = pl.multiple_of(owner * rows, 16)
            pairs.append((parts[shift].at[:, pl.ds(0, 2 * width)], out.at[pl.ds(row, rows), :]))
        staged(pairs, stages, sems)

    return pl.pallas_call(
        kernel,
        in_specs=[ANY] * (groups + len(after)),
        out_specs=ANY,
        out_shape=jax.ShapeDtypeStruct((groups * rows, 2 * width), jnp.bfloat16),
        scratch_shapes=stage_shapes([(rows, 2 * width)] * groups),
        cost_estimate=pl.CostEstimate(
            flops=0, bytes_accessed=8 * groups * rows * width, transcendentals=0
        ),
        compiler_params=pltpu.CompilerParams(vmem_limit_bytes=VMEM_LIMIT),
        name="assemble",
    )(*pieces, *after)


def place(chunks, group_width, total_width, target=None):
    groups = len(chunks[0][1])
    rows = chunks[0][1][0].shape[0]
    blocks = [block for _, parts in chunks for block in parts]
    extra = [] if target is None else [target]

    def kernel(*refs):
        out = refs[len(blocks) + len(extra)]
        stages, sems = refs[len(blocks) + len(extra) + 1 : -1], refs[-1]
        me = lax.axis_index("head")
        pairs = []
        for i, (start, parts) in enumerate(chunks):
            for shift, part in enumerate(parts):
                group = lax.rem(me + shift, groups)
                column = pl.multiple_of(group * group_width + start, LANES)
                pairs.append((refs[i * groups + shift], out.at[:, pl.ds(column, part.shape[1])]))
        staged(pairs, stages, sems)

    return pl.pallas_call(
        kernel,
        in_specs=[ANY] * (len(blocks) + len(extra)),
        out_specs=ANY,
        out_shape=jax.ShapeDtypeStruct((rows, total_width), jnp.bfloat16),
        scratch_shapes=stage_shapes([block.shape for block in blocks]),
        input_output_aliases={len(blocks): 0} if extra else {},
        cost_estimate=pl.CostEstimate(
            flops=0,
            bytes_accessed=4 * rows * sum(block.shape[1] for block in blocks),
            transcendentals=0,
        ),
        compiler_params=pltpu.CompilerParams(vmem_limit_bytes=VMEM_LIMIT),
        name="place",
    )(*blocks, *extra)


def lane_fold(op, wide):
    folded = wide[:, :LANES]
    for start in range(LANES, wide.shape[1], LANES):
        folded = op(folded, wide[:, start : start + LANES])
    return folded


def attend_kernel(groups, heads, first_head, tile_count, *refs):
    plan_ref, pieces = refs[0], refs[1 : 1 + groups]
    prev_ref, own_ref, next_ref, keep_ref = refs[1 + groups : 5 + groups]
    outs = refs[-6 - groups : -6]
    q_ref, out_ref, scores_ref, top_ref, total_ref, sum_ref = refs[-6:]
    slab_rows, width = q_ref.shape
    local_rows = slab_rows // groups
    head_size = width // heads
    tile_rows = slab_rows // tile_count
    scale = math.log2(math.e) / math.sqrt(head_size)
    slabs = ((0, prev_ref), (1, own_ref), (2, next_ref))
    me = lax.axis_index("head")

    def owner_rows(shift):
        owner = lax.rem(me + groups - shift, groups)
        return pl.ds(pl.multiple_of(owner * local_rows, 16), local_rows)

    def tile(index):
        return pl.ds(pl.multiple_of(index * tile_rows, tile_rows), tile_rows)

    def lanes(index):
        return pl.ds(index * head_size, head_size)

    for shift in range(groups):
        q_ref[owner_rows(shift), :] = pieces[shift][...]

    def one_tile(i, carry):
        top_ref[...] = jnp.full_like(top_ref, -jnp.inf)
        total_ref[...] = jnp.zeros_like(total_ref)
        sum_ref[...] = jnp.zeros_like(sum_ref)

        for slab, pair_ref in slabs:

            def score(place, carry, slab=slab, pair_ref=pair_ref):
                column = slab * tile_count + place

                @pl.when(plan_ref[i * 3 * tile_count + column] > 0)
                def _():
                    for h in range(heads):
                        found = lax.dot_general(
                            q_ref[tile(i), lanes(h)],
                            pair_ref[tile(place), lanes(h)],
                            (((1,), (1,)), ((), ())),
                            preferred_element_type=jnp.float32,
                        )
                        scores_ref[h, column] = found
                        top_ref[h] = jnp.maximum(top_ref[h], lane_fold(jnp.maximum, found))

                return carry

            lax.fori_loop(0, tile_count, score, 0)

        for h in range(heads):
            highest = jnp.max(top_ref[h], axis=1, keepdims=True) * scale
            top_ref[h] = jnp.broadcast_to(highest, top_ref.shape[1:])

        for slab, pair_ref in slabs:

            def weigh(place, carry, slab=slab, pair_ref=pair_ref):
                column = slab * tile_count + place

                @pl.when(plan_ref[i * 3 * tile_count + column] > 0)
                def _():
                    for h in range(heads):
                        highest = jnp.concatenate([top_ref[h]] * (tile_rows // LANES), axis=1)
                        weights = jnp.exp2(scores_ref[h, column] * scale - highest)
                        total_ref[h] += lane_fold(jnp.add, weights)
                        sum_ref[h] += jnp.dot(
                            weights.astype(jnp.bfloat16),
                            pair_ref[tile(place), lanes(heads + h)],
                            preferred_element_type=jnp.float32,
                        )

                return carry

            lax.fori_loop(0, tile_count, weigh, 0)

        keep = keep_ref[tile(i), :].astype(jnp.float32)
        numbers = lax.broadcasted_iota(jnp.int32, keep.shape, 1)
        for h in range(heads):
            totals = jnp.sum(total_ref[h], axis=1, keepdims=True)
            mine = jnp.where(numbers == first_head + h, keep, 0.0)
            factor = jnp.sum(mine, axis=1, keepdims=True) * (10.0 / 9.0)
            out_ref[tile(i), lanes(h)] = (sum_ref[h] * (factor / totals)).astype(out_ref.dtype)
        return carry

    lax.fori_loop(0, tile_count, one_tile, 0)

    for shift in range(groups):
        outs[shift][...] = out_ref[owner_rows(shift), :]


def attend(plan, pieces, prev, own, behind, keep_mask, after, first_head, heads, tile_count):
    groups = len(pieces)
    slab_rows = own.shape[0]
    local_rows = slab_rows // groups
    width = own.shape[1] // 2
    tile_rows = slab_rows // tile_count
    head_size = width // heads
    pairs = heads * slab_rows * 3 * slab_rows
    whole = pl.BlockSpec(own.shape, lambda s, plan: (0, 0))
    accumulator = pltpu.VMEM((heads, tile_rows, LANES), jnp.float32)
    return pl.pallas_call(
        functools.partial(attend_kernel, groups, heads, first_head, tile_count),
        grid_spec=pltpu.PrefetchScalarGridSpec(
            num_scalar_prefetch=1,
            grid=(1,),
            in_specs=[pl.BlockSpec((local_rows, width), lambda s, plan: (0, 2))] * groups
            + [whole] * 3
            + [pl.BlockSpec(keep_mask.shape, lambda s, plan: (0, 0))]
            + [ANY] * len(after),
            out_specs=[pl.BlockSpec((local_rows, width), lambda s, plan: (0, 0))] * groups,
            scratch_shapes=[
                pltpu.VMEM((slab_rows, width), jnp.bfloat16),
                pltpu.VMEM((slab_rows, width), jnp.bfloat16),
                pltpu.VMEM((heads, 3 * tile_count, tile_rows, tile_rows), jnp.float32),
                accumulator,
                accumulator,
                pltpu.VMEM((heads, tile_rows, head_size), jnp.float32),
            ],
        ),
        out_shape=[jax.ShapeDtypeStruct((local_rows, width), jnp.bfloat16)] * groups,
        compiler_params=pltpu.CompilerParams(vmem_limit_bytes=VMEM_LIMIT),
        cost_estimate=pl.CostEstimate(
            flops=16 * pairs * head_size,
            bytes_accessed=16 * slab_rows * width,
            transcendentals=pairs,
        ),
        name="attend",
    )(plan, *pieces, prev, own, behind, keep_mask, *after)


def on_device(queries, key_vectors, value_vectors, reach_time, reach_width, keep_mask):
    groups = lax.axis_size("head")
    slab_count = lax.axis_size("seq")
    total_width = queries.shape[1]
    group_heads = keep_mask.shape[1]
    group_width = total_width // groups
    head_size = group_width // group_heads
    tile_count = reach_time.shape[0]
    allowed = tile_mask(reach_time, reach_width, lax.axis_index("seq"), slab_count)
    plan = allowed.astype(jnp.int32).reshape(-1)
    onward = [(i, i + 1) for i in range(slab_count - 1)]
    backward = [(i + 1, i) for i in range(slab_count - 1)]

    def turn(array, shift):
        return lax.ppermute(array, "head", [(i, (i + shift) % groups) for i in range(groups)])

    count = min(CHUNKS, group_heads)
    sizes = [group_heads // count + (i < group_heads % count) for i in range(count)]
    firsts = [sum(sizes[:i]) for i in range(count)]
    sources = (key_vectors, value_vectors, queries)

    def send(i, after):
        width = sizes[i] * head_size
        blocks = pack(sources, after, groups, group_width, firsts[i] * head_size, width)
        return [blocks[0]] + [turn(blocks[shift], shift) for shift in range(1, groups)]

    pieces = [send(i, []) for i in range(min(2, count))]
    done = []
    for i, heads in enumerate(sizes):
        own = assemble(
            pieces[i],
            [part[0] for part in pieces[i + 1 :]] + [part[1][0] for part in done[-1:]],
            heads * head_size,
        )
        before = lax.ppermute(own, "seq", onward)
        behind = lax.ppermute(own, "seq", backward)
        if i + 2 < count:
            pieces.append(send(i + 2, [own]))
        hold = [part[0] for part in pieces[i + 2 :]]
        outs = attend(
            plan, pieces[i], before, own, behind, keep_mask, hold, firsts[i], heads, tile_count
        )
        back = [outs[0]] + [turn(outs[shift], groups - shift) for shift in range(1, groups)]
        done.append((firsts[i] * head_size, back))
    early = place(done[:-1], group_width, total_width) if count > 1 else None
    return place(done[-1:], group_width, total_width, early)


def solution(mesh):
    return jax.shard_map(
        on_device,
        mesh=mesh,
        in_specs=(
            P(("seq", "head"), None),
            P(("seq", "head"), None),
            P(("seq", "head"), None),
            P("seq"),
            P("seq"),
            P("seq", "head"),
        ),
        out_specs=P(("seq", "head"), None),
        check_vma=False,
    )
```

```python
import functools
import math

import jax
import jax.numpy as jnp
from jax import lax
from jax.experimental import pallas as pl
from jax.experimental.pallas import tpu as pltpu
from jax.sharding import PartitionSpec as P

LANES = 128
CHUNK_HEADS = 3
ANY = pl.BlockSpec(memory_space=pl.ANY)
VMEM_LIMIT = 56 * 2**20


def tile_mask(reach_t, reach_w, slab_index, slab_count):
    tile_count = reach_t.shape[0]
    places = jnp.arange(tile_count, dtype=jnp.int32)
    columns = jnp.arange(3 * tile_count, dtype=jnp.int32)
    offsets = columns // tile_count - 1
    key_place = columns % tile_count
    inside = (slab_index + offsets >= 0) & (slab_index + offsets < slab_count)
    near_time = jnp.abs(offsets)[None, :] <= reach_t[:, None]
    near_width = jnp.abs(key_place[None, :] - places[:, None]) <= reach_w[:, None]
    return near_time & near_width & inside[None, :]


def staged(pairs, stages, sems):
    arriving, leaving = [], []
    for i, (source, target) in enumerate(pairs):
        arriving.append(pltpu.make_async_copy(source, stages[i], sems.at[0, i]))
        leaving.append(pltpu.make_async_copy(stages[i], target, sems.at[1, i]))
    for copy in arriving:
        copy.start()
    for first, second in zip(arriving, leaving):
        first.wait()
        second.start()
    for copy in leaving:
        copy.wait()


def stage_shapes(shapes):
    return [pltpu.VMEM(shape, jnp.bfloat16) for shape in shapes] + [
        pltpu.SemaphoreType.DMA((2, len(shapes)))
    ]


def pack(arrays, after, groups, group_width, start, width):
    rows = arrays[0].shape[0]

    def kernel(*refs):
        sources, out = refs[:3], refs[3 + len(after)]
        stages, sems = refs[4 + len(after) : -1], refs[-1]
        pairs = []
        for group in range(groups):
            columns = pl.ds(group * group_width + start, width)
            for i, source in enumerate(sources):
                pairs.append((source.at[:, columns], out.at[group, :, pl.ds(i * width, width)]))
        staged(pairs, stages, sems)

    return pl.pallas_call(
        kernel,
        in_specs=[ANY] * (3 + len(after)),
        out_specs=ANY,
        out_shape=jax.ShapeDtypeStruct((groups, rows, 3 * width), jnp.bfloat16),
        scratch_shapes=stage_shapes([(rows, width)] * (3 * groups)),
        cost_estimate=pl.CostEstimate(
            flops=0, bytes_accessed=12 * groups * rows * width, transcendentals=0
        ),
        compiler_params=pltpu.CompilerParams(vmem_limit_bytes=VMEM_LIMIT),
        name="pack",
    )(*arrays, *after)


def gate(array, after):
    def kernel(*refs):
        del refs

    return pl.pallas_call(
        kernel,
        in_specs=[ANY] * (1 + len(after)),
        out_specs=ANY,
        out_shape=jax.ShapeDtypeStruct(array.shape, array.dtype),
        input_output_aliases={0: 0},
        compiler_params=pltpu.CompilerParams(vmem_limit_bytes=VMEM_LIMIT),
        name="gate",
    )(array, *after)


def place(chunks, group_width, total_width, target=None):
    groups = len(chunks[0][1])
    rows = chunks[0][1][0].shape[0]
    blocks = [block for _, parts in chunks for block in parts]
    extra = [] if target is None else [target]

    def kernel(*refs):
        out = refs[len(blocks) + len(extra)]
        stages, sems = refs[len(blocks) + len(extra) + 1 : -1], refs[-1]
        me = lax.axis_index("head")
        pairs = []
        for i, (start, parts) in enumerate(chunks):
            for shift, part in enumerate(parts):
                group = lax.rem(me + shift, groups)
                column = pl.multiple_of(group * group_width + start, LANES)
                pairs.append((refs[i * groups + shift], out.at[:, pl.ds(column, part.shape[1])]))
        staged(pairs, stages, sems)

    return pl.pallas_call(
        kernel,
        in_specs=[ANY] * (len(blocks) + len(extra)),
        out_specs=ANY,
        out_shape=jax.ShapeDtypeStruct((rows, total_width), jnp.bfloat16),
        scratch_shapes=stage_shapes([block.shape for block in blocks]),
        input_output_aliases={len(blocks): 0} if extra else {},
        cost_estimate=pl.CostEstimate(
            flops=0,
            bytes_accessed=4 * rows * sum(block.shape[1] for block in blocks),
            transcendentals=0,
        ),
        compiler_params=pltpu.CompilerParams(vmem_limit_bytes=VMEM_LIMIT),
        name="place",
    )(*blocks, *extra)


def lane_fold(op, wide):
    folded = wide[:, :LANES]
    for start in range(LANES, wide.shape[1], LANES):
        folded = op(folded, wide[:, start : start + LANES])
    return folded


def attend_kernel(groups, heads, first_head, tile_count, *refs):
    plan_ref, own_ref, prev_ref, next_ref, keep_ref = refs[:5]
    outs = refs[-5 - groups : -5]
    out_ref, scores_ref, top_ref, total_ref, sum_ref = refs[-5:]
    slab_rows, width = out_ref.shape
    local_rows = slab_rows // groups
    head_size = width // heads
    tile_rows = slab_rows // tile_count
    scale = math.log2(math.e) / math.sqrt(head_size)
    slabs = ((0, prev_ref), (1, own_ref), (2, next_ref))
    me = lax.axis_index("head")

    def owner_rows(shift):
        owner = lax.rem(me + groups - shift, groups)
        return pl.ds(pl.multiple_of(owner * local_rows, 16), local_rows)

    def tile(index):
        return pl.ds(pl.multiple_of(index * tile_rows, tile_rows), tile_rows)

    def lanes(index):
        return pl.ds(index * head_size, head_size)

    def one_tile(i, carry):
        top_ref[...] = jnp.full_like(top_ref, -jnp.inf)
        total_ref[...] = jnp.zeros_like(total_ref)
        sum_ref[...] = jnp.zeros_like(sum_ref)

        for slab, pair_ref in slabs:

            def score(place, carry, slab=slab, pair_ref=pair_ref):
                column = slab * tile_count + place

                @pl.when(plan_ref[i * 3 * tile_count + column] > 0)
                def _():
                    for h in range(heads):
                        found = lax.dot_general(
                            own_ref[tile(i), lanes(2 * heads + h)],
                            pair_ref[tile(place), lanes(h)],
                            (((1,), (1,)), ((), ())),
                            preferred_element_type=jnp.float32,
                        )
                        scores_ref[h, column] = found
                        top_ref[h] = jnp.maximum(top_ref[h], lane_fold(jnp.maximum, found))

                return carry

            lax.fori_loop(0, tile_count, score, 0)

        for h in range(heads):
            highest = jnp.max(top_ref[h], axis=1, keepdims=True) * scale
            top_ref[h] = jnp.broadcast_to(highest, top_ref.shape[1:])

        for slab, pair_ref in slabs:

            def weigh(place, carry, slab=slab, pair_ref=pair_ref):
                column = slab * tile_count + place

                @pl.when(plan_ref[i * 3 * tile_count + column] > 0)
                def _():
                    for h in range(heads):
                        highest = jnp.concatenate([top_ref[h]] * (tile_rows // LANES), axis=1)
                        weights = jnp.exp2(scores_ref[h, column] * scale - highest)
                        total_ref[h] += lane_fold(jnp.add, weights)
                        sum_ref[h] += jnp.dot(
                            weights.astype(jnp.bfloat16),
                            pair_ref[tile(place), lanes(heads + h)],
                            preferred_element_type=jnp.float32,
                        )

                return carry

            lax.fori_loop(0, tile_count, weigh, 0)

        keep = keep_ref[tile(i), :].astype(jnp.float32)
        numbers = lax.broadcasted_iota(jnp.int32, keep.shape, 1)
        for h in range(heads):
            totals = jnp.sum(total_ref[h], axis=1, keepdims=True)
            mine = jnp.where(numbers == first_head + h, keep, 0.0)
            factor = jnp.sum(mine, axis=1, keepdims=True) * (10.0 / 9.0)
            out_ref[tile(i), lanes(h)] = (sum_ref[h] * (factor / totals)).astype(out_ref.dtype)
        return carry

    lax.fori_loop(0, tile_count, one_tile, 0)

    for shift in range(groups):
        outs[shift][...] = out_ref[owner_rows(shift), :]


def attend(plan, own, prev, behind, keep_mask, after, groups, first_head, heads, tile_count):
    slab_rows, width = own.shape[0], own.shape[1] // 3
    local_rows = slab_rows // groups
    tile_rows = slab_rows // tile_count
    head_size = width // heads
    pairs = heads * slab_rows * 3 * slab_rows
    wholes = [
        pl.BlockSpec(array.shape, lambda s, plan: (0, 0))
        for array in (own, prev, behind, keep_mask)
    ]
    accumulator = pltpu.VMEM((heads, tile_rows, LANES), jnp.float32)
    return pl.pallas_call(
        functools.partial(attend_kernel, groups, heads, first_head, tile_count),
        grid_spec=pltpu.PrefetchScalarGridSpec(
            num_scalar_prefetch=1,
            grid=(1,),
            in_specs=wholes + [ANY] * len(after),
            out_specs=[pl.BlockSpec((local_rows, width), lambda s, plan: (0, 0))] * groups,
            scratch_shapes=[
                pltpu.VMEM((slab_rows, width), jnp.bfloat16),
                pltpu.VMEM((heads, 3 * tile_count, tile_rows, tile_rows), jnp.float32),
                accumulator,
                accumulator,
                pltpu.VMEM((heads, tile_rows, head_size), jnp.float32),
            ],
        ),
        out_shape=[jax.ShapeDtypeStruct((local_rows, width), jnp.bfloat16)] * groups,
        compiler_params=pltpu.CompilerParams(vmem_limit_bytes=VMEM_LIMIT),
        cost_estimate=pl.CostEstimate(
            flops=16 * pairs * head_size,
            bytes_accessed=16 * slab_rows * width,
            transcendentals=pairs,
        ),
        name="attend",
    )(plan, own, prev, behind, keep_mask, *after)


def on_device(queries, key_vectors, value_vectors, reach_time, reach_width, keep_mask):
    groups = lax.axis_size("head")
    slab_count = lax.axis_size("seq")
    total_width = queries.shape[1]
    group_heads = keep_mask.shape[1]
    group_width = total_width // groups
    head_size = group_width // group_heads
    tile_count = reach_time.shape[0]
    allowed = tile_mask(reach_time, reach_width, lax.axis_index("seq"), slab_count)
    plan = allowed.astype(jnp.int32).reshape(-1)
    onward = [(i, i + 1) for i in range(slab_count - 1)]
    backward = [(i + 1, i) for i in range(slab_count - 1)]

    def turn(array, shift):
        return lax.ppermute(array, "head", [(i, (i + shift) % groups) for i in range(groups)])

    parts = -(-(group_heads - 1) // CHUNK_HEADS)
    sizes = [(group_heads - 1 + i) // parts for i in reversed(range(parts))] + [1]
    count = len(sizes)
    firsts = [sum(sizes[:i]) for i in range(count)]
    sources = (key_vectors, value_vectors, queries)

    def packed(i, after):
        start, width = firsts[i] * head_size, sizes[i] * head_size
        return pack(sources, after, groups, group_width, start, width)

    def arrive(parts, after):
        own = lax.all_to_all(parts, "head", split_axis=0, concat_axis=0, tiled=True)
        own = gate(own, after) if after else own
        own = own.reshape(-1, own.shape[2])
        pairs = own[:, : own.shape[1] // 3 * 2]
        return own, lax.ppermute(pairs, "seq", onward), lax.ppermute(pairs, "seq", backward)

    sent = [packed(i, []) for i in range(min(2, count))]
    there, done = [arrive(sent[0], [])], []
    if count > 1:
        sent[1] = gate(sent[1], there[0][:1])
    for i, heads in enumerate(sizes):
        if i + 1 < count:
            there.append(arrive(sent[i + 1], [part[1][0] for part in done[-1:]]))
        if i + 2 < count:
            sent.append(gate(packed(i + 2, [there[i][0]]), there[i + 1][:1]))
        hold = [part[0] for part in there[i + 1 :]] + sent[i + 2 :]
        hold += [part[1][0] for part in done[-1:]]
        hold += [block for part in done[-2:-1] for block in part[1][1:]]
        outs = attend(
            plan, *there[i], keep_mask, hold, groups, firsts[i], heads, tile_count
        )
        back = [outs[0]] + [turn(outs[shift], groups - shift) for shift in range(1, groups)]
        done.append((firsts[i] * head_size, back))
    early = place(done[:-1], group_width, total_width) if count > 1 else None
    return place(done[-1:], group_width, total_width, early)


def solution(mesh):
    return jax.shard_map(
        on_device,
        mesh=mesh,
        in_specs=(
            P(("seq", "head"), None),
            P(("seq", "head"), None),
            P(("seq", "head"), None),
            P("seq"),
            P("seq"),
            P("seq", "head"),
        ),
        out_specs=P(("seq", "head"), None),
        check_vma=False,
    )
```

```python
import functools
import math

import jax
import jax.numpy as jnp
from jax import lax
from jax.experimental import pallas as pl
from jax.experimental.pallas import tpu as pltpu
from jax.sharding import PartitionSpec as P

LANES = 128
CHUNK_HEADS = 3
ANY = pl.BlockSpec(memory_space=pl.ANY)
VMEM_LIMIT = 60 * 2**20


def tile_mask(reach_t, reach_w, slab_index, slab_count):
    tile_count = reach_t.shape[0]
    places = jnp.arange(tile_count, dtype=jnp.int32)
    columns = jnp.arange(3 * tile_count, dtype=jnp.int32)
    offsets = columns // tile_count - 1
    key_place = columns % tile_count
    inside = (slab_index + offsets >= 0) & (slab_index + offsets < slab_count)
    near_time = jnp.abs(offsets)[None, :] <= reach_t[:, None]
    near_width = jnp.abs(key_place[None, :] - places[:, None]) <= reach_w[:, None]
    return near_time & near_width & inside[None, :]


def staged(pairs, stages, sems):
    arriving, leaving = [], []
    for i, (source, target) in enumerate(pairs):
        arriving.append(pltpu.make_async_copy(source, stages[i], sems.at[0, i]))
        leaving.append(pltpu.make_async_copy(stages[i], target, sems.at[1, i]))
    for copy in arriving:
        copy.start()
    for first, second in zip(arriving, leaving):
        first.wait()
        second.start()
    for copy in leaving:
        copy.wait()


def stage_shapes(shapes):
    return [pltpu.VMEM(shape, jnp.bfloat16) for shape in shapes] + [
        pltpu.SemaphoreType.DMA((2, len(shapes)))
    ]


def pack(arrays, after, groups, group_width, start, width):
    rows = arrays[0].shape[0]

    def kernel(*refs):
        sources, out = refs[: len(arrays)], refs[len(arrays) + len(after)]
        stages, sems = refs[len(arrays) + len(after) + 1 : -1], refs[-1]
        pairs = []
        for group in range(groups):
            columns = pl.ds(group * group_width + start, width)
            for i, source in enumerate(sources):
                pairs.append((source.at[:, columns], out.at[group, :, pl.ds(i * width, width)]))
        staged(pairs, stages, sems)

    return pl.pallas_call(
        kernel,
        in_specs=[ANY] * (len(arrays) + len(after)),
        out_specs=ANY,
        out_shape=jax.ShapeDtypeStruct((groups, rows, len(arrays) * width), jnp.bfloat16),
        scratch_shapes=stage_shapes([(rows, width)] * (len(arrays) * groups)),
        cost_estimate=pl.CostEstimate(
            flops=0,
            bytes_accessed=4 * len(arrays) * groups * rows * width,
            transcendentals=0,
        ),
        compiler_params=pltpu.CompilerParams(vmem_limit_bytes=VMEM_LIMIT),
        name="pack",
    )(*arrays, *after)


def pack_turned(array, after, groups, group_width, start, width):
    rows = array.shape[0]

    def kernel(*refs):
        outs = refs[1 + len(after) : 1 + len(after) + groups]
        stages, sems = refs[1 + len(after) + groups : -1], refs[-1]
        me = lax.axis_index("head")
        pairs = []
        for shift in range(groups):
            group = lax.rem(me + shift, groups)
            column = pl.multiple_of(group * group_width + start, LANES)
            pairs.append((refs[0].at[:, pl.ds(column, width)], outs[shift]))
        staged(pairs, stages, sems)

    return pl.pallas_call(
        kernel,
        in_specs=[ANY] * (1 + len(after)),
        out_specs=[ANY] * groups,
        out_shape=[jax.ShapeDtypeStruct((rows, width), jnp.bfloat16)] * groups,
        scratch_shapes=stage_shapes([(rows, width)] * groups),
        cost_estimate=pl.CostEstimate(
            flops=0, bytes_accessed=4 * groups * rows * width, transcendentals=0
        ),
        compiler_params=pltpu.CompilerParams(vmem_limit_bytes=VMEM_LIMIT),
        name="pack_turned",
    )(array, *after)


def gate(array, after):
    def kernel(*refs):
        del refs

    return pl.pallas_call(
        kernel,
        in_specs=[ANY] * (1 + len(after)),
        out_specs=ANY,
        out_shape=jax.ShapeDtypeStruct(array.shape, array.dtype),
        input_output_aliases={0: 0},
        compiler_params=pltpu.CompilerParams(vmem_limit_bytes=VMEM_LIMIT),
        name="gate",
    )(array, *after)


def place(chunks, group_width, total_width, target=None):
    groups = len(chunks[0][1])
    rows = chunks[0][1][0].shape[0]
    blocks = [block for _, parts in chunks for block in parts]
    extra = [] if target is None else [target]

    def kernel(*refs):
        out = refs[len(blocks) + len(extra)]
        stages, sems = refs[len(blocks) + len(extra) + 1 : -1], refs[-1]
        me = lax.axis_index("head")
        pairs = []
        for i, (start, parts) in enumerate(chunks):
            for shift, part in enumerate(parts):
                group = lax.rem(me + shift, groups)
                column = pl.multiple_of(group * group_width + start, LANES)
                pairs.append((refs[i * groups + shift], out.at[:, pl.ds(column, part.shape[1])]))
        staged(pairs, stages, sems)

    return pl.pallas_call(
        kernel,
        in_specs=[ANY] * (len(blocks) + len(extra)),
        out_specs=ANY,
        out_shape=jax.ShapeDtypeStruct((rows, total_width), jnp.bfloat16),
        scratch_shapes=stage_shapes([block.shape for block in blocks]),
        input_output_aliases={len(blocks): 0} if extra else {},
        cost_estimate=pl.CostEstimate(
            flops=0,
            bytes_accessed=4 * rows * sum(block.shape[1] for block in blocks),
            transcendentals=0,
        ),
        compiler_params=pltpu.CompilerParams(vmem_limit_bytes=VMEM_LIMIT),
        name="place",
    )(*blocks, *extra)


def lane_fold(op, wide):
    folded = wide[:, :LANES]
    for start in range(LANES, wide.shape[1], LANES):
        folded = op(folded, wide[:, start : start + LANES])
    return folded


def attend_kernel(groups, heads, first_head, tile_count, *refs):
    plan_ref, own_ref, prev_ref, next_ref, keep_ref = refs[:5]
    pieces = refs[5 : 5 + groups]
    outs = refs[-6 - groups : -6]
    q_ref, out_ref, scores_ref, top_ref, total_ref, sum_ref = refs[-6:]
    slab_rows, width = out_ref.shape
    local_rows = slab_rows // groups
    head_size = width // heads
    tile_rows = slab_rows // tile_count
    scale = math.log2(math.e) / math.sqrt(head_size)
    slabs = ((0, prev_ref), (1, own_ref), (2, next_ref))
    me = lax.axis_index("head")

    def owner_rows(shift):
        owner = lax.rem(me + groups - shift, groups)
        return pl.ds(pl.multiple_of(owner * local_rows, 16), local_rows)

    def tile(index):
        return pl.ds(pl.multiple_of(index * tile_rows, tile_rows), tile_rows)

    def lanes(index):
        return pl.ds(index * head_size, head_size)

    for shift in range(groups):
        q_ref[owner_rows(shift), :] = pieces[shift][...]

    def one_tile(i, carry):
        top_ref[...] = jnp.full_like(top_ref, -jnp.inf)
        total_ref[...] = jnp.zeros_like(total_ref)
        sum_ref[...] = jnp.zeros_like(sum_ref)

        for slab, pair_ref in slabs:

            def score(place, carry, slab=slab, pair_ref=pair_ref):
                column = slab * tile_count + place

                @pl.when(plan_ref[i * 3 * tile_count + column] > 0)
                def _():
                    for h in range(heads):
                        found = lax.dot_general(
                            q_ref[tile(i), lanes(h)],
                            pair_ref[tile(place), lanes(h)],
                            (((1,), (1,)), ((), ())),
                            preferred_element_type=jnp.float32,
                        )
                        scores_ref[h, column] = found
                        top_ref[h] = jnp.maximum(top_ref[h], lane_fold(jnp.maximum, found))

                return carry

            lax.fori_loop(0, tile_count, score, 0)

        for h in range(heads):
            highest = jnp.max(top_ref[h], axis=1, keepdims=True) * scale
            top_ref[h] = jnp.broadcast_to(highest, top_ref.shape[1:])

        for slab, pair_ref in slabs:

            def weigh(place, carry, slab=slab, pair_ref=pair_ref):
                column = slab * tile_count + place

                @pl.when(plan_ref[i * 3 * tile_count + column] > 0)
                def _():
                    for h in range(heads):
                        highest = jnp.concatenate([top_ref[h]] * (tile_rows // LANES), axis=1)
                        weights = jnp.exp2(scores_ref[h, column] * scale - highest)
                        total_ref[h] += lane_fold(jnp.add, weights)
                        sum_ref[h] += jnp.dot(
                            weights.astype(jnp.bfloat16),
                            pair_ref[tile(place), lanes(heads + h)],
                            preferred_element_type=jnp.float32,
                        )

                return carry

            lax.fori_loop(0, tile_count, weigh, 0)

        keep = keep_ref[tile(i), :].astype(jnp.float32)
        numbers = lax.broadcasted_iota(jnp.int32, keep.shape, 1)
        for h in range(heads):
            totals = jnp.sum(total_ref[h], axis=1, keepdims=True)
            mine = jnp.where(numbers == first_head + h, keep, 0.0)
            factor = jnp.sum(mine, axis=1, keepdims=True) * (10.0 / 9.0)
            out_ref[tile(i), lanes(h)] = (sum_ref[h] * (factor / totals)).astype(out_ref.dtype)
        return carry

    lax.fori_loop(0, tile_count, one_tile, 0)

    for shift in range(groups):
        outs[shift][...] = out_ref[owner_rows(shift), :]


def attend(plan, own, prev, behind, keep_mask, pieces, after, first_head, heads, tile_count):
    groups = len(pieces)
    slab_rows, width = own.shape[0], own.shape[1] // 2
    local_rows = slab_rows // groups
    tile_rows = slab_rows // tile_count
    head_size = width // heads
    pairs = heads * slab_rows * 3 * slab_rows
    wholes = [
        pl.BlockSpec(array.shape, lambda s, plan: (0, 0))
        for array in (own, prev, behind, keep_mask, *pieces)
    ]
    accumulator = pltpu.VMEM((heads, tile_rows, LANES), jnp.float32)
    return pl.pallas_call(
        functools.partial(attend_kernel, groups, heads, first_head, tile_count),
        grid_spec=pltpu.PrefetchScalarGridSpec(
            num_scalar_prefetch=1,
            grid=(1,),
            in_specs=wholes + [ANY] * len(after),
            out_specs=[pl.BlockSpec((local_rows, width), lambda s, plan: (0, 0))] * groups,
            scratch_shapes=[
                pltpu.VMEM((slab_rows, width), jnp.bfloat16),
                pltpu.VMEM((slab_rows, width), jnp.bfloat16),
                pltpu.VMEM((heads, 3 * tile_count, tile_rows, tile_rows), jnp.float32),
                accumulator,
                accumulator,
                pltpu.VMEM((heads, tile_rows, head_size), jnp.float32),
            ],
        ),
        out_shape=[jax.ShapeDtypeStruct((local_rows, width), jnp.bfloat16)] * groups,
        compiler_params=pltpu.CompilerParams(vmem_limit_bytes=VMEM_LIMIT),
        cost_estimate=pl.CostEstimate(
            flops=16 * pairs * head_size,
            bytes_accessed=16 * slab_rows * width,
            transcendentals=pairs,
        ),
        name="attend",
    )(plan, own, prev, behind, keep_mask, *pieces, *after)


def on_device(queries, key_vectors, value_vectors, reach_time, reach_width, keep_mask):
    groups = lax.axis_size("head")
    slab_count = lax.axis_size("seq")
    total_width = queries.shape[1]
    group_heads = keep_mask.shape[1]
    group_width = total_width // groups
    head_size = group_width // group_heads
    tile_count = reach_time.shape[0]
    allowed = tile_mask(reach_time, reach_width, lax.axis_index("seq"), slab_count)
    plan = allowed.astype(jnp.int32).reshape(-1)
    onward = [(i, i + 1) for i in range(slab_count - 1)]
    backward = [(i + 1, i) for i in range(slab_count - 1)]

    def turn(array, shift):
        return lax.ppermute(array, "head", [(i, (i + shift) % groups) for i in range(groups)])

    parts = -(-(group_heads - 1) // CHUNK_HEADS)
    sizes = [(group_heads - 1 + i) // parts for i in reversed(range(parts))] + [1]
    count = len(sizes)
    firsts = [sum(sizes[:i]) for i in range(count)]

    def packed(i, after):
        arrays = (key_vectors, value_vectors)
        start, width = firsts[i] * head_size, sizes[i] * head_size
        return pack(arrays, after, groups, group_width, start, width)

    def asked(i, after):
        start, width = firsts[i] * head_size, sizes[i] * head_size
        blocks = pack_turned(queries, after, groups, group_width, start, width)
        return [blocks[0]] + [turn(blocks[shift], shift) for shift in range(1, groups)]

    def arrive(parts, after):
        own = lax.all_to_all(parts, "head", split_axis=0, concat_axis=0, tiled=True)
        own = gate(own, after) if after else own
        own = own.reshape(-1, own.shape[2])
        return own, lax.ppermute(own, "seq", onward), lax.ppermute(own, "seq", backward)

    sent = [packed(0, [])]
    there, asks, done, early = [arrive(sent[0], [])], [asked(0, sent)], [], None
    if count > 1:
        sent.append(gate(packed(1, sent), there[0][:1]))
        asks.append(asked(1, there[0][:1]))
    for i, heads in enumerate(sizes):
        if i + 1 < count:
            there.append(arrive(sent[i + 1], [part[1][0] for part in done[-1:]]))
        if i + 2 < count:
            sent.append(gate(packed(i + 2, there[i][:1]), there[i + 1][:1]))
            asks.append(asked(i + 2, there[i + 1][:1]))
        hold = [part[0] for part in there[i + 1 :] + asks[i + 2 :]] + sent[i + 2 :]
        hold += [part[1][0] for part in done[-1:]]
        hold += [block for part in done[-2:-1] for block in part[1][1:]]
        if i + 1 == count and count > 2:
            early = place(done[:-1], group_width, total_width)
            hold.append(early)
        outs = attend(
            plan, *there[i], keep_mask, asks[i], hold, firsts[i], heads, tile_count
        )
        back = [outs[0]] + [turn(outs[shift], groups - shift) for shift in range(1, groups)]
        done.append((firsts[i] * head_size, back))
    return place(done[-2:] if count > 2 else done, group_width, total_width, early)


def solution(mesh):
    return jax.shard_map(
        on_device,
        mesh=mesh,
        in_specs=(
            P(("seq", "head"), None),
            P(("seq", "head"), None),
            P(("seq", "head"), None),
            P("seq"),
            P("seq"),
            P("seq", "head"),
        ),
        out_specs=P(("seq", "head"), None),
        check_vma=False,
    )
```

```python
import functools
import math

import jax
import jax.numpy as jnp
from jax import lax
from jax.experimental import pallas as pl
from jax.experimental.pallas import tpu as pltpu
from jax.sharding import PartitionSpec as P

LANES = 128
LARGEST_CHUNK = 4
ANY = pl.BlockSpec(memory_space=pl.ANY)
VMEM_LIMIT = 60 * 2**20


def tile_mask(reach_t, reach_w, slab_index, slab_count):
    tile_count = reach_t.shape[0]
    places = jnp.arange(tile_count, dtype=jnp.int32)
    columns = jnp.arange(3 * tile_count, dtype=jnp.int32)
    offsets = columns // tile_count - 1
    key_place = columns % tile_count
    inside = (slab_index + offsets >= 0) & (slab_index + offsets < slab_count)
    near_time = jnp.abs(offsets)[None, :] <= reach_t[:, None]
    near_width = jnp.abs(key_place[None, :] - places[:, None]) <= reach_w[:, None]
    return near_time & near_width & inside[None, :]


def staged(pairs, stages, sems):
    arriving, leaving = [], []
    for i, (source, target) in enumerate(pairs):
        arriving.append(pltpu.make_async_copy(source, stages[i], sems.at[0, i]))
        leaving.append(pltpu.make_async_copy(stages[i], target, sems.at[1, i]))
    for copy in arriving:
        copy.start()
    for first, second in zip(arriving, leaving):
        first.wait()
        second.start()
    for copy in leaving:
        copy.wait()


def stage_shapes(shapes):
    return [pltpu.VMEM(shape, jnp.bfloat16) for shape in shapes] + [
        pltpu.SemaphoreType.DMA((2, len(shapes)))
    ]


def pack(arrays, after, groups, group_width, start, width):
    rows = arrays[0].shape[0]

    def kernel(*refs):
        sources, out = refs[: len(arrays)], refs[len(arrays) + len(after)]
        stages, sems = refs[len(arrays) + len(after) + 1 : -1], refs[-1]
        pairs = []
        for group in range(groups):
            columns = pl.ds(group * group_width + start, width)
            for i, source in enumerate(sources):
                pairs.append((source.at[:, columns], out.at[group, :, pl.ds(i * width, width)]))
        staged(pairs, stages, sems)

    return pl.pallas_call(
        kernel,
        in_specs=[ANY] * (len(arrays) + len(after)),
        out_specs=ANY,
        out_shape=jax.ShapeDtypeStruct((groups, rows, len(arrays) * width), jnp.bfloat16),
        scratch_shapes=stage_shapes([(rows, width)] * (len(arrays) * groups)),
        cost_estimate=pl.CostEstimate(
            flops=0,
            bytes_accessed=4 * len(arrays) * groups * rows * width,
            transcendentals=0,
        ),
        compiler_params=pltpu.CompilerParams(vmem_limit_bytes=VMEM_LIMIT),
        name="pack",
    )(*arrays, *after)


def pack_turned(array, after, groups, group_width, start, width):
    rows = array.shape[0]

    def kernel(*refs):
        outs = refs[1 + len(after) : 1 + len(after) + groups]
        stages, sems = refs[1 + len(after) + groups : -1], refs[-1]
        me = lax.axis_index("head")
        pairs = []
        for shift in range(groups):
            group = lax.rem(me + shift, groups)
            column = pl.multiple_of(group * group_width + start, LANES)
            pairs.append((refs[0].at[:, pl.ds(column, width)], outs[shift]))
        staged(pairs, stages, sems)

    return pl.pallas_call(
        kernel,
        in_specs=[ANY] * (1 + len(after)),
        out_specs=[ANY] * groups,
        out_shape=[jax.ShapeDtypeStruct((rows, width), jnp.bfloat16)] * groups,
        scratch_shapes=stage_shapes([(rows, width)] * groups),
        cost_estimate=pl.CostEstimate(
            flops=0, bytes_accessed=4 * groups * rows * width, transcendentals=0
        ),
        compiler_params=pltpu.CompilerParams(vmem_limit_bytes=VMEM_LIMIT),
        name="pack_turned",
    )(array, *after)


def gate(array, after):
    def kernel(*refs):
        del refs

    return pl.pallas_call(
        kernel,
        in_specs=[ANY] * (1 + len(after)),
        out_specs=ANY,
        out_shape=jax.ShapeDtypeStruct(array.shape, array.dtype),
        input_output_aliases={0: 0},
        compiler_params=pltpu.CompilerParams(vmem_limit_bytes=VMEM_LIMIT),
        name="gate",
    )(array, *after)


def place(chunks, group_width, total_width, target=None):
    groups = len(chunks[0][1])
    rows = chunks[0][1][0].shape[0]
    blocks = [block for _, parts in chunks for block in parts]
    extra = [] if target is None else [target]

    def kernel(*refs):
        out = refs[len(blocks) + len(extra)]
        stages, sems = refs[len(blocks) + len(extra) + 1 : -1], refs[-1]
        me = lax.axis_index("head")
        pairs = []
        for i, (start, parts) in enumerate(chunks):
            for shift, part in enumerate(parts):
                group = lax.rem(me + shift, groups)
                column = pl.multiple_of(group * group_width + start, LANES)
                pairs.append((refs[i * groups + shift], out.at[:, pl.ds(column, part.shape[1])]))
        staged(pairs, stages, sems)

    return pl.pallas_call(
        kernel,
        in_specs=[ANY] * (len(blocks) + len(extra)),
        out_specs=ANY,
        out_shape=jax.ShapeDtypeStruct((rows, total_width), jnp.bfloat16),
        scratch_shapes=stage_shapes([block.shape for block in blocks]),
        input_output_aliases={len(blocks): 0} if extra else {},
        cost_estimate=pl.CostEstimate(
            flops=0,
            bytes_accessed=4 * rows * sum(block.shape[1] for block in blocks),
            transcendentals=0,
        ),
        compiler_params=pltpu.CompilerParams(vmem_limit_bytes=VMEM_LIMIT),
        name="place",
    )(*blocks, *extra)


def lane_fold(op, wide):
    folded = wide[:, :LANES]
    for start in range(LANES, wide.shape[1], LANES):
        folded = op(folded, wide[:, start : start + LANES])
    return folded


def attend_kernel(groups, heads, first_head, tile_count, in_pieces, *refs):
    plan_ref, own_ref, prev_ref, next_ref, keep_ref = refs[:5]
    pieces = refs[5 : 5 + groups] if in_pieces else ()
    outs = refs[-6 - groups : -6]
    q_ref, out_ref, scores_ref, top_ref, total_ref, sum_ref = refs[-6:]
    slab_rows, width = out_ref.shape
    local_rows = slab_rows // groups
    head_size = width // heads
    tile_rows = slab_rows // tile_count
    scale = math.log2(math.e) / math.sqrt(head_size)
    slabs = ((0, prev_ref), (1, own_ref), (2, next_ref))
    me = lax.axis_index("head")

    def owner_rows(shift):
        owner = lax.rem(me + groups - shift, groups)
        return pl.ds(pl.multiple_of(owner * local_rows, 16), local_rows)

    def tile(index):
        return pl.ds(pl.multiple_of(index * tile_rows, tile_rows), tile_rows)

    def lanes(index):
        return pl.ds(index * head_size, head_size)

    for shift, piece in enumerate(pieces):
        q_ref[owner_rows(shift), :] = piece[...]
    query_ref, first_query = (q_ref, 0) if pieces else (own_ref, 2 * heads)

    def one_tile(i, carry):
        top_ref[...] = jnp.full_like(top_ref, -jnp.inf)
        total_ref[...] = jnp.zeros_like(total_ref)
        sum_ref[...] = jnp.zeros_like(sum_ref)

        for slab, pair_ref in slabs:

            def score(place, carry, slab=slab, pair_ref=pair_ref):
                column = slab * tile_count + place

                @pl.when(plan_ref[i * 3 * tile_count + column] > 0)
                def _():
                    for h in range(heads):
                        found = lax.dot_general(
                            query_ref[tile(i), lanes(first_query + h)],
                            pair_ref[tile(place), lanes(h)],
                            (((1,), (1,)), ((), ())),
                            preferred_element_type=jnp.float32,
                        )
                        scores_ref[h, column] = found
                        top_ref[h] = jnp.maximum(top_ref[h], lane_fold(jnp.maximum, found))

                return carry

            lax.fori_loop(0, tile_count, score, 0)

        for h in range(heads):
            highest = jnp.max(top_ref[h], axis=1, keepdims=True) * scale
            top_ref[h] = jnp.broadcast_to(highest, top_ref.shape[1:])

        for slab, pair_ref in slabs:

            def weigh(place, carry, slab=slab, pair_ref=pair_ref):
                column = slab * tile_count + place

                @pl.when(plan_ref[i * 3 * tile_count + column] > 0)
                def _():
                    for h in range(heads):
                        highest = jnp.concatenate([top_ref[h]] * (tile_rows // LANES), axis=1)
                        weights = jnp.exp2(scores_ref[h, column] * scale - highest)
                        total_ref[h] += lane_fold(jnp.add, weights)
                        sum_ref[h] += jnp.dot(
                            weights.astype(jnp.bfloat16),
                            pair_ref[tile(place), lanes(heads + h)],
                            preferred_element_type=jnp.float32,
                        )

                return carry

            lax.fori_loop(0, tile_count, weigh, 0)

        keep = keep_ref[tile(i), :].astype(jnp.float32)
        numbers = lax.broadcasted_iota(jnp.int32, keep.shape, 1)
        for h in range(heads):
            totals = jnp.sum(total_ref[h], axis=1, keepdims=True)
            mine = jnp.where(numbers == first_head + h, keep, 0.0)
            factor = jnp.sum(mine, axis=1, keepdims=True) * (10.0 / 9.0)
            out_ref[tile(i), lanes(h)] = (sum_ref[h] * (factor / totals)).astype(out_ref.dtype)
        return carry

    lax.fori_loop(0, tile_count, one_tile, 0)

    for shift in range(groups):
        outs[shift][...] = out_ref[owner_rows(shift), :]


def attend(
    plan, own, prev, behind, keep_mask, pieces, after, groups, first_head, heads, tile_count
):
    slab_rows, width = prev.shape[0], prev.shape[1] // 2
    local_rows = slab_rows // groups
    tile_rows = slab_rows // tile_count
    head_size = width // heads
    pairs = heads * slab_rows * 3 * slab_rows
    wholes = [
        pl.BlockSpec(array.shape, lambda s, plan: (0, 0))
        for array in (own, prev, behind, keep_mask, *pieces)
    ]
    accumulator = pltpu.VMEM((heads, tile_rows, LANES), jnp.float32)
    return pl.pallas_call(
        functools.partial(attend_kernel, groups, heads, first_head, tile_count, bool(pieces)),
        grid_spec=pltpu.PrefetchScalarGridSpec(
            num_scalar_prefetch=1,
            grid=(1,),
            in_specs=wholes + [ANY] * len(after),
            out_specs=[pl.BlockSpec((local_rows, width), lambda s, plan: (0, 0))] * groups,
            scratch_shapes=[
                pltpu.VMEM((slab_rows, width), jnp.bfloat16),
                pltpu.VMEM((slab_rows, width), jnp.bfloat16),
                pltpu.VMEM((heads, 3 * tile_count, tile_rows, tile_rows), jnp.float32),
                accumulator,
                accumulator,
                pltpu.VMEM((heads, tile_rows, head_size), jnp.float32),
            ],
        ),
        out_shape=[jax.ShapeDtypeStruct((local_rows, width), jnp.bfloat16)] * groups,
        compiler_params=pltpu.CompilerParams(vmem_limit_bytes=VMEM_LIMIT),
        cost_estimate=pl.CostEstimate(
            flops=16 * pairs * head_size,
            bytes_accessed=16 * slab_rows * width,
            transcendentals=pairs,
        ),
        name="attend",
    )(plan, own, prev, behind, keep_mask, *pieces, *after)


def on_device(queries, key_vectors, value_vectors, reach_time, reach_width, keep_mask):
    groups = lax.axis_size("head")
    slab_count = lax.axis_size("seq")
    total_width = queries.shape[1]
    group_heads = keep_mask.shape[1]
    group_width = total_width // groups
    head_size = group_width // group_heads
    tile_count = reach_time.shape[0]
    allowed = tile_mask(reach_time, reach_width, lax.axis_index("seq"), slab_count)
    plan = allowed.astype(jnp.int32).reshape(-1)
    onward = [(i, i + 1) for i in range(slab_count - 1)]
    backward = [(i + 1, i) for i in range(slab_count - 1)]

    def turn(array, shift):
        return lax.ppermute(array, "head", [(i, (i + shift) % groups) for i in range(groups)])

    sizes, left = [], group_heads
    while left:
        sizes.append(min(len(sizes) + 1, LARGEST_CHUNK, left))
        left -= sizes[-1]
    sizes.sort(reverse=True)
    count = len(sizes)
    firsts = [sum(sizes[:i]) for i in range(count)]

    def packed(i, after):
        arrays = (key_vectors, value_vectors, queries)[: 2 + (i + 1 == count)]
        start, width = firsts[i] * head_size, sizes[i] * head_size
        return pack(arrays, after, groups, group_width, start, width)

    def asked(i, after):
        start, width = firsts[i] * head_size, sizes[i] * head_size
        blocks = pack_turned(queries, after, groups, group_width, start, width)
        return [blocks[0]] + [turn(blocks[shift], shift) for shift in range(1, groups)]

    def arrive(i, after):
        own = lax.all_to_all(sent[i], "head", split_axis=0, concat_axis=0, tiled=True)
        own = gate(own, after) if after else own
        own = own.reshape(-1, own.shape[2])
        pairs = own[:, : 2 * sizes[i] * head_size]
        return own, lax.ppermute(pairs, "seq", onward), lax.ppermute(pairs, "seq", backward)

    sent, there, asks, done, early = [packed(0, [])], [], [], [], None
    there.append(arrive(0, []))
    if count > 1:
        asks.append(asked(0, sent))
        sent.append(gate(packed(1, sent), there[0][:1]))
    for i, heads in enumerate(sizes):
        if i + 1 < count:
            there.append(arrive(i + 1, [part[1][0] for part in done[-1:]]))
        if i == 0 and count > 2:
            asks.append(asked(1, there[0][1:]))
        if i + 2 < count:
            behind = there[i + 1][:1] + tuple(asks[1][:1] if i == 0 else [])
            sent.append(gate(packed(i + 2, there[i][:1]), behind))
        if i and i + 2 < count:
            asks.append(asked(i + 1, sent[i + 2 :] + done[i - 1][1][1:]))
        hold = [part[0] for part in there[i + 1 :] + asks[i + 1 :]] + sent[i + 2 :]
        hold += [part[1][0] for part in done[-1:]]
        if i + 1 == count and count > 2:
            early = place(done[:-1], group_width, total_width)
            hold.append(early)
        pieces = asks[i] if i + 1 < count else []
        outs = attend(
            plan, *there[i], keep_mask, pieces, hold, groups, firsts[i], heads, tile_count
        )
        back = [outs[0]] + [turn(outs[shift], groups - shift) for shift in range(1, groups)]
        done.append((firsts[i] * head_size, back))
    return place(done[-2:] if count > 2 else done, group_width, total_width, early)


def solution(mesh):
    return jax.shard_map(
        on_device,
        mesh=mesh,
        in_specs=(
            P(("seq", "head"), None),
            P(("seq", "head"), None),
            P(("seq", "head"), None),
            P("seq"),
            P("seq"),
            P("seq", "head"),
        ),
        out_specs=P(("seq", "head"), None),
        check_vma=False,
    )
```

```python
import functools
import math

import jax
import jax.numpy as jnp
from jax import lax
from jax.experimental import pallas as pl
from jax.experimental.pallas import tpu as pltpu
from jax.sharding import PartitionSpec as P

LANES = 128
CHUNK_HEADS = 3
ANY = pl.BlockSpec(memory_space=pl.ANY)
VMEM_LIMIT = 60 * 2**20


def tile_mask(reach_t, reach_w, slab_index, slab_count):
    tile_count = reach_t.shape[0]
    places = jnp.arange(tile_count, dtype=jnp.int32)
    columns = jnp.arange(3 * tile_count, dtype=jnp.int32)
    offsets = columns // tile_count - 1
    key_place = columns % tile_count
    inside = (slab_index + offsets >= 0) & (slab_index + offsets < slab_count)
    near_time = jnp.abs(offsets)[None, :] <= reach_t[:, None]
    near_width = jnp.abs(key_place[None, :] - places[:, None]) <= reach_w[:, None]
    return near_time & near_width & inside[None, :]


def staged(pairs, stages, sems):
    arriving, leaving = [], []
    for i, (source, target) in enumerate(pairs):
        arriving.append(pltpu.make_async_copy(source, stages[i], sems.at[0, i]))
        leaving.append(pltpu.make_async_copy(stages[i], target, sems.at[1, i]))
    for copy in arriving:
        copy.start()
    for first, second in zip(arriving, leaving):
        first.wait()
        second.start()
    for copy in leaving:
        copy.wait()


def stage_shapes(shapes):
    return [pltpu.VMEM(shape, jnp.bfloat16) for shape in shapes] + [
        pltpu.SemaphoreType.DMA((2, len(shapes)))
    ]


def pack(arrays, after, groups, group_width, start, width):
    rows = arrays[0].shape[0]

    def kernel(*refs):
        sources, out = refs[: len(arrays)], refs[len(arrays) + len(after)]
        stages, sems = refs[len(arrays) + len(after) + 1 : -1], refs[-1]
        pairs = []
        for group in range(groups):
            columns = pl.ds(group * group_width + start, width)
            for i, source in enumerate(sources):
                pairs.append((source.at[:, columns], out.at[group, :, pl.ds(i * width, width)]))
        staged(pairs, stages, sems)

    return pl.pallas_call(
        kernel,
        in_specs=[ANY] * (len(arrays) + len(after)),
        out_specs=ANY,
        out_shape=jax.ShapeDtypeStruct((groups, rows, len(arrays) * width), jnp.bfloat16),
        scratch_shapes=stage_shapes([(rows, width)] * (len(arrays) * groups)),
        cost_estimate=pl.CostEstimate(
            flops=0,
            bytes_accessed=4 * len(arrays) * groups * rows * width,
            transcendentals=0,
        ),
        compiler_params=pltpu.CompilerParams(vmem_limit_bytes=VMEM_LIMIT),
        name="pack",
    )(*arrays, *after)


def pack_turned(array, after, groups, group_width, start, width):
    rows = array.shape[0]

    def kernel(*refs):
        outs = refs[1 + len(after) : 1 + len(after) + groups]
        stages, sems = refs[1 + len(after) + groups : -1], refs[-1]
        me = lax.axis_index("head")
        pairs = []
        for shift in range(groups):
            group = lax.rem(me + shift, groups)
            column = pl.multiple_of(group * group_width + start, LANES)
            pairs.append((refs[0].at[:, pl.ds(column, width)], outs[shift]))
        staged(pairs, stages, sems)

    return pl.pallas_call(
        kernel,
        in_specs=[ANY] * (1 + len(after)),
        out_specs=[ANY] * groups,
        out_shape=[jax.ShapeDtypeStruct((rows, width), jnp.bfloat16)] * groups,
        scratch_shapes=stage_shapes([(rows, width)] * groups),
        cost_estimate=pl.CostEstimate(
            flops=0, bytes_accessed=4 * groups * rows * width, transcendentals=0
        ),
        compiler_params=pltpu.CompilerParams(vmem_limit_bytes=VMEM_LIMIT),
        name="pack_turned",
    )(array, *after)


def gate(array, after):
    def kernel(*refs):
        del refs

    return pl.pallas_call(
        kernel,
        in_specs=[ANY] * (1 + len(after)),
        out_specs=ANY,
        out_shape=jax.ShapeDtypeStruct(array.shape, array.dtype),
        input_output_aliases={0: 0},
        compiler_params=pltpu.CompilerParams(vmem_limit_bytes=VMEM_LIMIT),
        name="gate",
    )(array, *after)


def place(chunks, group_width, total_width, target=None):
    groups = len(chunks[0][1])
    rows = chunks[0][1][0].shape[0]
    blocks = [block for _, parts in chunks for block in parts]
    extra = [] if target is None else [target]

    def kernel(*refs):
        out = refs[len(blocks) + len(extra)]
        stages, sems = refs[len(blocks) + len(extra) + 1 : -1], refs[-1]
        me = lax.axis_index("head")
        pairs = []
        for i, (start, parts) in enumerate(chunks):
            for shift, part in enumerate(parts):
                group = lax.rem(me + shift, groups)
                column = pl.multiple_of(group * group_width + start, LANES)
                pairs.append((refs[i * groups + shift], out.at[:, pl.ds(column, part.shape[1])]))
        staged(pairs, stages, sems)

    return pl.pallas_call(
        kernel,
        in_specs=[ANY] * (len(blocks) + len(extra)),
        out_specs=ANY,
        out_shape=jax.ShapeDtypeStruct((rows, total_width), jnp.bfloat16),
        scratch_shapes=stage_shapes([block.shape for block in blocks]),
        input_output_aliases={len(blocks): 0} if extra else {},
        cost_estimate=pl.CostEstimate(
            flops=0,
            bytes_accessed=4 * rows * sum(block.shape[1] for block in blocks),
            transcendentals=0,
        ),
        compiler_params=pltpu.CompilerParams(vmem_limit_bytes=VMEM_LIMIT),
        name="place",
    )(*blocks, *extra)


def lane_fold(op, wide):
    folded = wide[:, :LANES]
    for start in range(LANES, wide.shape[1], LANES):
        folded = op(folded, wide[:, start : start + LANES])
    return folded


def attend_kernel(groups, heads, first_head, tile_count, in_pieces, *refs):
    plan_ref, own_ref, prev_ref, next_ref, keep_ref = refs[:5]
    pieces = refs[5 : 5 + groups] if in_pieces else ()
    outs = refs[-6 - groups : -6]
    q_ref, out_ref, scores_ref, top_ref, total_ref, sum_ref = refs[-6:]
    slab_rows, width = out_ref.shape
    local_rows = slab_rows // groups
    head_size = width // heads
    tile_rows = slab_rows // tile_count
    scale = math.log2(math.e) / math.sqrt(head_size)
    slabs = ((0, prev_ref), (1, own_ref), (2, next_ref))
    me = lax.axis_index("head")

    def owner_rows(shift):
        owner = lax.rem(me + groups - shift, groups)
        return pl.ds(pl.multiple_of(owner * local_rows, 16), local_rows)

    def tile(index):
        return pl.ds(pl.multiple_of(index * tile_rows, tile_rows), tile_rows)

    def lanes(index):
        return pl.ds(index * head_size, head_size)

    for shift, piece in enumerate(pieces):
        q_ref[owner_rows(shift), :] = piece[...]
    query_ref, first_query = (q_ref, 0) if pieces else (own_ref, 2 * heads)

    def one_tile(i, carry):
        top_ref[...] = jnp.full_like(top_ref, -jnp.inf)
        total_ref[...] = jnp.zeros_like(total_ref)
        sum_ref[...] = jnp.zeros_like(sum_ref)

        for slab, pair_ref in slabs:

            def score(place, carry, slab=slab, pair_ref=pair_ref):
                column = slab * tile_count + place

                @pl.when(plan_ref[i * 3 * tile_count + column] > 0)
                def _():
                    for h in range(heads):
                        found = lax.dot_general(
                            query_ref[tile(i), lanes(first_query + h)],
                            pair_ref[tile(place), lanes(h)],
                            (((1,), (1,)), ((), ())),
                            preferred_element_type=jnp.float32,
                        )
                        scores_ref[h, column] = found
                        top_ref[h] = jnp.maximum(top_ref[h], lane_fold(jnp.maximum, found))

                return carry

            lax.fori_loop(0, tile_count, score, 0)

        for h in range(heads):
            highest = jnp.max(top_ref[h], axis=1, keepdims=True) * scale
            top_ref[h] = jnp.broadcast_to(highest, top_ref.shape[1:])

        for slab, pair_ref in slabs:

            def weigh(place, carry, slab=slab, pair_ref=pair_ref):
                column = slab * tile_count + place

                @pl.when(plan_ref[i * 3 * tile_count + column] > 0)
                def _():
                    for h in range(heads):
                        highest = jnp.concatenate([top_ref[h]] * (tile_rows // LANES), axis=1)
                        weights = jnp.exp2(scores_ref[h, column] * scale - highest)
                        total_ref[h] += lane_fold(jnp.add, weights)
                        sum_ref[h] += jnp.dot(
                            weights.astype(jnp.bfloat16),
                            pair_ref[tile(place), lanes(heads + h)],
                            preferred_element_type=jnp.float32,
                        )

                return carry

            lax.fori_loop(0, tile_count, weigh, 0)

        keep = keep_ref[tile(i), :].astype(jnp.float32)
        numbers = lax.broadcasted_iota(jnp.int32, keep.shape, 1)
        for h in range(heads):
            totals = jnp.sum(total_ref[h], axis=1, keepdims=True)
            mine = jnp.where(numbers == first_head + h, keep, 0.0)
            factor = jnp.sum(mine, axis=1, keepdims=True) * (10.0 / 9.0)
            out_ref[tile(i), lanes(h)] = (sum_ref[h] * (factor / totals)).astype(out_ref.dtype)
        return carry

    lax.fori_loop(0, tile_count, one_tile, 0)

    for shift in range(groups):
        outs[shift][...] = out_ref[owner_rows(shift), :]


def attend(
    plan, own, prev, behind, keep_mask, pieces, after, groups, first_head, heads, tile_count
):
    slab_rows, width = prev.shape[0], prev.shape[1] // 2
    local_rows = slab_rows // groups
    tile_rows = slab_rows // tile_count
    head_size = width // heads
    pairs = heads * slab_rows * 3 * slab_rows
    wholes = [
        pl.BlockSpec(array.shape, lambda s, plan: (0, 0))
        for array in (own, prev, behind, keep_mask, *pieces)
    ]
    accumulator = pltpu.VMEM((heads, tile_rows, LANES), jnp.float32)
    return pl.pallas_call(
        functools.partial(attend_kernel, groups, heads, first_head, tile_count, bool(pieces)),
        grid_spec=pltpu.PrefetchScalarGridSpec(
            num_scalar_prefetch=1,
            grid=(1,),
            in_specs=wholes + [ANY] * len(after),
            out_specs=[pl.BlockSpec((local_rows, width), lambda s, plan: (0, 0))] * groups,
            scratch_shapes=[
                pltpu.VMEM((slab_rows, width), jnp.bfloat16),
                pltpu.VMEM((slab_rows, width), jnp.bfloat16),
                pltpu.VMEM((heads, 3 * tile_count, tile_rows, tile_rows), jnp.float32),
                accumulator,
                accumulator,
                pltpu.VMEM((heads, tile_rows, head_size), jnp.float32),
            ],
        ),
        out_shape=[jax.ShapeDtypeStruct((local_rows, width), jnp.bfloat16)] * groups,
        compiler_params=pltpu.CompilerParams(vmem_limit_bytes=VMEM_LIMIT),
        cost_estimate=pl.CostEstimate(
            flops=16 * pairs * head_size,
            bytes_accessed=16 * slab_rows * width,
            transcendentals=pairs,
        ),
        name="attend",
    )(plan, own, prev, behind, keep_mask, *pieces, *after)


def on_device(queries, key_vectors, value_vectors, reach_time, reach_width, keep_mask):
    groups = lax.axis_size("head")
    slab_count = lax.axis_size("seq")
    total_width = queries.shape[1]
    group_heads = keep_mask.shape[1]
    group_width = total_width // groups
    head_size = group_width // group_heads
    tile_count = reach_time.shape[0]
    allowed = tile_mask(reach_time, reach_width, lax.axis_index("seq"), slab_count)
    plan = allowed.astype(jnp.int32).reshape(-1)
    onward = [(i, i + 1) for i in range(slab_count - 1)]
    backward = [(i + 1, i) for i in range(slab_count - 1)]

    def turn(array, shift):
        return lax.ppermute(array, "head", [(i, (i + shift) % groups) for i in range(groups)])

    parts = -(-(group_heads - 1) // CHUNK_HEADS)
    sizes = [(group_heads - 1 + i) // parts for i in reversed(range(parts))] + [1]
    count = len(sizes)
    firsts = [sum(sizes[:i]) for i in range(count)]

    def packed(i, after):
        arrays = (key_vectors, value_vectors, queries)[: 2 + (i + 1 == count)]
        start, width = firsts[i] * head_size, sizes[i] * head_size
        return pack(arrays, after, groups, group_width, start, width)

    def asked(i, after):
        start, width = firsts[i] * head_size, sizes[i] * head_size
        blocks = pack_turned(queries, after, groups, group_width, start, width)
        return [blocks[0]] + [turn(blocks[shift], shift) for shift in range(1, groups)]

    def arrive(i, after):
        own = lax.all_to_all(sent[i], "head", split_axis=0, concat_axis=0, tiled=True)
        own = gate(own, after) if after else own
        own = own.reshape(-1, own.shape[2])
        pairs = own[:, : 2 * sizes[i] * head_size]
        return own, lax.ppermute(pairs, "seq", onward), lax.ppermute(pairs, "seq", backward)

    sent, there, asks, done, early = [packed(0, [])], [], [], [], None
    there.append(arrive(0, []))
    if count > 1:
        asks.append(asked(0, sent))
        sent.append(gate(packed(1, sent), there[0][:1]))
    if count > 2:
        asks.append(asked(1, there[0][:1]))
    for i, heads in enumerate(sizes):
        if i + 1 < count:
            there.append(arrive(i + 1, [part[1][0] for part in done[-1:]]))
        if i + 2 < count:
            sent.append(gate(packed(i + 2, there[i][:1]), there[i + 1][:1]))
            if i:
                asks.append(asked(i + 1, done[i - 1][1][1:] + sent[i + 2 :]))
        hold = [part[0] for part in there[i + 1 :]] + sent[i + 2 :]
        hold += [part[1][0] for part in done[-1:]]
        hold += [block for part in done[-2:-1] for block in part[1][1:]]
        if i == 0:
            hold += [part[0] for part in asks[1:]]
        if i + 1 == count and count > 2:
            early = place(done[:-1], group_width, total_width)
            hold.append(early)
        pieces = asks[i] if i + 1 < count else []
        outs = attend(
            plan, *there[i], keep_mask, pieces, hold, groups, firsts[i], heads, tile_count
        )
        back = [outs[0]] + [turn(outs[shift], groups - shift) for shift in range(1, groups)]
        done.append((firsts[i] * head_size, back))
    return place(done[-2:] if count > 2 else done, group_width, total_width, early)


def solution(mesh):
    return jax.shard_map(
        on_device,
        mesh=mesh,
        in_specs=(
            P(("seq", "head"), None),
            P(("seq", "head"), None),
            P(("seq", "head"), None),
            P("seq"),
            P("seq"),
            P("seq", "head"),
        ),
        out_specs=P(("seq", "head"), None),
        check_vma=False,
    )
```

```python
import functools
import math

import jax
import jax.numpy as jnp
from jax import lax
from jax.experimental import pallas as pl
from jax.experimental.pallas import tpu as pltpu
from jax.sharding import PartitionSpec as P

LANES = 128
CHUNK_HEADS = 3
ANY = pl.BlockSpec(memory_space=pl.ANY)
VMEM_LIMIT = 60 * 2**20


def reach_plan(reach_t, reach_w, slab_index, slab_count):
    tile_count = reach_t.shape[0]
    places = jnp.arange(tile_count, dtype=jnp.int32)
    before = jnp.minimum(jnp.minimum(reach_t, 1), slab_index)
    behind = jnp.minimum(jnp.minimum(reach_t, 1), slab_count - 1 - slab_index)
    low = jnp.maximum(places - reach_w, 0)
    high = jnp.minimum(places + reach_w, tile_count - 1)
    return jnp.stack([1 - before, before + 1 + behind, low, high - low + 1], axis=1).reshape(-1)


def staged(pairs, stages, sems):
    arriving, leaving = [], []
    for i, (source, target) in enumerate(pairs):
        arriving.append(pltpu.make_async_copy(source, stages[i], sems.at[0, i]))
        leaving.append(pltpu.make_async_copy(stages[i], target, sems.at[1, i]))
    for copy in arriving:
        copy.start()
    for first, second in zip(arriving, leaving):
        first.wait()
        second.start()
    for copy in leaving:
        copy.wait()


def stage_shapes(shapes):
    return [pltpu.VMEM(shape, jnp.bfloat16) for shape in shapes] + [
        pltpu.SemaphoreType.DMA((2, len(shapes)))
    ]


def pack(arrays, after, groups, group_width, start, width):
    rows = arrays[0].shape[0]

    def kernel(*refs):
        sources, out = refs[: len(arrays)], refs[len(arrays) + len(after)]
        stages, sems = refs[len(arrays) + len(after) + 1 : -1], refs[-1]
        pairs = []
        for group in range(groups):
            columns = pl.ds(group * group_width + start, width)
            for i, source in enumerate(sources):
                pairs.append((source.at[:, columns], out.at[group, :, pl.ds(i * width, width)]))
        staged(pairs, stages, sems)

    return pl.pallas_call(
        kernel,
        in_specs=[ANY] * (len(arrays) + len(after)),
        out_specs=ANY,
        out_shape=jax.ShapeDtypeStruct((groups, rows, len(arrays) * width), jnp.bfloat16),
        scratch_shapes=stage_shapes([(rows, width)] * (len(arrays) * groups)),
        cost_estimate=pl.CostEstimate(
            flops=0,
            bytes_accessed=4 * len(arrays) * groups * rows * width,
            transcendentals=0,
        ),
        compiler_params=pltpu.CompilerParams(vmem_limit_bytes=VMEM_LIMIT),
        name="pack",
    )(*arrays, *after)


def pack_turned(array, after, groups, group_width, start, width):
    rows = array.shape[0]

    def kernel(*refs):
        outs = refs[1 + len(after) : 1 + len(after) + groups]
        stages, sems = refs[1 + len(after) + groups : -1], refs[-1]
        me = lax.axis_index("head")
        pairs = []
        for shift in range(groups):
            group = lax.rem(me + shift, groups)
            column = pl.multiple_of(group * group_width + start, LANES)
            pairs.append((refs[0].at[:, pl.ds(column, width)], outs[shift]))
        staged(pairs, stages, sems)

    return pl.pallas_call(
        kernel,
        in_specs=[ANY] * (1 + len(after)),
        out_specs=[ANY] * groups,
        out_shape=[jax.ShapeDtypeStruct((rows, width), jnp.bfloat16)] * groups,
        scratch_shapes=stage_shapes([(rows, width)] * groups),
        cost_estimate=pl.CostEstimate(
            flops=0, bytes_accessed=4 * groups * rows * width, transcendentals=0
        ),
        compiler_params=pltpu.CompilerParams(vmem_limit_bytes=VMEM_LIMIT),
        name="pack_turned",
    )(array, *after)


def gate(array, after):
    def kernel(*refs):
        del refs

    return pl.pallas_call(
        kernel,
        in_specs=[ANY] * (1 + len(after)),
        out_specs=ANY,
        out_shape=jax.ShapeDtypeStruct(array.shape, array.dtype),
        input_output_aliases={0: 0},
        compiler_params=pltpu.CompilerParams(vmem_limit_bytes=VMEM_LIMIT),
        name="gate",
    )(array, *after)


def place(chunks, group_width, total_width, target=None):
    groups = len(chunks[0][1])
    rows = chunks[0][1][0].shape[0]
    blocks = [block for _, parts in chunks for block in parts]
    extra = [] if target is None else [target]

    def kernel(*refs):
        out = refs[len(blocks) + len(extra)]
        stages, sems = refs[len(blocks) + len(extra) + 1 : -1], refs[-1]
        me = lax.axis_index("head")
        pairs = []
        for i, (start, parts) in enumerate(chunks):
            for shift, part in enumerate(parts):
                group = lax.rem(me + shift, groups)
                column = pl.multiple_of(group * group_width + start, LANES)
                pairs.append((refs[i * groups + shift], out.at[:, pl.ds(column, part.shape[1])]))
        staged(pairs, stages, sems)

    return pl.pallas_call(
        kernel,
        in_specs=[ANY] * (len(blocks) + len(extra)),
        out_specs=ANY,
        out_shape=jax.ShapeDtypeStruct((rows, total_width), jnp.bfloat16),
        scratch_shapes=stage_shapes([block.shape for block in blocks]),
        input_output_aliases={len(blocks): 0} if extra else {},
        cost_estimate=pl.CostEstimate(
            flops=0,
            bytes_accessed=4 * rows * sum(block.shape[1] for block in blocks),
            transcendentals=0,
        ),
        compiler_params=pltpu.CompilerParams(vmem_limit_bytes=VMEM_LIMIT),
        name="place",
    )(*blocks, *extra)


def lane_fold(op, wide):
    folded = wide[:, :LANES]
    for start in range(LANES, wide.shape[1], LANES):
        folded = op(folded, wide[:, start : start + LANES])
    return folded


def attend_kernel(groups, heads, first_head, tile_count, in_pieces, *refs):
    plan_ref, own_ref, prev_ref, next_ref, keep_ref = refs[:5]
    pieces = refs[5 : 5 + groups] if in_pieces else ()
    outs = refs[-8 - groups : -8]
    pair_ref, q_ref, out_ref, scores_ref, top_ref, total_ref, sum_ref, sems = refs[-8:]
    slab_rows, width = out_ref.shape
    local_rows = slab_rows // groups
    head_size = width // heads
    tile_rows = slab_rows // tile_count
    scale = math.log2(math.e) / math.sqrt(head_size)
    me = lax.axis_index("head")

    def owner_rows(shift):
        owner = lax.rem(me + groups - shift, groups)
        return pl.ds(pl.multiple_of(owner * local_rows, 16), local_rows)

    def lanes(index):
        return pl.ds(index * head_size, head_size)

    loads = [
        (prev_ref, pair_ref.at[0]),
        (own_ref.at[:, pl.ds(0, 2 * width)], pair_ref.at[1]),
        (next_ref, pair_ref.at[2]),
    ]
    loads += [(piece, q_ref.at[owner_rows(i), :]) for i, piece in enumerate(pieces)]
    if not pieces:
        loads.append((own_ref.at[:, pl.ds(2 * width, width)], q_ref))
    copies = [
        pltpu.make_async_copy(source, target, sems.at[i])
        for i, (source, target) in enumerate(loads)
    ]
    for copy in copies:
        copy.start()
    for copy in copies:
        copy.wait()

    def one_tile(i, carry):
        first_slab, slabs = plan_ref[4 * i], plan_ref[4 * i + 1]
        first_place, places = plan_ref[4 * i + 2], plan_ref[4 * i + 3]
        mine = pl.ds(pl.multiple_of(i * tile_rows, tile_rows), tile_rows)
        start = pl.multiple_of(first_place * tile_rows, tile_rows)
        top_ref[...] = jnp.full_like(top_ref, -jnp.inf)
        total_ref[...] = jnp.zeros_like(total_ref)
        sum_ref[...] = jnp.zeros_like(sum_ref)

        for count in range(1, tile_count + 1):
            rows = count * tile_rows

            def score(slab, carry, rows=rows):
                for h in range(heads):
                    found = lax.dot_general(
                        q_ref[mine, lanes(h)],
                        pair_ref[slab, pl.ds(start, rows), lanes(h)],
                        (((1,), (1,)), ((), ())),
                        preferred_element_type=jnp.float32,
                    )
                    scores_ref[h, slab, :, pl.ds(0, rows)] = found
                    top_ref[h] = jnp.maximum(top_ref[h], lane_fold(jnp.maximum, found))
                return carry

            @pl.when(places == count)
            def _(score=score):
                lax.fori_loop(first_slab, first_slab + slabs, score, 0)

        for h in range(heads):
            highest = jnp.max(top_ref[h], axis=1, keepdims=True) * scale
            top_ref[h] = jnp.broadcast_to(highest, top_ref.shape[1:])

        for count in range(1, tile_count + 1):
            rows = count * tile_rows

            def weigh(slab, carry, rows=rows):
                for h in range(heads):
                    highest = jnp.concatenate([top_ref[h]] * (rows // LANES), axis=1)
                    weights = jnp.exp2(scores_ref[h, slab, :, pl.ds(0, rows)] * scale - highest)
                    total_ref[h] += lane_fold(jnp.add, weights)
                    sum_ref[h] += jnp.dot(
                        weights.astype(jnp.bfloat16),
                        pair_ref[slab, pl.ds(start, rows), lanes(heads + h)],
                        preferred_element_type=jnp.float32,
                    )
                return carry

            @pl.when(places == count)
            def _(weigh=weigh):
                lax.fori_loop(first_slab, first_slab + slabs, weigh, 0)

        keep = keep_ref[mine, :].astype(jnp.float32)
        numbers = lax.broadcasted_iota(jnp.int32, keep.shape, 1)
        for h in range(heads):
            totals = jnp.sum(total_ref[h], axis=1, keepdims=True)
            kept = jnp.where(numbers == first_head + h, keep, 0.0)
            factor = jnp.sum(kept, axis=1, keepdims=True) * (10.0 / 9.0)
            out_ref[mine, lanes(h)] = (sum_ref[h] * (factor / totals)).astype(out_ref.dtype)
        return carry

    lax.fori_loop(0, tile_count, one_tile, 0)

    for shift in range(groups):
        outs[shift][...] = out_ref[owner_rows(shift), :]


def attend(
    plan, own, prev, behind, keep_mask, pieces, after, groups, first_head, heads, tile_count
):
    slab_rows, width = prev.shape[0], prev.shape[1] // 2
    local_rows = slab_rows // groups
    tile_rows = slab_rows // tile_count
    head_size = width // heads
    pairs = heads * slab_rows * 3 * slab_rows
    accumulator = pltpu.VMEM((heads, tile_rows, LANES), jnp.float32)
    return pl.pallas_call(
        functools.partial(attend_kernel, groups, heads, first_head, tile_count, bool(pieces)),
        grid_spec=pltpu.PrefetchScalarGridSpec(
            num_scalar_prefetch=1,
            grid=(1,),
            in_specs=[ANY] * 3
            + [pl.BlockSpec(keep_mask.shape, lambda s, plan: (0, 0))]
            + [ANY] * (len(pieces) + len(after)),
            out_specs=[pl.BlockSpec((local_rows, width), lambda s, plan: (0, 0))] * groups,
            scratch_shapes=[
                pltpu.VMEM((3, slab_rows, 2 * width), jnp.bfloat16),
                pltpu.VMEM((slab_rows, width), jnp.bfloat16),
                pltpu.VMEM((slab_rows, width), jnp.bfloat16),
                pltpu.VMEM((heads, 3, tile_rows, slab_rows), jnp.float32),
                accumulator,
                accumulator,
                pltpu.VMEM((heads, tile_rows, head_size), jnp.float32),
                pltpu.SemaphoreType.DMA((3 + max(len(pieces), 1),)),
            ],
        ),
        out_shape=[jax.ShapeDtypeStruct((local_rows, width), jnp.bfloat16)] * groups,
        compiler_params=pltpu.CompilerParams(vmem_limit_bytes=VMEM_LIMIT),
        cost_estimate=pl.CostEstimate(
            flops=12 * pairs * head_size,
            bytes_accessed=16 * slab_rows * width,
            transcendentals=pairs,
        ),
        name="attend",
    )(plan, own, prev, behind, keep_mask, *pieces, *after)


def on_device(queries, key_vectors, value_vectors, reach_time, reach_width, keep_mask):
    groups = lax.axis_size("head")
    slab_count = lax.axis_size("seq")
    total_width = queries.shape[1]
    group_heads = keep_mask.shape[1]
    group_width = total_width // groups
    head_size = group_width // group_heads
    tile_count = reach_time.shape[0]
    plan = reach_plan(reach_time, reach_width, lax.axis_index("seq"), slab_count)
    onward = [(i, i + 1) for i in range(slab_count - 1)]
    backward = [(i + 1, i) for i in range(slab_count - 1)]

    def turn(array, shift):
        return lax.ppermute(array, "head", [(i, (i + shift) % groups) for i in range(groups)])

    parts = -(-(group_heads - 1) // CHUNK_HEADS)
    sizes = [(group_heads - 1 + i) // parts for i in reversed(range(parts))] + [1]
    count = len(sizes)
    firsts = [sum(sizes[:i]) for i in range(count)]
    with_permutes = min(2, count - 1)

    def packed(i, after):
        arrays = (key_vectors, value_vectors, queries)[: 3 - (i < with_permutes)]
        start, width = firsts[i] * head_size, sizes[i] * head_size
        return pack(arrays, after, groups, group_width, start, width)

    def asked(i, after):
        start, width = firsts[i] * head_size, sizes[i] * head_size
        blocks = pack_turned(queries, after, groups, group_width, start, width)
        return [blocks[0]] + [turn(blocks[shift], shift) for shift in range(1, groups)]

    def arrive(i, after):
        own = lax.all_to_all(sent[i], "head", split_axis=0, concat_axis=0, tiled=True)
        own = gate(own, after) if after else own
        own = own.reshape(-1, own.shape[2])
        pairs = own[:, : 2 * sizes[i] * head_size]
        return own, lax.ppermute(pairs, "seq", onward), lax.ppermute(pairs, "seq", backward)

    sent, there, asks, done, early = [packed(0, [])], [], [], [], None
    there.append(arrive(0, []))
    if count > 1:
        sent.append(gate(packed(1, sent), there[0][:1]))
    for i in range(with_permutes):
        asks.append(asked(i, there[i - 1][:1] if i else sent[:1]))
    for i, heads in enumerate(sizes):
        if i + 1 < count:
            there.append(arrive(i + 1, [part[1][0] for part in done[-1:]]))
        if i + 2 < count:
            sent.append(gate(packed(i + 2, there[i][:1]), there[i + 1][:1]))
        hold = [part[0] for part in there[i + 1 :]] + sent[i + 2 :]
        hold += [part[1][0] for part in done[-1:]]
        hold += [block for part in done[-2:-1] for block in part[1][1:]]
        hold += [part[0] for part in asks[i + 1 :]]
        if i + 1 == count and count > 2:
            early = place(done[:-1], group_width, total_width)
            hold.append(early)
        pieces = asks[i] if i < with_permutes else []
        outs = attend(
            plan, *there[i], keep_mask, pieces, hold, groups, firsts[i], heads, tile_count
        )
        back = [outs[0]] + [turn(outs[shift], groups - shift) for shift in range(1, groups)]
        done.append((firsts[i] * head_size, back))
    return place(done[-2:] if count > 2 else done, group_width, total_width, early)


def solution(mesh):
    return jax.shard_map(
        on_device,
        mesh=mesh,
        in_specs=(
            P(("seq", "head"), None),
            P(("seq", "head"), None),
            P(("seq", "head"), None),
            P("seq"),
            P("seq"),
            P("seq", "head"),
        ),
        out_specs=P(("seq", "head"), None),
        check_vma=False,
    )
```

```python
import functools
import math

import jax
import jax.numpy as jnp
from jax import lax
from jax.experimental import pallas as pl
from jax.experimental.pallas import tpu as pltpu
from jax.sharding import PartitionSpec as P

LANES = 128
CHUNK_HEADS = 3
ANY = pl.BlockSpec(memory_space=pl.ANY)
VMEM_LIMIT = 60 * 2**20


def reach_plan(reach_t, reach_w, slab_index, slab_count):
    tile_count = reach_t.shape[0]
    places = jnp.arange(tile_count, dtype=jnp.int32)
    before = jnp.minimum(jnp.minimum(reach_t, 1), slab_index)
    behind = jnp.minimum(jnp.minimum(reach_t, 1), slab_count - 1 - slab_index)
    low = jnp.maximum(places - reach_w, 0)
    high = jnp.minimum(places + reach_w, tile_count - 1)
    return jnp.stack([1 - before, before + 1 + behind, low, high - low + 1], axis=1).reshape(-1)


def staged(pairs, stages, sems):
    arriving, leaving = [], []
    for i, (source, target) in enumerate(pairs):
        arriving.append(pltpu.make_async_copy(source, stages[i], sems.at[0, i]))
        leaving.append(pltpu.make_async_copy(stages[i], target, sems.at[1, i]))
    for copy in arriving:
        copy.start()
    for first, second in zip(arriving, leaving):
        first.wait()
        second.start()
    for copy in leaving:
        copy.wait()


def stage_shapes(shapes):
    return [pltpu.VMEM(shape, jnp.bfloat16) for shape in shapes] + [
        pltpu.SemaphoreType.DMA((2, len(shapes)))
    ]


def pack(parts, after, groups, group_width):
    rows = parts[0][0].shape[0]
    arrays = [array for array, _, _ in parts]
    total = sum(width for _, _, width in parts)

    def kernel(*refs):
        out = refs[len(parts) + len(after)]
        stages, sems = refs[len(parts) + len(after) + 1 : -1], refs[-1]
        pairs = []
        for group in range(groups):
            filled = 0
            for source, (_, start, width) in zip(refs, parts):
                columns = pl.ds(group * group_width + start, width)
                pairs.append((source.at[:, columns], out.at[group, :, pl.ds(filled, width)]))
                filled += width
        staged(pairs, stages, sems)

    return pl.pallas_call(
        kernel,
        in_specs=[ANY] * (len(parts) + len(after)),
        out_specs=ANY,
        out_shape=jax.ShapeDtypeStruct((groups, rows, total), jnp.bfloat16),
        scratch_shapes=stage_shapes([(rows, width) for _, _, width in parts] * groups),
        cost_estimate=pl.CostEstimate(
            flops=0, bytes_accessed=4 * groups * rows * total, transcendentals=0
        ),
        compiler_params=pltpu.CompilerParams(vmem_limit_bytes=VMEM_LIMIT),
        name="pack",
    )(*arrays, *after)


def pack_turned(array, after, groups, group_width, start, width):
    rows = array.shape[0]

    def kernel(*refs):
        outs = refs[1 + len(after) : 1 + len(after) + groups]
        stages, sems = refs[1 + len(after) + groups : -1], refs[-1]
        me = lax.axis_index("head")
        pairs = []
        for shift in range(groups):
            group = lax.rem(me + shift, groups)
            column = pl.multiple_of(group * group_width + start, LANES)
            pairs.append((refs[0].at[:, pl.ds(column, width)], outs[shift]))
        staged(pairs, stages, sems)

    return pl.pallas_call(
        kernel,
        in_specs=[ANY] * (1 + len(after)),
        out_specs=[ANY] * groups,
        out_shape=[jax.ShapeDtypeStruct((rows, width), jnp.bfloat16)] * groups,
        scratch_shapes=stage_shapes([(rows, width)] * groups),
        cost_estimate=pl.CostEstimate(
            flops=0, bytes_accessed=4 * groups * rows * width, transcendentals=0
        ),
        compiler_params=pltpu.CompilerParams(vmem_limit_bytes=VMEM_LIMIT),
        name="pack_turned",
    )(array, *after)


def gate(array, after):
    def kernel(*refs):
        del refs

    return pl.pallas_call(
        kernel,
        in_specs=[ANY] * (1 + len(after)),
        out_specs=ANY,
        out_shape=jax.ShapeDtypeStruct(array.shape, array.dtype),
        input_output_aliases={0: 0},
        compiler_params=pltpu.CompilerParams(vmem_limit_bytes=VMEM_LIMIT),
        name="gate",
    )(array, *after)


def place(chunks, group_width, total_width, target=None):
    groups = len(chunks[0][1])
    rows = chunks[0][1][0].shape[0]
    blocks = [block for _, parts in chunks for block in parts]
    extra = [] if target is None else [target]

    def kernel(*refs):
        out = refs[len(blocks) + len(extra)]
        stages, sems = refs[len(blocks) + len(extra) + 1 : -1], refs[-1]
        me = lax.axis_index("head")
        pairs = []
        for i, (start, parts) in enumerate(chunks):
            for shift, part in enumerate(parts):
                group = lax.rem(me + shift, groups)
                column = pl.multiple_of(group * group_width + start, LANES)
                pairs.append((refs[i * groups + shift], out.at[:, pl.ds(column, part.shape[1])]))
        staged(pairs, stages, sems)

    return pl.pallas_call(
        kernel,
        in_specs=[ANY] * (len(blocks) + len(extra)),
        out_specs=ANY,
        out_shape=jax.ShapeDtypeStruct((rows, total_width), jnp.bfloat16),
        scratch_shapes=stage_shapes([block.shape for block in blocks]),
        input_output_aliases={len(blocks): 0} if extra else {},
        cost_estimate=pl.CostEstimate(
            flops=0,
            bytes_accessed=4 * rows * sum(block.shape[1] for block in blocks),
            transcendentals=0,
        ),
        compiler_params=pltpu.CompilerParams(vmem_limit_bytes=VMEM_LIMIT),
        name="place",
    )(*blocks, *extra)


def lane_fold(op, wide):
    folded = wide[:, :LANES]
    for start in range(LANES, wide.shape[1], LANES):
        folded = op(folded, wide[:, start : start + LANES])
    return folded


def attend_kernel(groups, heads, first_head, tile_count, query_lane, *refs):
    plan_ref, own_ref, prev_ref, next_ref, keep_ref = refs[:5]
    asked = refs[5 : 5 + groups] if query_lane is None else refs[5:6]
    outs = refs[-8 - groups : -8]
    pair_ref, q_ref, out_ref, scores_ref, top_ref, total_ref, sum_ref, sems = refs[-8:]
    slab_rows, width = out_ref.shape
    local_rows = slab_rows // groups
    head_size = width // heads
    tile_rows = slab_rows // tile_count
    scale = math.log2(math.e) / math.sqrt(head_size)
    me = lax.axis_index("head")

    def owner_rows(shift):
        owner = lax.rem(me + groups - shift, groups)
        return pl.ds(pl.multiple_of(owner * local_rows, 16), local_rows)

    def lanes(index):
        return pl.ds(index * head_size, head_size)

    loads = [
        (prev_ref, pair_ref.at[0]),
        (own_ref.at[:, pl.ds(0, 2 * width)], pair_ref.at[1]),
        (next_ref, pair_ref.at[2]),
    ]
    if query_lane is None:
        loads += [(piece, q_ref.at[owner_rows(i), :]) for i, piece in enumerate(asked)]
    else:
        loads.append((asked[0].at[:, pl.ds(query_lane, width)], q_ref))
    copies = [
        pltpu.make_async_copy(source, target, sems.at[i])
        for i, (source, target) in enumerate(loads)
    ]
    for copy in copies:
        copy.start()
    for copy in copies:
        copy.wait()

    def one_tile(i, carry):
        first_slab, slabs = plan_ref[4 * i], plan_ref[4 * i + 1]
        first_place, places = plan_ref[4 * i + 2], plan_ref[4 * i + 3]
        mine = pl.ds(pl.multiple_of(i * tile_rows, tile_rows), tile_rows)
        start = pl.multiple_of(first_place * tile_rows, tile_rows)
        top_ref[...] = jnp.full_like(top_ref, -jnp.inf)
        total_ref[...] = jnp.zeros_like(total_ref)
        sum_ref[...] = jnp.zeros_like(sum_ref)

        for count in range(1, tile_count + 1):
            rows = count * tile_rows

            def score(slab, carry, rows=rows):
                for h in range(heads):
                    found = lax.dot_general(
                        q_ref[mine, lanes(h)],
                        pair_ref[slab, pl.ds(start, rows), lanes(h)],
                        (((1,), (1,)), ((), ())),
                        preferred_element_type=jnp.float32,
                    )
                    scores_ref[h, slab, :, pl.ds(0, rows)] = found
                    top_ref[h] = jnp.maximum(top_ref[h], lane_fold(jnp.maximum, found))
                return carry

            @pl.when(places == count)
            def _(score=score):
                lax.fori_loop(first_slab, first_slab + slabs, score, 0)

        for h in range(heads):
            highest = jnp.max(top_ref[h], axis=1, keepdims=True) * scale
            top_ref[h] = jnp.broadcast_to(highest, top_ref.shape[1:])

        for count in range(1, tile_count + 1):
            rows = count * tile_rows

            def weigh(slab, carry, rows=rows):
                for h in range(heads):
                    highest = jnp.concatenate([top_ref[h]] * (rows // LANES), axis=1)
                    weights = jnp.exp2(scores_ref[h, slab, :, pl.ds(0, rows)] * scale - highest)
                    total_ref[h] += lane_fold(jnp.add, weights)
                    sum_ref[h] += jnp.dot(
                        weights.astype(jnp.bfloat16),
                        pair_ref[slab, pl.ds(start, rows), lanes(heads + h)],
                        preferred_element_type=jnp.float32,
                    )
                return carry

            @pl.when(places == count)
            def _(weigh=weigh):
                lax.fori_loop(first_slab, first_slab + slabs, weigh, 0)

        keep = keep_ref[mine, :].astype(jnp.float32)
        numbers = lax.broadcasted_iota(jnp.int32, keep.shape, 1)
        for h in range(heads):
            totals = jnp.sum(total_ref[h], axis=1, keepdims=True)
            kept = jnp.where(numbers == first_head + h, keep, 0.0)
            factor = jnp.sum(kept, axis=1, keepdims=True) * (10.0 / 9.0)
            out_ref[mine, lanes(h)] = (sum_ref[h] * (factor / totals)).astype(out_ref.dtype)
        return carry

    lax.fori_loop(0, tile_count, one_tile, 0)

    for shift in range(groups):
        outs[shift][...] = out_ref[owner_rows(shift), :]


def attend(
    plan, own, prev, behind, keep_mask, asked, lane, after, groups, first_head, heads, tile_count
):
    slab_rows, width = prev.shape[0], prev.shape[1] // 2
    local_rows = slab_rows // groups
    tile_rows = slab_rows // tile_count
    head_size = width // heads
    pairs = heads * slab_rows * 3 * slab_rows
    accumulator = pltpu.VMEM((heads, tile_rows, LANES), jnp.float32)
    return pl.pallas_call(
        functools.partial(attend_kernel, groups, heads, first_head, tile_count, lane),
        grid_spec=pltpu.PrefetchScalarGridSpec(
            num_scalar_prefetch=1,
            grid=(1,),
            in_specs=[ANY] * 3
            + [pl.BlockSpec(keep_mask.shape, lambda s, plan: (0, 0))]
            + [ANY] * (len(asked) + len(after)),
            out_specs=[pl.BlockSpec((local_rows, width), lambda s, plan: (0, 0))] * groups,
            scratch_shapes=[
                pltpu.VMEM((3, slab_rows, 2 * width), jnp.bfloat16),
                pltpu.VMEM((slab_rows, width), jnp.bfloat16),
                pltpu.VMEM((slab_rows, width), jnp.bfloat16),
                pltpu.VMEM((heads, 3, tile_rows, slab_rows), jnp.float32),
                accumulator,
                accumulator,
                pltpu.VMEM((heads, tile_rows, head_size), jnp.float32),
                pltpu.SemaphoreType.DMA((3 + len(asked),)),
            ],
        ),
        out_shape=[jax.ShapeDtypeStruct((local_rows, width), jnp.bfloat16)] * groups,
        compiler_params=pltpu.CompilerParams(vmem_limit_bytes=VMEM_LIMIT),
        cost_estimate=pl.CostEstimate(
            flops=12 * pairs * head_size,
            bytes_accessed=16 * slab_rows * width,
            transcendentals=pairs,
        ),
        name="attend",
    )(plan, own, prev, behind, keep_mask, *asked, *after)


def on_device(queries, key_vectors, value_vectors, reach_time, reach_width, keep_mask):
    groups = lax.axis_size("head")
    slab_count = lax.axis_size("seq")
    total_width = queries.shape[1]
    group_heads = keep_mask.shape[1]
    group_width = total_width // groups
    head_size = group_width // group_heads
    tile_count = reach_time.shape[0]
    plan = reach_plan(reach_time, reach_width, lax.axis_index("seq"), slab_count)
    onward = [(i, i + 1) for i in range(slab_count - 1)]
    backward = [(i + 1, i) for i in range(slab_count - 1)]

    def turn(array, shift):
        return lax.ppermute(array, "head", [(i, (i + shift) % groups) for i in range(groups)])

    parts = -(-(group_heads - 1) // CHUNK_HEADS)
    sizes = [(group_heads - 1 + i) // parts for i in reversed(range(parts))] + [1]
    count = len(sizes)
    firsts = [sum(sizes[:i]) for i in range(count)]
    by_permutes = max(count - 2, 0)

    def columns(i):
        return firsts[i] * head_size, sizes[i] * head_size

    def packed(i, after):
        parts = [(key_vectors, *columns(i)), (value_vectors, *columns(i))]
        if i + 1 == count:
            parts += [(queries, *columns(j)) for j in reversed(range(by_permutes, count))]
        return pack(parts, after, groups, group_width)

    def asked(i, after):
        blocks = pack_turned(queries, after, groups, group_width, *columns(i))
        return [blocks[0]] + [turn(blocks[shift], shift) for shift in range(1, groups)]

    def arrive(i, after):
        own = lax.all_to_all(sent[i], "head", split_axis=0, concat_axis=0, tiled=True)
        own = gate(own, after) if after else own
        own = own.reshape(-1, own.shape[2])
        pairs = own[:, : 2 * sizes[i] * head_size]
        return own, lax.ppermute(pairs, "seq", onward), lax.ppermute(pairs, "seq", backward)

    sent, there, asks, done, early = [packed(0, [])], [], [], [], None
    there.append(arrive(0, []))
    if count > 1:
        sent.append(gate(packed(1, sent), there[0][:1]))
    for i in range(by_permutes):
        asks.append(asked(i, there[i - 1][:1] if i else sent[:1]))
    for i, heads in enumerate(sizes):
        if i + 1 < count:
            there.append(arrive(i + 1, [part[1][0] for part in done[-1:]]))
        if i + 2 < count:
            landed = [*there[i + 1][:1], *there[i][1:], *asks[i][1:]]
            sent.append(gate(packed(i + 2, there[i][:1]), landed))
        hold = [part[0] for part in there[i + 1 :]] + sent[i + 2 :]
        hold += [part[1][0] for part in done[-1:]]
        hold += [block for part in done[-2:-1] for block in part[1][1:]]
        hold += [part[0] for part in asks[i + 1 :]]
        if i + 1 == count and count > 2:
            early = place(done[:-1], group_width, total_width)
            hold.append(early)
        if i < by_permutes:
            source, lane = asks[i], None
        else:
            source, lane = there[-1][:1], 2 * columns(count - 1)[1]
            lane += sum(columns(j)[1] for j in range(i + 1, count))
        outs = attend(
            plan, *there[i], keep_mask, source, lane, hold, groups, firsts[i], heads, tile_count
        )
        back = [outs[0]] + [turn(outs[shift], groups - shift) for shift in range(1, groups)]
        done.append((firsts[i] * head_size, back))
    return place(done[-2:] if count > 2 else done, group_width, total_width, early)


def solution(mesh):
    return jax.shard_map(
        on_device,
        mesh=mesh,
        in_specs=(
            P(("seq", "head"), None),
            P(("seq", "head"), None),
            P(("seq", "head"), None),
            P("seq"),
            P("seq"),
            P("seq", "head"),
        ),
        out_specs=P(("seq", "head"), None),
        check_vma=False,
    )
```

```python
import functools
import math

import jax
import jax.numpy as jnp
from jax import lax
from jax.experimental import pallas as pl
from jax.experimental.pallas import tpu as pltpu
from jax.sharding import PartitionSpec as P

LANES = 128
CHUNK_HEADS = 3
ANY = pl.BlockSpec(memory_space=pl.ANY)
VMEM_LIMIT = 60 * 2**20


def reach_plan(reach_t, reach_w, slab_index, slab_count):
    tile_count = reach_t.shape[0]
    places = jnp.arange(tile_count, dtype=jnp.int32)
    before = jnp.minimum(jnp.minimum(reach_t, 1), slab_index)
    behind = jnp.minimum(jnp.minimum(reach_t, 1), slab_count - 1 - slab_index)
    low = jnp.maximum(places - reach_w, 0)
    high = jnp.minimum(places + reach_w, tile_count - 1)
    return jnp.stack([1 - before, before + 1 + behind, low, high - low + 1], axis=1).reshape(-1)


def staged(pairs, stages, sems):
    arriving, leaving = [], []
    for i, (source, target) in enumerate(pairs):
        arriving.append(pltpu.make_async_copy(source, stages[i], sems.at[0, i]))
        leaving.append(pltpu.make_async_copy(stages[i], target, sems.at[1, i]))
    for copy in arriving:
        copy.start()
    for first, second in zip(arriving, leaving):
        first.wait()
        second.start()
    for copy in leaving:
        copy.wait()


def stage_shapes(shapes):
    return [pltpu.VMEM(shape, jnp.bfloat16) for shape in shapes] + [
        pltpu.SemaphoreType.DMA((2, len(shapes)))
    ]


def pack(parts, after, groups, group_width):
    rows = parts[0][0].shape[0]
    arrays = [array for array, _, _ in parts]
    total = sum(width for _, _, width in parts)

    def kernel(*refs):
        out = refs[len(parts) + len(after)]
        stages, sems = refs[len(parts) + len(after) + 1 : -1], refs[-1]
        pairs = []
        for group in range(groups):
            filled = 0
            for source, (_, start, width) in zip(refs, parts):
                columns = pl.ds(group * group_width + start, width)
                pairs.append((source.at[:, columns], out.at[group, :, pl.ds(filled, width)]))
                filled += width
        staged(pairs, stages, sems)

    return pl.pallas_call(
        kernel,
        in_specs=[ANY] * (len(parts) + len(after)),
        out_specs=ANY,
        out_shape=jax.ShapeDtypeStruct((groups, rows, total), jnp.bfloat16),
        scratch_shapes=stage_shapes([(rows, width) for _, _, width in parts] * groups),
        cost_estimate=pl.CostEstimate(
            flops=0, bytes_accessed=4 * groups * rows * total, transcendentals=0
        ),
        compiler_params=pltpu.CompilerParams(vmem_limit_bytes=VMEM_LIMIT),
        name="pack",
    )(*arrays, *after)


def pack_turned(array, after, groups, group_width, start, width):
    rows = array.shape[0]

    def kernel(*refs):
        outs = refs[1 + len(after) : 1 + len(after) + groups]
        stages, sems = refs[1 + len(after) + groups : -1], refs[-1]
        me = lax.axis_index("head")
        pairs = []
        for shift in range(groups):
            group = lax.rem(me + shift, groups)
            column = pl.multiple_of(group * group_width + start, LANES)
            pairs.append((refs[0].at[:, pl.ds(column, width)], outs[shift]))
        staged(pairs, stages, sems)

    return pl.pallas_call(
        kernel,
        in_specs=[ANY] * (1 + len(after)),
        out_specs=[ANY] * groups,
        out_shape=[jax.ShapeDtypeStruct((rows, width), jnp.bfloat16)] * groups,
        scratch_shapes=stage_shapes([(rows, width)] * groups),
        cost_estimate=pl.CostEstimate(
            flops=0, bytes_accessed=4 * groups * rows * width, transcendentals=0
        ),
        compiler_params=pltpu.CompilerParams(vmem_limit_bytes=VMEM_LIMIT),
        name="pack_turned",
    )(array, *after)


def gate(array, after):
    def kernel(*refs):
        del refs

    return pl.pallas_call(
        kernel,
        in_specs=[ANY] * (1 + len(after)),
        out_specs=ANY,
        out_shape=jax.ShapeDtypeStruct(array.shape, array.dtype),
        input_output_aliases={0: 0},
        compiler_params=pltpu.CompilerParams(vmem_limit_bytes=VMEM_LIMIT),
        name="gate",
    )(array, *after)


def place(chunks, group_width, total_width, target=None):
    groups = len(chunks[0][1])
    rows = chunks[0][1][0].shape[0]
    blocks = [block for _, parts in chunks for block in parts]
    extra = [] if target is None else [target]

    def kernel(*refs):
        out = refs[len(blocks) + len(extra)]
        stages, sems = refs[len(blocks) + len(extra) + 1 : -1], refs[-1]
        me = lax.axis_index("head")
        pairs = []
        for i, (start, parts) in enumerate(chunks):
            for shift, part in enumerate(parts):
                group = lax.rem(me + shift, groups)
                column = pl.multiple_of(group * group_width + start, LANES)
                pairs.append((refs[i * groups + shift], out.at[:, pl.ds(column, part.shape[1])]))
        staged(pairs, stages, sems)

    return pl.pallas_call(
        kernel,
        in_specs=[ANY] * (len(blocks) + len(extra)),
        out_specs=ANY,
        out_shape=jax.ShapeDtypeStruct((rows, total_width), jnp.bfloat16),
        scratch_shapes=stage_shapes([block.shape for block in blocks]),
        input_output_aliases={len(blocks): 0} if extra else {},
        cost_estimate=pl.CostEstimate(
            flops=0,
            bytes_accessed=4 * rows * sum(block.shape[1] for block in blocks),
            transcendentals=0,
        ),
        compiler_params=pltpu.CompilerParams(vmem_limit_bytes=VMEM_LIMIT),
        name="place",
    )(*blocks, *extra)


def lane_fold(op, wide):
    folded = wide[:, :LANES]
    for start in range(LANES, wide.shape[1], LANES):
        folded = op(folded, wide[:, start : start + LANES])
    return folded


def attend_kernel(groups, heads, first_head, tile_count, query_lane, *refs):
    plan_ref, own_ref, prev_ref, next_ref, keep_ref = refs[:5]
    asked = refs[5 : 5 + groups] if query_lane is None else refs[5:6]
    outs = refs[-8 - groups : -8]
    pair_ref, q_ref, out_ref, scores_ref, top_ref, total_ref, sum_ref, sems = refs[-8:]
    slab_rows, width = out_ref.shape
    local_rows = slab_rows // groups
    head_size = width // heads
    tile_rows = slab_rows // tile_count
    scale = math.log2(math.e) / math.sqrt(head_size)
    me = lax.axis_index("head")

    def owner_rows(shift):
        owner = lax.rem(me + groups - shift, groups)
        return pl.ds(pl.multiple_of(owner * local_rows, 16), local_rows)

    def lanes(index):
        return pl.ds(index * head_size, head_size)

    loads = [
        (prev_ref, pair_ref.at[0]),
        (own_ref.at[:, pl.ds(0, 2 * width)], pair_ref.at[1]),
        (next_ref, pair_ref.at[2]),
    ]
    if query_lane is None:
        loads += [(piece, q_ref.at[owner_rows(i), :]) for i, piece in enumerate(asked)]
    else:
        loads.append((asked[0].at[:, pl.ds(query_lane, width)], q_ref))
    copies = [
        pltpu.make_async_copy(source, target, sems.at[i])
        for i, (source, target) in enumerate(loads)
    ]
    for copy in copies:
        copy.start()
    for copy in copies:
        copy.wait()

    def one_tile(i, carry):
        first_slab, slabs = plan_ref[4 * i], plan_ref[4 * i + 1]
        first_place, places = plan_ref[4 * i + 2], plan_ref[4 * i + 3]
        mine = pl.ds(pl.multiple_of(i * tile_rows, tile_rows), tile_rows)
        start = pl.multiple_of(first_place * tile_rows, tile_rows)
        top_ref[...] = jnp.full_like(top_ref, -jnp.inf)
        total_ref[...] = jnp.zeros_like(total_ref)
        sum_ref[...] = jnp.zeros_like(sum_ref)

        for count in range(1, tile_count + 1):
            rows = count * tile_rows

            def score(slab, carry, rows=rows):
                for h in range(heads):
                    found = lax.dot_general(
                        q_ref[mine, lanes(h)],
                        pair_ref[slab, pl.ds(start, rows), lanes(h)],
                        (((1,), (1,)), ((), ())),
                        preferred_element_type=jnp.float32,
                    )
                    scores_ref[h, slab, :, pl.ds(0, rows)] = found
                    top_ref[h] = jnp.maximum(top_ref[h], lane_fold(jnp.maximum, found))
                return carry

            @pl.when(places == count)
            def _(score=score):
                lax.fori_loop(first_slab, first_slab + slabs, score, 0)

        for h in range(heads):
            highest = jnp.max(top_ref[h], axis=1, keepdims=True) * scale
            top_ref[h] = jnp.broadcast_to(highest, top_ref.shape[1:])

        for count in range(1, tile_count + 1):
            rows = count * tile_rows

            def weigh(slab, carry, rows=rows):
                for h in range(heads):
                    highest = jnp.concatenate([top_ref[h]] * (rows // LANES), axis=1)
                    weights = jnp.exp2(scores_ref[h, slab, :, pl.ds(0, rows)] * scale - highest)
                    total_ref[h] += lane_fold(jnp.add, weights)
                    sum_ref[h] += jnp.dot(
                        weights.astype(jnp.bfloat16),
                        pair_ref[slab, pl.ds(start, rows), lanes(heads + h)],
                        preferred_element_type=jnp.float32,
                    )
                return carry

            @pl.when(places == count)
            def _(weigh=weigh):
                lax.fori_loop(first_slab, first_slab + slabs, weigh, 0)

        keep = keep_ref[mine, :].astype(jnp.float32)
        numbers = lax.broadcasted_iota(jnp.int32, keep.shape, 1)
        for h in range(heads):
            totals = jnp.sum(total_ref[h], axis=1, keepdims=True)
            kept = jnp.where(numbers == first_head + h, keep, 0.0)
            factor = jnp.sum(kept, axis=1, keepdims=True) * (10.0 / 9.0)
            out_ref[mine, lanes(h)] = (sum_ref[h] * (factor / totals)).astype(out_ref.dtype)
        return carry

    lax.fori_loop(0, tile_count, one_tile, 0)

    for shift in range(groups):
        outs[shift][...] = out_ref[owner_rows(shift), :]


def attend(
    plan, own, prev, behind, keep_mask, asked, lane, after, groups, first_head, heads, tile_count
):
    slab_rows, width = prev.shape[0], prev.shape[1] // 2
    local_rows = slab_rows // groups
    tile_rows = slab_rows // tile_count
    head_size = width // heads
    pairs = heads * slab_rows * 3 * slab_rows
    accumulator = pltpu.VMEM((heads, tile_rows, LANES), jnp.float32)
    return pl.pallas_call(
        functools.partial(attend_kernel, groups, heads, first_head, tile_count, lane),
        grid_spec=pltpu.PrefetchScalarGridSpec(
            num_scalar_prefetch=1,
            grid=(1,),
            in_specs=[ANY] * 3
            + [pl.BlockSpec(keep_mask.shape, lambda s, plan: (0, 0))]
            + [ANY] * (len(asked) + len(after)),
            out_specs=[pl.BlockSpec((local_rows, width), lambda s, plan: (0, 0))] * groups,
            scratch_shapes=[
                pltpu.VMEM((3, slab_rows, 2 * width), jnp.bfloat16),
                pltpu.VMEM((slab_rows, width), jnp.bfloat16),
                pltpu.VMEM((slab_rows, width), jnp.bfloat16),
                pltpu.VMEM((heads, 3, tile_rows, slab_rows), jnp.float32),
                accumulator,
                accumulator,
                pltpu.VMEM((heads, tile_rows, head_size), jnp.float32),
                pltpu.SemaphoreType.DMA((3 + len(asked),)),
            ],
        ),
        out_shape=[jax.ShapeDtypeStruct((local_rows, width), jnp.bfloat16)] * groups,
        compiler_params=pltpu.CompilerParams(vmem_limit_bytes=VMEM_LIMIT),
        cost_estimate=pl.CostEstimate(
            flops=12 * pairs * head_size,
            bytes_accessed=16 * slab_rows * width,
            transcendentals=pairs,
        ),
        name="attend",
    )(plan, own, prev, behind, keep_mask, *asked, *after)


def on_device(queries, key_vectors, value_vectors, reach_time, reach_width, keep_mask):
    groups = lax.axis_size("head")
    slab_count = lax.axis_size("seq")
    total_width = queries.shape[1]
    group_heads = keep_mask.shape[1]
    group_width = total_width // groups
    head_size = group_width // group_heads
    tile_count = reach_time.shape[0]
    plan = reach_plan(reach_time, reach_width, lax.axis_index("seq"), slab_count)
    onward = [(i, i + 1) for i in range(slab_count - 1)]
    backward = [(i + 1, i) for i in range(slab_count - 1)]

    def turn(array, shift):
        return lax.ppermute(array, "head", [(i, (i + shift) % groups) for i in range(groups)])

    parts = -(-(group_heads - 1) // CHUNK_HEADS)
    sizes = [(group_heads - 1 + i) // parts for i in reversed(range(parts))] + [1]
    count = len(sizes)
    firsts = [sum(sizes[:i]) for i in range(count)]
    by_permutes = max(count - 2, 0)

    def columns(i):
        return firsts[i] * head_size, sizes[i] * head_size

    def packed(i, after):
        parts = [(key_vectors, *columns(i)), (value_vectors, *columns(i))]
        if i + 1 == count:
            parts += [(queries, *columns(j)) for j in reversed(range(by_permutes, count))]
        return pack(parts, after, groups, group_width)

    def asked(i, after):
        blocks = pack_turned(queries, after, groups, group_width, *columns(i))
        return [blocks[0]] + [turn(blocks[shift], shift) for shift in range(1, groups)]

    def back_home(outs):
        return [outs[0]] + [turn(outs[shift], groups - shift) for shift in range(1, groups)]

    def arrive(i, after):
        own = lax.all_to_all(sent[i], "head", split_axis=0, concat_axis=0, tiled=True)
        own = gate(own, after) if after else own
        own = own.reshape(-1, own.shape[2])
        pairs = own[:, : 2 * sizes[i] * head_size]
        return own, lax.ppermute(pairs, "seq", onward), lax.ppermute(pairs, "seq", backward)

    sent, there, asks, done, early = [packed(0, [])], [], [], [], None
    there.append(arrive(0, []))
    if count > 1:
        sent.append(gate(packed(1, sent), there[0][:1]))
    for i in range(by_permutes):
        asks.append(asked(i, there[i - 1][1:] if i else sent[:1]))
    for i, heads in enumerate(sizes):
        if i + 1 < count:
            there.append(arrive(i + 1, [part[1][0] for part in done[-1:]]))
        if i + 2 < count:
            landed = [*there[i + 1][:1], *there[i][1:]] + [part[0] for part in asks[i + 1 :]]
            sent.append(gate(packed(i + 2, there[i][:1]), landed))
        hold = [part[0] for part in there[i + 1 :]] + sent[i + 2 :]
        hold += [part[1][0] for part in done[-1:]]
        hold += [part[0] for part in asks[i + 1 :]]
        if 0 < i == count - 2:
            hold += done[0][1][1:]
        if i + 1 == count and count > 2:
            early = place(done[:1], group_width, total_width)
            hold.append(early)
        if i < by_permutes:
            source, lane = asks[i], None
        else:
            source, lane = there[-1][:1], 2 * columns(count - 1)[1]
            lane += sum(columns(j)[1] for j in range(i + 1, count))
        outs = attend(
            plan, *there[i], keep_mask, source, lane, hold, groups, firsts[i], heads, tile_count
        )
        done.append((firsts[i] * head_size, back_home(outs) if i == 0 else outs))
    final = []
    for i, (start, outs) in enumerate(done):
        if 0 < i < count - 2:
            outs = [outs[0]] + [gate(block, there[-1][:1]) for block in outs[1:]]
        final.append((start, back_home(outs) if i else outs))
    return place(final[1:] if count > 2 else final, group_width, total_width, early)


def solution(mesh):
    return jax.shard_map(
        on_device,
        mesh=mesh,
        in_specs=(
            P(("seq", "head"), None),
            P(("seq", "head"), None),
            P(("seq", "head"), None),
            P("seq"),
            P("seq"),
            P("seq", "head"),
        ),
        out_specs=P(("seq", "head"), None),
        check_vma=False,
    )
```

```python
import functools
import math

import jax
import jax.numpy as jnp
from jax import lax
from jax.experimental import pallas as pl
from jax.experimental.pallas import tpu as pltpu
from jax.sharding import PartitionSpec as P

LANES = 128
CHUNK_HEADS = 3
ANY = pl.BlockSpec(memory_space=pl.ANY)
VMEM_LIMIT = 60 * 2**20


def reach_plan(reach_t, reach_w, slab_index, slab_count):
    tile_count = reach_t.shape[0]
    places = jnp.arange(tile_count, dtype=jnp.int32)
    before = jnp.minimum(jnp.minimum(reach_t, 1), slab_index)
    behind = jnp.minimum(jnp.minimum(reach_t, 1), slab_count - 1 - slab_index)
    low = jnp.maximum(places - reach_w, 0)
    high = jnp.minimum(places + reach_w, tile_count - 1)
    return jnp.stack([1 - before, before + 1 + behind, low, high - low + 1], axis=1).reshape(-1)


def staged(pairs, stages, sems):
    arriving, leaving = [], []
    for i, (source, target) in enumerate(pairs):
        arriving.append(pltpu.make_async_copy(source, stages[i], sems.at[0, i]))
        leaving.append(pltpu.make_async_copy(stages[i], target, sems.at[1, i]))
    for copy in arriving:
        copy.start()
    for first, second in zip(arriving, leaving):
        first.wait()
        second.start()
    for copy in leaving:
        copy.wait()


def stage_shapes(shapes):
    return [pltpu.VMEM(shape, jnp.bfloat16) for shape in shapes] + [
        pltpu.SemaphoreType.DMA((2, len(shapes)))
    ]


def pack(arrays, after, groups, group_width, start, width):
    rows = arrays[0].shape[0]

    def kernel(*refs):
        sources, out = refs[: len(arrays)], refs[len(arrays) + len(after)]
        stages, sems = refs[len(arrays) + len(after) + 1 : -1], refs[-1]
        pairs = []
        for group in range(groups):
            columns = pl.ds(group * group_width + start, width)
            for i, source in enumerate(sources):
                pairs.append((source.at[:, columns], out.at[group, :, pl.ds(i * width, width)]))
        staged(pairs, stages, sems)

    return pl.pallas_call(
        kernel,
        in_specs=[ANY] * (len(arrays) + len(after)),
        out_specs=ANY,
        out_shape=jax.ShapeDtypeStruct((groups, rows, len(arrays) * width), jnp.bfloat16),
        scratch_shapes=stage_shapes([(rows, width)] * (len(arrays) * groups)),
        cost_estimate=pl.CostEstimate(
            flops=0,
            bytes_accessed=4 * len(arrays) * groups * rows * width,
            transcendentals=0,
        ),
        compiler_params=pltpu.CompilerParams(vmem_limit_bytes=VMEM_LIMIT),
        name="pack",
    )(*arrays, *after)


def pack_turned(array, after, groups, group_width, start, width):
    rows = array.shape[0]

    def kernel(*refs):
        outs = refs[1 + len(after) : 1 + len(after) + groups]
        stages, sems = refs[1 + len(after) + groups : -1], refs[-1]
        me = lax.axis_index("head")
        pairs = []
        for shift in range(groups):
            group = lax.rem(me + shift, groups)
            column = pl.multiple_of(group * group_width + start, LANES)
            pairs.append((refs[0].at[:, pl.ds(column, width)], outs[shift]))
        staged(pairs, stages, sems)

    return pl.pallas_call(
        kernel,
        in_specs=[ANY] * (1 + len(after)),
        out_specs=[ANY] * groups,
        out_shape=[jax.ShapeDtypeStruct((rows, width), jnp.bfloat16)] * groups,
        scratch_shapes=stage_shapes([(rows, width)] * groups),
        cost_estimate=pl.CostEstimate(
            flops=0, bytes_accessed=4 * groups * rows * width, transcendentals=0
        ),
        compiler_params=pltpu.CompilerParams(vmem_limit_bytes=VMEM_LIMIT),
        name="pack_turned",
    )(array, *after)


def gate(array, after):
    def kernel(*refs):
        del refs

    return pl.pallas_call(
        kernel,
        in_specs=[ANY] * (1 + len(after)),
        out_specs=ANY,
        out_shape=jax.ShapeDtypeStruct(array.shape, array.dtype),
        input_output_aliases={0: 0},
        compiler_params=pltpu.CompilerParams(vmem_limit_bytes=VMEM_LIMIT),
        name="gate",
    )(array, *after)


def place(chunks, group_width, total_width, target=None):
    groups = len(chunks[0][1])
    rows = chunks[0][1][0].shape[0]
    blocks = [block for _, parts in chunks for block in parts]
    extra = [] if target is None else [target]

    def kernel(*refs):
        out = refs[len(blocks) + len(extra)]
        stages, sems = refs[len(blocks) + len(extra) + 1 : -1], refs[-1]
        me = lax.axis_index("head")
        pairs = []
        for i, (start, parts) in enumerate(chunks):
            for shift, part in enumerate(parts):
                group = lax.rem(me + shift, groups)
                column = pl.multiple_of(group * group_width + start, LANES)
                pairs.append((refs[i * groups + shift], out.at[:, pl.ds(column, part.shape[1])]))
        staged(pairs, stages, sems)

    return pl.pallas_call(
        kernel,
        in_specs=[ANY] * (len(blocks) + len(extra)),
        out_specs=ANY,
        out_shape=jax.ShapeDtypeStruct((rows, total_width), jnp.bfloat16),
        scratch_shapes=stage_shapes([block.shape for block in blocks]),
        input_output_aliases={len(blocks): 0} if extra else {},
        cost_estimate=pl.CostEstimate(
            flops=0,
            bytes_accessed=4 * rows * sum(block.shape[1] for block in blocks),
            transcendentals=0,
        ),
        compiler_params=pltpu.CompilerParams(vmem_limit_bytes=VMEM_LIMIT),
        name="place",
    )(*blocks, *extra)


def lane_fold(op, wide):
    folded = wide[:, :LANES]
    for start in range(LANES, wide.shape[1], LANES):
        folded = op(folded, wide[:, start : start + LANES])
    return folded


def attend_kernel(groups, heads, first_head, tile_count, in_pieces, *refs):
    plan_ref, own_ref, prev_ref, next_ref, keep_ref = refs[:5]
    pieces = refs[5 : 5 + groups] if in_pieces else ()
    outs = refs[-8 - groups : -8]
    pair_ref, q_ref, out_ref, scores_ref, top_ref, total_ref, sum_ref, sems = refs[-8:]
    slab_rows, width = out_ref.shape
    local_rows = slab_rows // groups
    head_size = width // heads
    tile_rows = slab_rows // tile_count
    scale = math.log2(math.e) / math.sqrt(head_size)
    me = lax.axis_index("head")

    def owner_rows(shift):
        owner = lax.rem(me + groups - shift, groups)
        return pl.ds(pl.multiple_of(owner * local_rows, 16), local_rows)

    def lanes(index):
        return pl.ds(index * head_size, head_size)

    loads = [
        (prev_ref, pair_ref.at[0]),
        (own_ref.at[:, pl.ds(0, 2 * width)], pair_ref.at[1]),
        (next_ref, pair_ref.at[2]),
    ]
    loads += [(piece, q_ref.at[owner_rows(i), :]) for i, piece in enumerate(pieces)]
    if not pieces:
        loads.append((own_ref.at[:, pl.ds(2 * width, width)], q_ref))
    copies = [
        pltpu.make_async_copy(source, target, sems.at[i])
        for i, (source, target) in enumerate(loads)
    ]
    for copy in copies:
        copy.start()
    for copy in copies:
        copy.wait()

    def one_tile(i, carry):
        first_slab, slabs = plan_ref[4 * i], plan_ref[4 * i + 1]
        first_place, places = plan_ref[4 * i + 2], plan_ref[4 * i + 3]
        mine = pl.ds(pl.multiple_of(i * tile_rows, tile_rows), tile_rows)
        start = pl.multiple_of(first_place * tile_rows, tile_rows)
        top_ref[...] = jnp.full_like(top_ref, -jnp.inf)
        total_ref[...] = jnp.zeros_like(total_ref)
        sum_ref[...] = jnp.zeros_like(sum_ref)

        for count in range(1, tile_count + 1):
            rows = count * tile_rows

            def score(slab, carry, rows=rows):
                for h in range(heads):
                    found = lax.dot_general(
                        q_ref[mine, lanes(h)],
                        pair_ref[slab, pl.ds(start, rows), lanes(h)],
                        (((1,), (1,)), ((), ())),
                        preferred_element_type=jnp.float32,
                    )
                    scores_ref[h, slab, :, pl.ds(0, rows)] = found
                    top_ref[h] = jnp.maximum(top_ref[h], lane_fold(jnp.maximum, found))
                return carry

            @pl.when(places == count)
            def _(score=score):
                lax.fori_loop(first_slab, first_slab + slabs, score, 0)

        for h in range(heads):
            highest = jnp.max(top_ref[h], axis=1, keepdims=True) * scale
            top_ref[h] = jnp.broadcast_to(highest, top_ref.shape[1:])

        for count in range(1, tile_count + 1):
            rows = count * tile_rows

            def weigh(slab, carry, rows=rows):
                for h in range(heads):
                    highest = jnp.concatenate([top_ref[h]] * (rows // LANES), axis=1)
                    weights = jnp.exp2(scores_ref[h, slab, :, pl.ds(0, rows)] * scale - highest)
                    total_ref[h] += lane_fold(jnp.add, weights)
                    sum_ref[h] += jnp.dot(
                        weights.astype(jnp.bfloat16),
                        pair_ref[slab, pl.ds(start, rows), lanes(heads + h)],
                        preferred_element_type=jnp.float32,
                    )
                return carry

            @pl.when(places == count)
            def _(weigh=weigh):
                lax.fori_loop(first_slab, first_slab + slabs, weigh, 0)

        keep = keep_ref[mine, :].astype(jnp.float32)
        numbers = lax.broadcasted_iota(jnp.int32, keep.shape, 1)
        for h in range(heads):
            totals = jnp.sum(total_ref[h], axis=1, keepdims=True)
            kept = jnp.where(numbers == first_head + h, keep, 0.0)
            factor = jnp.sum(kept, axis=1, keepdims=True) * (10.0 / 9.0)
            out_ref[mine, lanes(h)] = (sum_ref[h] * (factor / totals)).astype(out_ref.dtype)
        return carry

    lax.fori_loop(0, tile_count, one_tile, 0)

    for shift in range(groups):
        outs[shift][...] = out_ref[owner_rows(shift), :]


def attend(
    plan, own, prev, behind, keep_mask, pieces, after, groups, first_head, heads, tile_count
):
    slab_rows, width = prev.shape[0], prev.shape[1] // 2
    local_rows = slab_rows // groups
    tile_rows = slab_rows // tile_count
    head_size = width // heads
    pairs = heads * slab_rows * 3 * slab_rows
    accumulator = pltpu.VMEM((heads, tile_rows, LANES), jnp.float32)
    return pl.pallas_call(
        functools.partial(attend_kernel, groups, heads, first_head, tile_count, bool(pieces)),
        grid_spec=pltpu.PrefetchScalarGridSpec(
            num_scalar_prefetch=1,
            grid=(1,),
            in_specs=[ANY] * 3
            + [pl.BlockSpec(keep_mask.shape, lambda s, plan: (0, 0))]
            + [ANY] * (len(pieces) + len(after)),
            out_specs=[pl.BlockSpec((local_rows, width), lambda s, plan: (0, 0))] * groups,
            scratch_shapes=[
                pltpu.VMEM((3, slab_rows, 2 * width), jnp.bfloat16),
                pltpu.VMEM((slab_rows, width), jnp.bfloat16),
                pltpu.VMEM((slab_rows, width), jnp.bfloat16),
                pltpu.VMEM((heads, 3, tile_rows, slab_rows), jnp.float32),
                accumulator,
                accumulator,
                pltpu.VMEM((heads, tile_rows, head_size), jnp.float32),
                pltpu.SemaphoreType.DMA((3 + max(len(pieces), 1),)),
            ],
        ),
        out_shape=[jax.ShapeDtypeStruct((local_rows, width), jnp.bfloat16)] * groups,
        compiler_params=pltpu.CompilerParams(vmem_limit_bytes=VMEM_LIMIT),
        cost_estimate=pl.CostEstimate(
            flops=16 * pairs * head_size,
            bytes_accessed=16 * slab_rows * width,
            transcendentals=pairs,
        ),
        name="attend",
    )(plan, own, prev, behind, keep_mask, *pieces, *after)


def on_device(queries, key_vectors, value_vectors, reach_time, reach_width, keep_mask):
    groups = lax.axis_size("head")
    slab_count = lax.axis_size("seq")
    total_width = queries.shape[1]
    group_heads = keep_mask.shape[1]
    group_width = total_width // groups
    head_size = group_width // group_heads
    tile_count = reach_time.shape[0]
    plan = reach_plan(reach_time, reach_width, lax.axis_index("seq"), slab_count)
    onward = [(i, i + 1) for i in range(slab_count - 1)]
    backward = [(i + 1, i) for i in range(slab_count - 1)]

    def turn(array, shift):
        return lax.ppermute(array, "head", [(i, (i + shift) % groups) for i in range(groups)])

    parts = -(-(group_heads - 1) // CHUNK_HEADS)
    sizes = [(group_heads - 1 + i) // parts for i in reversed(range(parts))] + [1]
    count = len(sizes)
    firsts = [sum(sizes[:i]) for i in range(count)]

    def packed(i, after):
        arrays = (key_vectors, value_vectors, queries)[: 2 + (i + 1 == count)]
        start, width = firsts[i] * head_size, sizes[i] * head_size
        return pack(arrays, after, groups, group_width, start, width)

    def asked(i, after):
        start, width = firsts[i] * head_size, sizes[i] * head_size
        blocks = pack_turned(queries, after, groups, group_width, start, width)
        return [blocks[0]] + [turn(blocks[shift], shift) for shift in range(1, groups)]

    def arrive(i, after):
        own = lax.all_to_all(sent[i], "head", split_axis=0, concat_axis=0, tiled=True)
        own = gate(own, after) if after else own
        own = own.reshape(-1, own.shape[2])
        pairs = own[:, : 2 * sizes[i] * head_size]
        return own, lax.ppermute(pairs, "seq", onward), lax.ppermute(pairs, "seq", backward)

    sent, there, asks, done, early = [packed(0, [])], [], [], [], None
    there.append(arrive(0, []))
    if count > 1:
        asks.append(asked(0, sent))
        sent.append(gate(packed(1, sent), there[0][:1]))
    if count > 2:
        asks.append(asked(1, there[0][:1]))
    for i, heads in enumerate(sizes):
        if i + 1 < count:
            there.append(arrive(i + 1, [part[1][0] for part in done[-1:]]))
        if i + 2 < count:
            sent.append(gate(packed(i + 2, there[i][:1]), there[i + 1][:1]))
            if i:
                asks.append(asked(i + 1, done[i - 1][1][1:] + sent[i + 2 :]))
        hold = [part[0] for part in there[i + 1 :]] + sent[i + 2 :]
        hold += [part[1][0] for part in done[-1:]]
        hold += [block for part in done[-2:-1] for block in part[1][1:]]
        if i == 0:
            hold += [part[0] for part in asks[1:]]
        if i + 1 == count and count > 2:
            early = place(done[:-1], group_width, total_width)
            hold.append(early)
        pieces = asks[i] if i + 1 < count else []
        outs = attend(
            plan, *there[i], keep_mask, pieces, hold, groups, firsts[i], heads, tile_count
        )
        back = [outs[0]] + [turn(outs[shift], groups - shift) for shift in range(1, groups)]
        done.append((firsts[i] * head_size, back))
    return place(done[-2:] if count > 2 else done, group_width, total_width, early)


def solution(mesh):
    return jax.shard_map(
        on_device,
        mesh=mesh,
        in_specs=(
            P(("seq", "head"), None),
            P(("seq", "head"), None),
            P(("seq", "head"), None),
            P("seq"),
            P("seq"),
            P("seq", "head"),
        ),
        out_specs=P(("seq", "head"), None),
        check_vma=False,
    )
```

```python
import functools
import math

import jax
import jax.numpy as jnp
from jax import lax
from jax.experimental import pallas as pl
from jax.experimental.pallas import tpu as pltpu
from jax.sharding import PartitionSpec as P

LANES = 128
CHUNK_HEADS = 3
ANY = pl.BlockSpec(memory_space=pl.ANY)
VMEM_LIMIT = 60 * 2**20


def reach_plan(reach_t, reach_w, slab_index, slab_count):
    tile_count = reach_t.shape[0]
    places = jnp.arange(tile_count, dtype=jnp.int32)
    before = jnp.minimum(jnp.minimum(reach_t, 1), slab_index)
    behind = jnp.minimum(jnp.minimum(reach_t, 1), slab_count - 1 - slab_index)
    low = jnp.maximum(places - reach_w, 0)
    high = jnp.minimum(places + reach_w, tile_count - 1)
    return jnp.stack([1 - before, before + 1 + behind, low, high - low + 1], axis=1).reshape(-1)


def staged(pairs, stages, sems):
    arriving, leaving = [], []
    for i, (source, target) in enumerate(pairs):
        arriving.append(pltpu.make_async_copy(source, stages[i], sems.at[0, i]))
        leaving.append(pltpu.make_async_copy(stages[i], target, sems.at[1, i]))
    for copy in arriving:
        copy.start()
    for first, second in zip(arriving, leaving):
        first.wait()
        second.start()
    for copy in leaving:
        copy.wait()


def stage_shapes(shapes):
    return [pltpu.VMEM(shape, jnp.bfloat16) for shape in shapes] + [
        pltpu.SemaphoreType.DMA((2, len(shapes)))
    ]


def pack(arrays, after, groups, group_width, start, width):
    rows = arrays[0].shape[0]

    def kernel(*refs):
        sources, out = refs[: len(arrays)], refs[len(arrays) + len(after)]
        stages, sems = refs[len(arrays) + len(after) + 1 : -1], refs[-1]
        pairs = []
        for group in range(groups):
            columns = pl.ds(group * group_width + start, width)
            for i, source in enumerate(sources):
                pairs.append((source.at[:, columns], out.at[group, :, pl.ds(i * width, width)]))
        staged(pairs, stages, sems)

    return pl.pallas_call(
        kernel,
        in_specs=[ANY] * (len(arrays) + len(after)),
        out_specs=ANY,
        out_shape=jax.ShapeDtypeStruct((groups, rows, len(arrays) * width), jnp.bfloat16),
        scratch_shapes=stage_shapes([(rows, width)] * (len(arrays) * groups)),
        cost_estimate=pl.CostEstimate(
            flops=0,
            bytes_accessed=4 * len(arrays) * groups * rows * width,
            transcendentals=0,
        ),
        compiler_params=pltpu.CompilerParams(vmem_limit_bytes=VMEM_LIMIT),
        name="pack",
    )(*arrays, *after)


def pack_turned(array, after, groups, group_width, start, width):
    rows = array.shape[0]

    def kernel(*refs):
        outs = refs[1 + len(after) : 1 + len(after) + groups]
        stages, sems = refs[1 + len(after) + groups : -1], refs[-1]
        me = lax.axis_index("head")
        pairs = []
        for shift in range(groups):
            group = lax.rem(me + shift, groups)
            column = pl.multiple_of(group * group_width + start, LANES)
            pairs.append((refs[0].at[:, pl.ds(column, width)], outs[shift]))
        staged(pairs, stages, sems)

    return pl.pallas_call(
        kernel,
        in_specs=[ANY] * (1 + len(after)),
        out_specs=[ANY] * groups,
        out_shape=[jax.ShapeDtypeStruct((rows, width), jnp.bfloat16)] * groups,
        scratch_shapes=stage_shapes([(rows, width)] * groups),
        cost_estimate=pl.CostEstimate(
            flops=0, bytes_accessed=4 * groups * rows * width, transcendentals=0
        ),
        compiler_params=pltpu.CompilerParams(vmem_limit_bytes=VMEM_LIMIT),
        name="pack_turned",
    )(array, *after)


def gate(array, after):
    def kernel(*refs):
        del refs

    return pl.pallas_call(
        kernel,
        in_specs=[ANY] * (1 + len(after)),
        out_specs=ANY,
        out_shape=jax.ShapeDtypeStruct(array.shape, array.dtype),
        input_output_aliases={0: 0},
        compiler_params=pltpu.CompilerParams(vmem_limit_bytes=VMEM_LIMIT),
        name="gate",
    )(array, *after)


def place(chunks, group_width, total_width, target=None):
    groups = len(chunks[0][1])
    rows = chunks[0][1][0].shape[0]
    blocks = [block for _, parts in chunks for block in parts]
    extra = [] if target is None else [target]

    def kernel(*refs):
        out = refs[len(blocks) + len(extra)]
        stages, sems = refs[len(blocks) + len(extra) + 1 : -1], refs[-1]
        me = lax.axis_index("head")
        pairs = []
        for i, (start, parts) in enumerate(chunks):
            for shift, part in enumerate(parts):
                group = lax.rem(me + shift, groups)
                column = pl.multiple_of(group * group_width + start, LANES)
                pairs.append((refs[i * groups + shift], out.at[:, pl.ds(column, part.shape[1])]))
        staged(pairs, stages, sems)

    return pl.pallas_call(
        kernel,
        in_specs=[ANY] * (len(blocks) + len(extra)),
        out_specs=ANY,
        out_shape=jax.ShapeDtypeStruct((rows, total_width), jnp.bfloat16),
        scratch_shapes=stage_shapes([block.shape for block in blocks]),
        input_output_aliases={len(blocks): 0} if extra else {},
        cost_estimate=pl.CostEstimate(
            flops=0,
            bytes_accessed=4 * rows * sum(block.shape[1] for block in blocks),
            transcendentals=0,
        ),
        compiler_params=pltpu.CompilerParams(vmem_limit_bytes=VMEM_LIMIT),
        name="place",
    )(*blocks, *extra)


def lane_fold(op, wide):
    folded = wide[:, :LANES]
    for start in range(LANES, wide.shape[1], LANES):
        folded = op(folded, wide[:, start : start + LANES])
    return folded


def attend_kernel(groups, heads, first_head, tile_count, in_pieces, *refs):
    plan_ref, own_ref, prev_ref, next_ref, keep_ref = refs[:5]
    pieces = refs[5 : 5 + groups] if in_pieces else ()
    outs = refs[-8 - groups : -8]
    pair_ref, q_ref, out_ref, scores_ref, top_ref, total_ref, sum_ref, sems = refs[-8:]
    slab_rows, width = out_ref.shape
    local_rows = slab_rows // groups
    head_size = width // heads
    tile_rows = slab_rows // tile_count
    scale = math.log2(math.e) / math.sqrt(head_size)
    me = lax.axis_index("head")

    def owner_rows(shift):
        owner = lax.rem(me + groups - shift, groups)
        return pl.ds(pl.multiple_of(owner * local_rows, 16), local_rows)

    def lanes(index):
        return pl.ds(index * head_size, head_size)

    loads = [
        (prev_ref, pair_ref.at[0]),
        (own_ref.at[:, pl.ds(0, 2 * width)], pair_ref.at[1]),
        (next_ref, pair_ref.at[2]),
    ]
    loads += [(piece, q_ref.at[owner_rows(i), :]) for i, piece in enumerate(pieces)]
    if not pieces:
        loads.append((own_ref.at[:, pl.ds(2 * width, width)], q_ref))
    copies = [
        pltpu.make_async_copy(source, target, sems.at[i])
        for i, (source, target) in enumerate(loads)
    ]
    for copy in copies:
        copy.start()
    for copy in copies:
        copy.wait()

    def one_tile(i, carry):
        first_slab, slabs = plan_ref[4 * i], plan_ref[4 * i + 1]
        first_place, places = plan_ref[4 * i + 2], plan_ref[4 * i + 3]
        mine = pl.ds(pl.multiple_of(i * tile_rows, tile_rows), tile_rows)
        start = pl.multiple_of(first_place * tile_rows, tile_rows)
        top_ref[...] = jnp.full_like(top_ref, -jnp.inf)
        total_ref[...] = jnp.zeros_like(total_ref)
        sum_ref[...] = jnp.zeros_like(sum_ref)

        for count in range(1, tile_count + 1):
            rows = count * tile_rows

            def score(slab, carry, rows=rows):
                for h in range(heads):
                    found = lax.dot_general(
                        q_ref[mine, lanes(h)],
                        pair_ref[slab, pl.ds(start, rows), lanes(h)],
                        (((1,), (1,)), ((), ())),
                        preferred_element_type=jnp.float32,
                    )
                    scores_ref[h, slab, :, pl.ds(0, rows)] = found
                    top_ref[h] = jnp.maximum(top_ref[h], lane_fold(jnp.maximum, found))
                return carry

            @pl.when(places == count)
            def _(score=score):
                lax.fori_loop(first_slab, first_slab + slabs, score, 0)

        for h in range(heads):
            highest = jnp.max(top_ref[h], axis=1, keepdims=True) * scale
            top_ref[h] = jnp.broadcast_to(highest, top_ref.shape[1:])

        for count in range(1, tile_count + 1):
            rows = count * tile_rows

            def weigh(slab, carry, rows=rows):
                for h in range(heads):
                    highest = jnp.concatenate([top_ref[h]] * (rows // LANES), axis=1)
                    weights = jnp.exp2(scores_ref[h, slab, :, pl.ds(0, rows)] * scale - highest)
                    total_ref[h] += lane_fold(jnp.add, weights)
                    sum_ref[h] += jnp.dot(
                        weights.astype(jnp.bfloat16),
                        pair_ref[slab, pl.ds(start, rows), lanes(heads + h)],
                        preferred_element_type=jnp.float32,
                    )
                return carry

            @pl.when(places == count)
            def _(weigh=weigh):
                lax.fori_loop(first_slab, first_slab + slabs, weigh, 0)

        keep = keep_ref[mine, :].astype(jnp.float32)
        numbers = lax.broadcasted_iota(jnp.int32, keep.shape, 1)
        for h in range(heads):
            totals = jnp.sum(total_ref[h], axis=1, keepdims=True)
            kept = jnp.where(numbers == first_head + h, keep, 0.0)
            factor = jnp.sum(kept, axis=1, keepdims=True) * (10.0 / 9.0)
            out_ref[mine, lanes(h)] = (sum_ref[h] * (factor / totals)).astype(out_ref.dtype)
        return carry

    lax.fori_loop(0, tile_count, one_tile, 0)

    for shift in range(groups):
        outs[shift][...] = out_ref[owner_rows(shift), :]


def attend(
    plan, own, prev, behind, keep_mask, pieces, after, groups, first_head, heads, tile_count
):
    slab_rows, width = prev.shape[0], prev.shape[1] // 2
    local_rows = slab_rows // groups
    tile_rows = slab_rows // tile_count
    head_size = width // heads
    pairs = heads * slab_rows * 3 * slab_rows
    accumulator = pltpu.VMEM((heads, tile_rows, LANES), jnp.float32)
    return pl.pallas_call(
        functools.partial(attend_kernel, groups, heads, first_head, tile_count, bool(pieces)),
        grid_spec=pltpu.PrefetchScalarGridSpec(
            num_scalar_prefetch=1,
            grid=(1,),
            in_specs=[ANY] * 3
            + [pl.BlockSpec(keep_mask.shape, lambda s, plan: (0, 0))]
            + [ANY] * (len(pieces) + len(after)),
            out_specs=[pl.BlockSpec((local_rows, width), lambda s, plan: (0, 0))] * groups,
            scratch_shapes=[
                pltpu.VMEM((3, slab_rows, 2 * width), jnp.bfloat16),
                pltpu.VMEM((slab_rows, width), jnp.bfloat16),
                pltpu.VMEM((slab_rows, width), jnp.bfloat16),
                pltpu.VMEM((heads, 3, tile_rows, slab_rows), jnp.float32),
                accumulator,
                accumulator,
                pltpu.VMEM((heads, tile_rows, head_size), jnp.float32),
                pltpu.SemaphoreType.DMA((3 + max(len(pieces), 1),)),
            ],
        ),
        out_shape=[jax.ShapeDtypeStruct((local_rows, width), jnp.bfloat16)] * groups,
        compiler_params=pltpu.CompilerParams(vmem_limit_bytes=VMEM_LIMIT),
        cost_estimate=pl.CostEstimate(
            flops=16 * pairs * head_size,
            bytes_accessed=16 * slab_rows * width,
            transcendentals=pairs,
        ),
        name="attend",
    )(plan, own, prev, behind, keep_mask, *pieces, *after)


def on_device(queries, key_vectors, value_vectors, reach_time, reach_width, keep_mask):
    groups = lax.axis_size("head")
    slab_count = lax.axis_size("seq")
    total_width = queries.shape[1]
    group_heads = keep_mask.shape[1]
    group_width = total_width // groups
    head_size = group_width // group_heads
    tile_count = reach_time.shape[0]
    plan = reach_plan(reach_time, reach_width, lax.axis_index("seq"), slab_count)
    onward = [(i, i + 1) for i in range(slab_count - 1)]
    backward = [(i + 1, i) for i in range(slab_count - 1)]

    def turn(array, shift):
        return lax.ppermute(array, "head", [(i, (i + shift) % groups) for i in range(groups)])

    parts = -(-(group_heads - 1) // CHUNK_HEADS)
    sizes = [(group_heads - 1 + i) // parts for i in reversed(range(parts))] + [1]
    count = len(sizes)
    firsts = [sum(sizes[:i]) for i in range(count)]

    def packed(i, after):
        arrays = (key_vectors, value_vectors, queries)[: 2 + (i + 1 == count)]
        start, width = firsts[i] * head_size, sizes[i] * head_size
        return pack(arrays, after, groups, group_width, start, width)

    def asked(i, after):
        start, width = firsts[i] * head_size, sizes[i] * head_size
        blocks = pack_turned(queries, after, groups, group_width, start, width)
        return [blocks[0]] + [turn(blocks[shift], shift) for shift in range(1, groups)]

    def arrive(i, after):
        own = lax.all_to_all(sent[i], "head", split_axis=0, concat_axis=0, tiled=True)
        own = gate(own, after) if after else own
        own = own.reshape(-1, own.shape[2])
        pairs = own[:, : 2 * sizes[i] * head_size]
        return own, lax.ppermute(pairs, "seq", onward), lax.ppermute(pairs, "seq", backward)

    sent, there, asks, done, early = [packed(0, [])], [], [], [], None
    there.append(arrive(0, []))
    if count > 1:
        asks.append(asked(0, sent))
        sent.append(gate(packed(1, sent), there[0][:1]))
    if count > 2:
        asks.append(asked(1, there[0][:1]))
    for i, heads in enumerate(sizes):
        if i + 1 < count:
            there.append(arrive(i + 1, [part[1][0] for part in done[-1:]]))
        if i + 2 < count:
            landed = [*there[i + 1][:1], *there[i][1:], asks[i][0]]
            sent.append(gate(packed(i + 2, there[i][:1]), landed))
            if i:
                asks.append(asked(i + 1, done[i - 1][1][1:] + sent[i + 2 :]))
        hold = [part[0] for part in there[i + 1 :]] + sent[i + 2 :]
        hold += [part[1][0] for part in done[-1:]]
        hold += [block for part in done[-2:-1] for block in part[1][1:]]
        if i == 0:
            hold += [part[0] for part in asks[1:]]
        if i + 1 == count and count > 2:
            early = place(done[:-1], group_width, total_width)
            hold.append(early)
        pieces = asks[i] if i + 1 < count else []
        outs = attend(
            plan, *there[i], keep_mask, pieces, hold, groups, firsts[i], heads, tile_count
        )
        back = [outs[0]] + [turn(outs[shift], groups - shift) for shift in range(1, groups)]
        done.append((firsts[i] * head_size, back))
    return place(done[-2:] if count > 2 else done, group_width, total_width, early)


def solution(mesh):
    return jax.shard_map(
        on_device,
        mesh=mesh,
        in_specs=(
            P(("seq", "head"), None),
            P(("seq", "head"), None),
            P(("seq", "head"), None),
            P("seq"),
            P("seq"),
            P("seq", "head"),
        ),
        out_specs=P(("seq", "head"), None),
        check_vma=False,
    )
```

```python
import functools
import math

import jax
import jax.numpy as jnp
from jax import lax
from jax.experimental import pallas as pl
from jax.experimental.pallas import tpu as pltpu
from jax.sharding import PartitionSpec as P

LANES = 128
CHUNK_HEADS = 3
ANY = pl.BlockSpec(memory_space=pl.ANY)
VMEM_LIMIT = 60 * 2**20


def reach_plan(reach_t, reach_w, slab_index, slab_count):
    tile_count = reach_t.shape[0]
    places = jnp.arange(tile_count, dtype=jnp.int32)
    before = jnp.minimum(jnp.minimum(reach_t, 1), slab_index)
    behind = jnp.minimum(jnp.minimum(reach_t, 1), slab_count - 1 - slab_index)
    low = jnp.maximum(places - reach_w, 0)
    high = jnp.minimum(places + reach_w, tile_count - 1)
    return jnp.stack([1 - before, before + 1 + behind, low, high - low + 1], axis=1).reshape(-1)


def staged(pairs, stages, sems):
    arriving, leaving = [], []
    for i, (source, target) in enumerate(pairs):
        arriving.append(pltpu.make_async_copy(source, stages[i], sems.at[0, i]))
        leaving.append(pltpu.make_async_copy(stages[i], target, sems.at[1, i]))
    for copy in arriving:
        copy.start()
    for first, second in zip(arriving, leaving):
        first.wait()
        second.start()
    for copy in leaving:
        copy.wait()


def stage_shapes(shapes):
    return [pltpu.VMEM(shape, jnp.bfloat16) for shape in shapes] + [
        pltpu.SemaphoreType.DMA((2, len(shapes)))
    ]


def pack(parts, after, groups, group_width):
    rows = parts[0][0].shape[0]
    arrays = [array for array, _, _ in parts]
    total = sum(width for _, _, width in parts)

    def kernel(*refs):
        out = refs[len(parts) + len(after)]
        stages, sems = refs[len(parts) + len(after) + 1 : -1], refs[-1]
        pairs = []
        for group in range(groups):
            filled = 0
            for source, (_, start, width) in zip(refs, parts):
                columns = pl.ds(group * group_width + start, width)
                pairs.append((source.at[:, columns], out.at[group, :, pl.ds(filled, width)]))
                filled += width
        staged(pairs, stages, sems)

    return pl.pallas_call(
        kernel,
        in_specs=[ANY] * (len(parts) + len(after)),
        out_specs=ANY,
        out_shape=jax.ShapeDtypeStruct((groups, rows, total), jnp.bfloat16),
        scratch_shapes=stage_shapes([(rows, width) for _, _, width in parts] * groups),
        cost_estimate=pl.CostEstimate(
            flops=0, bytes_accessed=4 * groups * rows * total, transcendentals=0
        ),
        compiler_params=pltpu.CompilerParams(vmem_limit_bytes=VMEM_LIMIT),
        name="pack",
    )(*arrays, *after)


def pack_turned(array, after, groups, group_width, start, width):
    rows = array.shape[0]

    def kernel(*refs):
        outs = refs[1 + len(after) : 1 + len(after) + groups]
        stages, sems = refs[1 + len(after) + groups : -1], refs[-1]
        me = lax.axis_index("head")
        pairs = []
        for shift in range(groups):
            group = lax.rem(me + shift, groups)
            column = pl.multiple_of(group * group_width + start, LANES)
            pairs.append((refs[0].at[:, pl.ds(column, width)], outs[shift]))
        staged(pairs, stages, sems)

    return pl.pallas_call(
        kernel,
        in_specs=[ANY] * (1 + len(after)),
        out_specs=[ANY] * groups,
        out_shape=[jax.ShapeDtypeStruct((rows, width), jnp.bfloat16)] * groups,
        scratch_shapes=stage_shapes([(rows, width)] * groups),
        cost_estimate=pl.CostEstimate(
            flops=0, bytes_accessed=4 * groups * rows * width, transcendentals=0
        ),
        compiler_params=pltpu.CompilerParams(vmem_limit_bytes=VMEM_LIMIT),
        name="pack_turned",
    )(array, *after)


def gate(array, after):
    def kernel(*refs):
        del refs

    return pl.pallas_call(
        kernel,
        in_specs=[ANY] * (1 + len(after)),
        out_specs=ANY,
        out_shape=jax.ShapeDtypeStruct(array.shape, array.dtype),
        input_output_aliases={0: 0},
        compiler_params=pltpu.CompilerParams(vmem_limit_bytes=VMEM_LIMIT),
        name="gate",
    )(array, *after)


def place(chunks, group_width, total_width, target=None):
    groups = len(chunks[0][1])
    rows = chunks[0][1][0].shape[0]
    blocks = [block for _, parts in chunks for block in parts]
    extra = [] if target is None else [target]

    def kernel(*refs):
        out = refs[len(blocks) + len(extra)]
        stages, sems = refs[len(blocks) + len(extra) + 1 : -1], refs[-1]
        me = lax.axis_index("head")
        pairs = []
        for i, (start, parts) in enumerate(chunks):
            for shift, part in enumerate(parts):
                group = lax.rem(me + shift, groups)
                column = pl.multiple_of(group * group_width + start, LANES)
                pairs.append((refs[i * groups + shift], out.at[:, pl.ds(column, part.shape[1])]))
        staged(pairs, stages, sems)

    return pl.pallas_call(
        kernel,
        in_specs=[ANY] * (len(blocks) + len(extra)),
        out_specs=ANY,
        out_shape=jax.ShapeDtypeStruct((rows, total_width), jnp.bfloat16),
        scratch_shapes=stage_shapes([block.shape for block in blocks]),
        input_output_aliases={len(blocks): 0} if extra else {},
        cost_estimate=pl.CostEstimate(
            flops=0,
            bytes_accessed=4 * rows * sum(block.shape[1] for block in blocks),
            transcendentals=0,
        ),
        compiler_params=pltpu.CompilerParams(vmem_limit_bytes=VMEM_LIMIT),
        name="place",
    )(*blocks, *extra)


def lane_fold(op, wide):
    folded = wide[:, :LANES]
    for start in range(LANES, wide.shape[1], LANES):
        folded = op(folded, wide[:, start : start + LANES])
    return folded


def attend_kernel(groups, heads, first_head, tile_count, query_lane, *refs):
    plan_ref, own_ref, prev_ref, next_ref, keep_ref = refs[:5]
    asked = refs[5 : 5 + groups] if query_lane is None else refs[5:6]
    outs = refs[-8 - groups : -8]
    pair_ref, q_ref, out_ref, scores_ref, top_ref, total_ref, sum_ref, sems = refs[-8:]
    slab_rows, width = out_ref.shape
    local_rows = slab_rows // groups
    head_size = width // heads
    tile_rows = slab_rows // tile_count
    scale = math.log2(math.e) / math.sqrt(head_size)
    me = lax.axis_index("head")

    def owner_rows(shift):
        owner = lax.rem(me + groups - shift, groups)
        return pl.ds(pl.multiple_of(owner * local_rows, 16), local_rows)

    def lanes(index):
        return pl.ds(index * head_size, head_size)

    loads = [
        (prev_ref, pair_ref.at[0]),
        (own_ref.at[:, pl.ds(0, 2 * width)], pair_ref.at[1]),
        (next_ref, pair_ref.at[2]),
    ]
    if query_lane is None:
        loads += [(piece, q_ref.at[owner_rows(i), :]) for i, piece in enumerate(asked)]
    else:
        loads.append((asked[0].at[:, pl.ds(query_lane, width)], q_ref))
    copies = [
        pltpu.make_async_copy(source, target, sems.at[i])
        for i, (source, target) in enumerate(loads)
    ]
    for copy in copies:
        copy.start()
    for copy in copies:
        copy.wait()

    def one_tile(i, carry):
        first_slab, slabs = plan_ref[4 * i], plan_ref[4 * i + 1]
        first_place, places = plan_ref[4 * i + 2], plan_ref[4 * i + 3]
        mine = pl.ds(pl.multiple_of(i * tile_rows, tile_rows), tile_rows)
        start = pl.multiple_of(first_place * tile_rows, tile_rows)
        top_ref[...] = jnp.full_like(top_ref, -jnp.inf)
        total_ref[...] = jnp.zeros_like(total_ref)
        sum_ref[...] = jnp.zeros_like(sum_ref)

        for count in range(1, tile_count + 1):
            rows = count * tile_rows

            def score(slab, carry, rows=rows):
                for h in range(heads):
                    found = lax.dot_general(
                        q_ref[mine, lanes(h)],
                        pair_ref[slab, pl.ds(start, rows), lanes(h)],
                        (((1,), (1,)), ((), ())),
                        preferred_element_type=jnp.float32,
                    )
                    scores_ref[h, slab, :, pl.ds(0, rows)] = found
                    top_ref[h] = jnp.maximum(top_ref[h], lane_fold(jnp.maximum, found))
                return carry

            @pl.when(places == count)
            def _(score=score):
                lax.fori_loop(first_slab, first_slab + slabs, score, 0)

        for h in range(heads):
            highest = jnp.max(top_ref[h], axis=1, keepdims=True) * scale
            top_ref[h] = jnp.broadcast_to(highest, top_ref.shape[1:])

        for count in range(1, tile_count + 1):
            rows = count * tile_rows

            def weigh(slab, carry, rows=rows):
                for h in range(heads):
                    highest = jnp.concatenate([top_ref[h]] * (rows // LANES), axis=1)
                    weights = jnp.exp2(scores_ref[h, slab, :, pl.ds(0, rows)] * scale - highest)
                    total_ref[h] += lane_fold(jnp.add, weights)
                    sum_ref[h] += jnp.dot(
                        weights.astype(jnp.bfloat16),
                        pair_ref[slab, pl.ds(start, rows), lanes(heads + h)],
                        preferred_element_type=jnp.float32,
                    )
                return carry

            @pl.when(places == count)
            def _(weigh=weigh):
                lax.fori_loop(first_slab, first_slab + slabs, weigh, 0)

        keep = keep_ref[mine, :].astype(jnp.float32)
        numbers = lax.broadcasted_iota(jnp.int32, keep.shape, 1)
        for h in range(heads):
            totals = jnp.sum(total_ref[h], axis=1, keepdims=True)
            kept = jnp.where(numbers == first_head + h, keep, 0.0)
            factor = jnp.sum(kept, axis=1, keepdims=True) * (10.0 / 9.0)
            out_ref[mine, lanes(h)] = (sum_ref[h] * (factor / totals)).astype(out_ref.dtype)
        return carry

    lax.fori_loop(0, tile_count, one_tile, 0)

    for shift in range(groups):
        outs[shift][...] = out_ref[owner_rows(shift), :]


def attend(
    plan, own, prev, behind, keep_mask, asked, lane, after, groups, first_head, heads, tile_count
):
    slab_rows, width = prev.shape[0], prev.shape[1] // 2
    local_rows = slab_rows // groups
    tile_rows = slab_rows // tile_count
    head_size = width // heads
    pairs = heads * slab_rows * 3 * slab_rows
    accumulator = pltpu.VMEM((heads, tile_rows, LANES), jnp.float32)
    return pl.pallas_call(
        functools.partial(attend_kernel, groups, heads, first_head, tile_count, lane),
        grid_spec=pltpu.PrefetchScalarGridSpec(
            num_scalar_prefetch=1,
            grid=(1,),
            in_specs=[ANY] * 3
            + [pl.BlockSpec(keep_mask.shape, lambda s, plan: (0, 0))]
            + [ANY] * (len(asked) + len(after)),
            out_specs=[pl.BlockSpec((local_rows, width), lambda s, plan: (0, 0))] * groups,
            scratch_shapes=[
                pltpu.VMEM((3, slab_rows, 2 * width), jnp.bfloat16),
                pltpu.VMEM((slab_rows, width), jnp.bfloat16),
                pltpu.VMEM((slab_rows, width), jnp.bfloat16),
                pltpu.VMEM((heads, 3, tile_rows, slab_rows), jnp.float32),
                accumulator,
                accumulator,
                pltpu.VMEM((heads, tile_rows, head_size), jnp.float32),
                pltpu.SemaphoreType.DMA((3 + len(asked),)),
            ],
        ),
        out_shape=[jax.ShapeDtypeStruct((local_rows, width), jnp.bfloat16)] * groups,
        compiler_params=pltpu.CompilerParams(vmem_limit_bytes=VMEM_LIMIT),
        cost_estimate=pl.CostEstimate(
            flops=12 * pairs * head_size,
            bytes_accessed=16 * slab_rows * width,
            transcendentals=pairs,
        ),
        name="attend",
    )(plan, own, prev, behind, keep_mask, *asked, *after)


def on_device(queries, key_vectors, value_vectors, reach_time, reach_width, keep_mask):
    groups = lax.axis_size("head")
    slab_count = lax.axis_size("seq")
    total_width = queries.shape[1]
    group_heads = keep_mask.shape[1]
    group_width = total_width // groups
    head_size = group_width // group_heads
    tile_count = reach_time.shape[0]
    plan = reach_plan(reach_time, reach_width, lax.axis_index("seq"), slab_count)
    onward = [(i, i + 1) for i in range(slab_count - 1)]
    backward = [(i + 1, i) for i in range(slab_count - 1)]

    def turn(array, shift):
        return lax.ppermute(array, "head", [(i, (i + shift) % groups) for i in range(groups)])

    parts = -(-(group_heads - 1) // CHUNK_HEADS)
    sizes = [(group_heads - 1 + i) // parts for i in reversed(range(parts))] + [1]
    count = len(sizes)
    firsts = [sum(sizes[:i]) for i in range(count)]
    by_permutes = max(count - 2, 0)

    def columns(i):
        return firsts[i] * head_size, sizes[i] * head_size

    def packed(i, after):
        parts = [(key_vectors, *columns(i)), (value_vectors, *columns(i))]
        if i >= by_permutes:
            parts.append((queries, *columns(i)))
        return pack(parts, after, groups, group_width)

    def asked(i, after):
        blocks = pack_turned(queries, after, groups, group_width, *columns(i))
        return [blocks[0]] + [turn(blocks[shift], shift) for shift in range(1, groups)]

    def arrive(i, after):
        own = lax.all_to_all(sent[i], "head", split_axis=0, concat_axis=0, tiled=True)
        own = gate(own, after) if after else own
        own = own.reshape(-1, own.shape[2])
        pairs = own[:, : 2 * sizes[i] * head_size]
        return own, lax.ppermute(pairs, "seq", onward), lax.ppermute(pairs, "seq", backward)

    sent, there, asks, done, early = [packed(0, [])], [], [], [], None
    there.append(arrive(0, []))
    if count > 1:
        sent.append(gate(packed(1, sent), there[0][:1]))
    for i in range(by_permutes):
        asks.append(asked(i, there[i - 1][:1] if i else sent[:1]))
    for i, heads in enumerate(sizes):
        if i + 1 < count:
            there.append(arrive(i + 1, [part[1][0] for part in done[-1:]]))
        if i + 2 < count:
            landed = [*there[i + 1][:1], *there[i][1:], *asks[i][1:]]
            sent.append(gate(packed(i + 2, there[i][:1]), landed))
        hold = [part[0] for part in there[i + 1 :]] + sent[i + 2 :]
        hold += [part[1][0] for part in done[-1:]]
        hold += [block for part in done[-2:-1] for block in part[1][1:]]
        hold += [part[0] for part in asks[i + 1 :]]
        if i + 1 == count and count > 2:
            early = place(done[:1], group_width, total_width)
            hold.append(early)
        if i < by_permutes:
            source, lane = asks[i], None
        else:
            source, lane = there[i][:1], 2 * columns(i)[1]
        outs = attend(
            plan, *there[i], keep_mask, source, lane, hold, groups, firsts[i], heads, tile_count
        )
        back = [outs[0]] + [turn(outs[shift], groups - shift) for shift in range(1, groups)]
        done.append((firsts[i] * head_size, back))
    return place(done[1:] if count > 2 else done, group_width, total_width, early)


def solution(mesh):
    return jax.shard_map(
        on_device,
        mesh=mesh,
        in_specs=(
            P(("seq", "head"), None),
            P(("seq", "head"), None),
            P(("seq", "head"), None),
            P("seq"),
            P("seq"),
            P("seq", "head"),
        ),
        out_specs=P(("seq", "head"), None),
        check_vma=False,
    )
```

```python
import functools
import math

import jax
import jax.numpy as jnp
from jax import lax
from jax.experimental import pallas as pl
from jax.experimental.pallas import tpu as pltpu
from jax.sharding import PartitionSpec as P

LANES = 128
CHUNK_HEADS = 3
ANY = pl.BlockSpec(memory_space=pl.ANY)
VMEM_LIMIT = 60 * 2**20


def reach_plan(reach_t, reach_w, slab_index, slab_count):
    tile_count = reach_t.shape[0]
    places = jnp.arange(tile_count, dtype=jnp.int32)
    before = jnp.minimum(jnp.minimum(reach_t, 1), slab_index)
    behind = jnp.minimum(jnp.minimum(reach_t, 1), slab_count - 1 - slab_index)
    low = jnp.maximum(places - reach_w, 0)
    high = jnp.minimum(places + reach_w, tile_count - 1)
    return jnp.stack([1 - before, before + 1 + behind, low, high - low + 1], axis=1).reshape(-1)


def staged(pairs, stages, sems):
    arriving, leaving = [], []
    for i, (source, target) in enumerate(pairs):
        arriving.append(pltpu.make_async_copy(source, stages[i], sems.at[0, i]))
        leaving.append(pltpu.make_async_copy(stages[i], target, sems.at[1, i]))
    for copy in arriving:
        copy.start()
    for first, second in zip(arriving, leaving):
        first.wait()
        second.start()
    for copy in leaving:
        copy.wait()


def stage_shapes(shapes):
    return [pltpu.VMEM(shape, jnp.bfloat16) for shape in shapes] + [
        pltpu.SemaphoreType.DMA((2, len(shapes)))
    ]


def pack(arrays, after, groups, group_width, start, width):
    rows = arrays[0].shape[0]

    def kernel(*refs):
        sources, out = refs[: len(arrays)], refs[len(arrays) + len(after)]
        stages, sems = refs[len(arrays) + len(after) + 1 : -1], refs[-1]
        pairs = []
        for group in range(groups):
            columns = pl.ds(group * group_width + start, width)
            for i, source in enumerate(sources):
                pairs.append((source.at[:, columns], out.at[group, :, pl.ds(i * width, width)]))
        staged(pairs, stages, sems)

    return pl.pallas_call(
        kernel,
        in_specs=[ANY] * (len(arrays) + len(after)),
        out_specs=ANY,
        out_shape=jax.ShapeDtypeStruct((groups, rows, len(arrays) * width), jnp.bfloat16),
        scratch_shapes=stage_shapes([(rows, width)] * (len(arrays) * groups)),
        cost_estimate=pl.CostEstimate(
            flops=0,
            bytes_accessed=4 * len(arrays) * groups * rows * width,
            transcendentals=0,
        ),
        compiler_params=pltpu.CompilerParams(vmem_limit_bytes=VMEM_LIMIT),
        name="pack",
    )(*arrays, *after)


def pack_turned(array, after, groups, group_width, start, width):
    rows = array.shape[0]

    def kernel(*refs):
        outs = refs[1 + len(after) : 1 + len(after) + groups]
        stages, sems = refs[1 + len(after) + groups : -1], refs[-1]
        me = lax.axis_index("head")
        pairs = []
        for shift in range(groups):
            group = lax.rem(me + shift, groups)
            column = pl.multiple_of(group * group_width + start, LANES)
            pairs.append((refs[0].at[:, pl.ds(column, width)], outs[shift]))
        staged(pairs, stages, sems)

    return pl.pallas_call(
        kernel,
        in_specs=[ANY] * (1 + len(after)),
        out_specs=[ANY] * groups,
        out_shape=[jax.ShapeDtypeStruct((rows, width), jnp.bfloat16)] * groups,
        scratch_shapes=stage_shapes([(rows, width)] * groups),
        cost_estimate=pl.CostEstimate(
            flops=0, bytes_accessed=4 * groups * rows * width, transcendentals=0
        ),
        compiler_params=pltpu.CompilerParams(vmem_limit_bytes=VMEM_LIMIT),
        name="pack_turned",
    )(array, *after)


def gate(array, after):
    def kernel(*refs):
        del refs

    return pl.pallas_call(
        kernel,
        in_specs=[ANY] * (1 + len(after)),
        out_specs=ANY,
        out_shape=jax.ShapeDtypeStruct(array.shape, array.dtype),
        input_output_aliases={0: 0},
        compiler_params=pltpu.CompilerParams(vmem_limit_bytes=VMEM_LIMIT),
        name="gate",
    )(array, *after)


def place(chunks, group_width, total_width, target=None):
    groups = len(chunks[0][1])
    rows = chunks[0][1][0].shape[0]
    blocks = [block for _, parts in chunks for block in parts]
    extra = [] if target is None else [target]

    def kernel(*refs):
        out = refs[len(blocks) + len(extra)]
        stages, sems = refs[len(blocks) + len(extra) + 1 : -1], refs[-1]
        me = lax.axis_index("head")
        pairs = []
        for i, (start, parts) in enumerate(chunks):
            for shift, part in enumerate(parts):
                group = lax.rem(me + shift, groups)
                column = pl.multiple_of(group * group_width + start, LANES)
                pairs.append((refs[i * groups + shift], out.at[:, pl.ds(column, part.shape[1])]))
        staged(pairs, stages, sems)

    return pl.pallas_call(
        kernel,
        in_specs=[ANY] * (len(blocks) + len(extra)),
        out_specs=ANY,
        out_shape=jax.ShapeDtypeStruct((rows, total_width), jnp.bfloat16),
        scratch_shapes=stage_shapes([block.shape for block in blocks]),
        input_output_aliases={len(blocks): 0} if extra else {},
        cost_estimate=pl.CostEstimate(
            flops=0,
            bytes_accessed=4 * rows * sum(block.shape[1] for block in blocks),
            transcendentals=0,
        ),
        compiler_params=pltpu.CompilerParams(vmem_limit_bytes=VMEM_LIMIT),
        name="place",
    )(*blocks, *extra)


def lane_fold(op, wide):
    folded = wide[:, :LANES]
    for start in range(LANES, wide.shape[1], LANES):
        folded = op(folded, wide[:, start : start + LANES])
    return folded


def attend_kernel(groups, heads, first_head, tile_count, in_pieces, *refs):
    plan_ref, own_ref, prev_ref, next_ref, keep_ref = refs[:5]
    pieces = refs[5 : 5 + groups] if in_pieces else ()
    outs = refs[-8 - groups : -8]
    pair_ref, q_ref, out_ref, scores_ref, top_ref, total_ref, sum_ref, sems = refs[-8:]
    slab_rows, width = out_ref.shape
    local_rows = slab_rows // groups
    head_size = width // heads
    tile_rows = slab_rows // tile_count
    scale = math.log2(math.e) / math.sqrt(head_size)
    me = lax.axis_index("head")

    def owner_rows(shift):
        owner = lax.rem(me + groups - shift, groups)
        return pl.ds(pl.multiple_of(owner * local_rows, 16), local_rows)

    def lanes(index):
        return pl.ds(index * head_size, head_size)

    loads = [
        (prev_ref, pair_ref.at[0]),
        (own_ref.at[:, pl.ds(0, 2 * width)], pair_ref.at[1]),
        (next_ref, pair_ref.at[2]),
    ]
    loads += [(piece, q_ref.at[owner_rows(i), :]) for i, piece in enumerate(pieces)]
    if not pieces:
        loads.append((own_ref.at[:, pl.ds(2 * width, width)], q_ref))
    copies = [
        pltpu.make_async_copy(source, target, sems.at[i])
        for i, (source, target) in enumerate(loads)
    ]
    for copy in copies:
        copy.start()
    for copy in copies:
        copy.wait()

    def one_tile(i, carry):
        first_slab, slabs = plan_ref[4 * i], plan_ref[4 * i + 1]
        first_place, places = plan_ref[4 * i + 2], plan_ref[4 * i + 3]
        mine = pl.ds(pl.multiple_of(i * tile_rows, tile_rows), tile_rows)
        start = pl.multiple_of(first_place * tile_rows, tile_rows)
        top_ref[...] = jnp.full_like(top_ref, -jnp.inf)
        total_ref[...] = jnp.zeros_like(total_ref)
        sum_ref[...] = jnp.zeros_like(sum_ref)

        for count in range(1, tile_count + 1):
            rows = count * tile_rows

            def score(slab, carry, rows=rows):
                for h in range(heads):
                    found = lax.dot_general(
                        q_ref[mine, lanes(h)],
                        pair_ref[slab, pl.ds(start, rows), lanes(h)],
                        (((1,), (1,)), ((), ())),
                        preferred_element_type=jnp.float32,
                    )
                    scores_ref[h, slab, :, pl.ds(0, rows)] = found
                    top_ref[h] = jnp.maximum(top_ref[h], lane_fold(jnp.maximum, found))
                return carry

            @pl.when(places == count)
            def _(score=score):
                lax.fori_loop(first_slab, first_slab + slabs, score, 0)

        for h in range(heads):
            highest = jnp.max(top_ref[h], axis=1, keepdims=True) * scale
            top_ref[h] = jnp.broadcast_to(highest, top_ref.shape[1:])

        for count in range(1, tile_count + 1):
            rows = count * tile_rows

            def weigh(slab, carry, rows=rows):
                for h in range(heads):
                    highest = jnp.concatenate([top_ref[h]] * (rows // LANES), axis=1)
                    weights = jnp.exp2(scores_ref[h, slab, :, pl.ds(0, rows)] * scale - highest)
                    total_ref[h] += lane_fold(jnp.add, weights)
                    sum_ref[h] += jnp.dot(
                        weights.astype(jnp.bfloat16),
                        pair_ref[slab, pl.ds(start, rows), lanes(heads + h)],
                        preferred_element_type=jnp.float32,
                    )
                return carry

            @pl.when(places == count)
            def _(weigh=weigh):
                lax.fori_loop(first_slab, first_slab + slabs, weigh, 0)

        keep = keep_ref[mine, :].astype(jnp.float32)
        numbers = lax.broadcasted_iota(jnp.int32, keep.shape, 1)
        for h in range(heads):
            totals = jnp.sum(total_ref[h], axis=1, keepdims=True)
            kept = jnp.where(numbers == first_head + h, keep, 0.0)
            factor = jnp.sum(kept, axis=1, keepdims=True) * (10.0 / 9.0)
            out_ref[mine, lanes(h)] = (sum_ref[h] * (factor / totals)).astype(out_ref.dtype)
        return carry

    lax.fori_loop(0, tile_count, one_tile, 0)

    for shift in range(groups):
        outs[shift][...] = out_ref[owner_rows(shift), :]


def attend(
    plan, own, prev, behind, keep_mask, pieces, after, groups, first_head, heads, tile_count
):
    slab_rows, width = prev.shape[0], prev.shape[1] // 2
    local_rows = slab_rows // groups
    tile_rows = slab_rows // tile_count
    head_size = width // heads
    pairs = heads * slab_rows * 3 * slab_rows
    accumulator = pltpu.VMEM((heads, tile_rows, LANES), jnp.float32)
    return pl.pallas_call(
        functools.partial(attend_kernel, groups, heads, first_head, tile_count, bool(pieces)),
        grid_spec=pltpu.PrefetchScalarGridSpec(
            num_scalar_prefetch=1,
            grid=(1,),
            in_specs=[ANY] * 3
            + [pl.BlockSpec(keep_mask.shape, lambda s, plan: (0, 0))]
            + [ANY] * (len(pieces) + len(after)),
            out_specs=[pl.BlockSpec((local_rows, width), lambda s, plan: (0, 0))] * groups,
            scratch_shapes=[
                pltpu.VMEM((3, slab_rows, 2 * width), jnp.bfloat16),
                pltpu.VMEM((slab_rows, width), jnp.bfloat16),
                pltpu.VMEM((slab_rows, width), jnp.bfloat16),
                pltpu.VMEM((heads, 3, tile_rows, slab_rows), jnp.float32),
                accumulator,
                accumulator,
                pltpu.VMEM((heads, tile_rows, head_size), jnp.float32),
                pltpu.SemaphoreType.DMA((3 + max(len(pieces), 1),)),
            ],
        ),
        out_shape=[jax.ShapeDtypeStruct((local_rows, width), jnp.bfloat16)] * groups,
        compiler_params=pltpu.CompilerParams(vmem_limit_bytes=VMEM_LIMIT),
        cost_estimate=pl.CostEstimate(
            flops=16 * pairs * head_size,
            bytes_accessed=16 * slab_rows * width,
            transcendentals=pairs,
        ),
        name="attend",
    )(plan, own, prev, behind, keep_mask, *pieces, *after)


def on_device(queries, key_vectors, value_vectors, reach_time, reach_width, keep_mask):
    groups = lax.axis_size("head")
    slab_count = lax.axis_size("seq")
    total_width = queries.shape[1]
    group_heads = keep_mask.shape[1]
    group_width = total_width // groups
    head_size = group_width // group_heads
    tile_count = reach_time.shape[0]
    plan = reach_plan(reach_time, reach_width, lax.axis_index("seq"), slab_count)
    onward = [(i, i + 1) for i in range(slab_count - 1)]
    backward = [(i + 1, i) for i in range(slab_count - 1)]

    def turn(array, shift):
        return lax.ppermute(array, "head", [(i, (i + shift) % groups) for i in range(groups)])

    parts = -(-(group_heads - 1) // CHUNK_HEADS)
    sizes = [(group_heads - 1 + i) // parts for i in reversed(range(parts))] + [1]
    count = len(sizes)
    firsts = [sum(sizes[:i]) for i in range(count)]

    def packed(i, after):
        arrays = (key_vectors, value_vectors)
        start, width = firsts[i] * head_size, sizes[i] * head_size
        return pack(arrays, after, groups, group_width, start, width)

    def asked(i, after):
        start, width = firsts[i] * head_size, sizes[i] * head_size
        blocks = pack_turned(queries, after, groups, group_width, start, width)
        return [blocks[0]] + [turn(blocks[shift], shift) for shift in range(1, groups)]

    def arrive(parts, after):
        own = lax.all_to_all(parts, "head", split_axis=0, concat_axis=0, tiled=True)
        own = gate(own, after) if after else own
        own = own.reshape(-1, own.shape[2])
        return own, lax.ppermute(own, "seq", onward), lax.ppermute(own, "seq", backward)

    sent = [packed(0, [])]
    there, asks, done, early = [arrive(sent[0], [])], [asked(0, sent)], [], None
    if count > 1:
        sent.append(gate(packed(1, sent), there[0][:1]))
        asks.append(asked(1, there[0][:1]))
    for i, heads in enumerate(sizes):
        if i + 1 < count:
            there.append(arrive(sent[i + 1], [part[1][0] for part in done[-1:]]))
        if i + 2 < count:
            sent.append(gate(packed(i + 2, there[i][:1]), there[i + 1][:1]))
            asks.append(asked(i + 2, there[i + 1][:1]))
        hold = [part[0] for part in there[i + 1 :] + asks[i + 2 :]] + sent[i + 2 :]
        hold += [part[1][0] for part in done[-1:]]
        hold += [block for part in done[-2:-1] for block in part[1][1:]]
        if i + 1 == count and count > 2:
            early = place(done[:-1], group_width, total_width)
            hold.append(early)
        outs = attend(
            plan, *there[i], keep_mask, asks[i], hold, groups, firsts[i], heads, tile_count
        )
        back = [outs[0]] + [turn(outs[shift], groups - shift) for shift in range(1, groups)]
        done.append((firsts[i] * head_size, back))
    return place(done[-2:] if count > 2 else done, group_width, total_width, early)


def solution(mesh):
    return jax.shard_map(
        on_device,
        mesh=mesh,
        in_specs=(
            P(("seq", "head"), None),
            P(("seq", "head"), None),
            P(("seq", "head"), None),
            P("seq"),
            P("seq"),
            P("seq", "head"),
        ),
        out_specs=P(("seq", "head"), None),
        check_vma=False,
    )
```
